32 devices in a mesh: row: 8 (over z, y), col: 4 (over x, core).
Axes of the slice: x: 2, y: 2, z: 4, core: 2. Of those that a mesh axis runs over, the one named last changes fastest.
Arguments:
- right_side: float32 [8192, 512], P(('row', 'col')), may hold values from -6 to 6
- earlier_panel: bfloat16 [8192, 8, 1024], P('row', None, 'col'), may hold values from -0.0625 to 0.0625
- earlier_solution: bfloat16 [8, 1024, 512], P('row', 'col'), may hold values from -6 to 6
- window_panel: bfloat16 [8192, 3, 1024], P(('row', 'col')), may hold values from -0.109375 to 0.109375
- diag_inverse: bfloat16 [3, 1024, 1024], P(None, 'col'), as said below
Outputs:
- solved: bfloat16 [3, 1024, 512], P(None, 'col')
- remaining: float32 [8192, 512], P(('row', 'col'))
The draws below stay inside these ranges and needn't reach their ends.
Inputs may be any that keep to these rules, and one draw needn't show every extreme that they name: Each diag_inverse[k] is zero above its diagonal, and its diagonal lies between 0.5 and 2.
All inputs are finite; a program needn't handle non-finite values.
Results may differ from the reference program's by a relative error of at most 0.013.
Values may be sent and summed in bfloat16 or wider, within the bound.
No kernel may reach another device: no remote copies, remote signals or barrier semaphores. Data moves between devices by JAX's collectives and lax.ppermute only.
A program may use at most 64 MiB of HBM per device.

```python
import math
import jax
import jax.numpy as jnp
from jax import lax

NB = 1024
NRHS = 512
STEPS = 3
PREV = 8
ROWS = 8192
N_COL = 4


def draw_diag_inverse(key, part):
    key = jax.random.fold_in(key, 11)
    key_lower, key_diagonal = jax.random.split(key)
    lower_values = jax.random.truncated_normal(key_lower, -4.0, 4.0, (STEPS, NB, NB), jnp.float32)
    diagonal = jnp.exp(jax.random.uniform(key_diagonal, (STEPS, NB), jnp.float32, math.log(0.5), math.log(2.0)))
    row_ids = lax.broadcasted_iota(jnp.int32, (STEPS, NB, NB), 1)
    col_ids = lax.broadcasted_iota(jnp.int32, (STEPS, NB, NB), 2)
    lower_part = jnp.where(row_ids > col_ids, lower_values / math.sqrt(NB), 0.0)
    whole = lower_part + jnp.where(row_ids == col_ids, diagonal[:, :, None], 0.0)
    return whole.astype(jnp.bfloat16)


def block_scale(rng, extent, pieces, low, largest):
    level, own = 1.0, jax.random.fold_in(rng, 6)
    for position, parts in pieces:
        draws = jnp.exp(jax.random.uniform(jax.random.fold_in(own, position), (parts,), jnp.float32, low / len(pieces), largest / len(pieces)))
        level = level * jnp.repeat(draws, extent[position] // parts).reshape([-1 if axis == position else 1 for axis in range(len(extent))])
    return level


def gaussian(own_key, shape, spread, bound, cuts=(), dtype=jnp.bfloat16):
    loudness = block_scale(own_key, shape, cuts, -0.22, 0.18) if cuts else 1.0
    values = jax.random.normal(own_key, shape, jnp.float32) * spread * loudness
    return jnp.minimum(jnp.maximum(values, -bound), bound).astype(dtype)


def setup_inputs(seed: int = 0) -> dict:
    key_of = jax.random.split(jax.random.key(seed), 6)
    return {
        "right_side": gaussian(key_of[0], (ROWS, NRHS), 1.0, 6.0, ((0, 32),), jnp.float32),
        "earlier_panel": gaussian(key_of[1], (ROWS, PREV, NB), (PREV * NB) ** -0.5, 0.0625, ((0, 8), (2, 4))),
        "earlier_solution": gaussian(key_of[2], (PREV, NB, NRHS), 1.0, 6.0, ((0, 8), (1, 4))),
        "window_panel": gaussian(key_of[3], (ROWS, STEPS, NB), (STEPS * NB) ** -0.5, 0.109375, ((0, 32),)),
        "diag_inverse": draw_diag_inverse(jax.random.fold_in(key_of[5], 71), 0),
    }


def reference(right_side, earlier_panel, earlier_solution, window_panel, diag_inverse):
    block_count = right_side.shape[0] // NB
    strip_width = NB // N_COL
    split_solution = earlier_solution.reshape(PREV, N_COL, strip_width, NRHS).astype(jnp.float32)

    def bulk_block(panel_rows):
        split_panel = panel_rows.reshape(NB, PREV, N_COL, strip_width).astype(jnp.float32)
        partial_value = jnp.einsum("ipcw,pcwn->cin", split_panel, split_solution, precision=lax.Precision.HIGHEST)
        rounded = lax.optimization_barrier(partial_value.astype(jnp.bfloat16))
        return jnp.sum(rounded.astype(jnp.float32), axis=0)

    bulk_term = lax.map(bulk_block, earlier_panel.reshape(block_count, NB, PREV, NB))
    current = right_side.reshape(block_count, NB, NRHS) - bulk_term
    block_ids = jnp.arange(block_count)
    window_blocks = window_panel.reshape(block_count, NB, STEPS, NB)
    solved = []
    for step_index in range(STEPS):
        residual = current[step_index].astype(jnp.bfloat16)
        solution = jnp.dot(diag_inverse[step_index], residual, preferred_element_type=jnp.float32).astype(jnp.bfloat16)
        solved.append(solution)
        update = jnp.einsum("bik,kn->bin", window_blocks[:, :, step_index, :].astype(jnp.float32), solution.astype(jnp.float32), precision=lax.Precision.HIGHEST)
        later_rows = (block_ids > step_index)[:, None, None]
        current = jnp.where(later_rows, current - update, current)
    return jnp.stack(solved), current.reshape(block_count * NB, NRHS)
```

```python
import jax
import jax.numpy as jnp
from jax import lax
from jax.sharding import PartitionSpec as P

F32 = jnp.float32
BF16 = jnp.bfloat16


def flip(value, axis, size, bit):
    return lax.ppermute(value, axis, [(i, i ^ bit) for i in range(size)])


def matmul(left, right):
    return jnp.dot(left, right, preferred_element_type=F32)


def halves(value, bit):
    kept = lax.dynamic_index_in_dim(value, bit, 0, keepdims=False)
    sent = lax.dynamic_index_in_dim(value, 1 - bit, 0, keepdims=False)
    return kept, sent


def gather_ordered(value, n_col, col):
    bit = n_col // 2
    bits = []
    while bit:
        bits.append(bit)
        bit //= 2
    order = [b for b in bits if b > 1] + [1]
    parts = {0: value}
    for b in order:
        moved = {f ^ b: flip(v, "col", n_col, b) for f, v in parts.items()}
        parts.update(moved)
    stacked = jnp.stack([parts[f] for f in range(n_col)])
    index = jnp.arange(n_col) ^ col
    return stacked[index].reshape(-1, value.shape[1])


def reduce_chunks(value, n_col, col):
    bit = 1
    while bit < n_col:
        rest = value.shape[0] // 2
        paired = value.reshape((rest, 2) + value.shape[1:]).swapaxes(0, 1)
        kept, sent = halves(paired, (col // bit) % 2)
        value = kept + flip(sent.astype(BF16), "col", n_col, bit).astype(F32)
        bit *= 2
    return value[0]


def gather_lines(block, n_row, row):
    per_line = 1
    while 4 * per_line * per_line <= n_row:
        per_line *= 2
    lines = n_row // per_line
    blocks = [(block, row)]
    up, down = block, block
    for s in range(1, lines):
        up = lax.ppermute(up, "row", [(i, i + per_line) for i in range((s - 1) * per_line, n_row - per_line)])
        down = lax.ppermute(down, "row", [(i, i - per_line) for i in range(per_line, n_row - (s - 1) * per_line)])
        blocks += [(up, row - s * per_line), (down, row + s * per_line)]
    for bit in range(1, per_line):
        blocks += [(flip(v, "row", n_row, bit), source ^ bit) for v, source in blocks[: 2 * lines - 1]]
    return blocks


def on_device(shape, right_side, earlier_panel, earlier_solution, window_panel, diag_inverse):
    n_row, n_col = shape
    step_count = diag_inverse.shape[0]
    row, col = lax.axis_index("row"), lax.axis_index("col")
    strip, nrhs = right_side.shape
    rows = earlier_panel.shape[0]
    chunk = nrhs // n_col
    weights = []
    for j in range(step_count):
        own = jnp.where(row == j, diag_inverse[j], window_panel[:, j, :])
        weights.append(gather_ordered(own, n_col, col))

    total = jnp.zeros((n_col, strip, nrhs), F32)
    total = lax.dynamic_update_index_in_dim(total, -right_side, col, 0).reshape(rows, nrhs)
    if n_row > 8:
        everything = lax.all_gather(earlier_solution, "row", axis=0, tiled=True)
        total = total + jnp.einsum("iqw,qwn->in", earlier_panel, everything, preferred_element_type=F32)
    else:
        panel = earlier_panel.swapaxes(0, 1)
        for v, source in gather_lines(earlier_solution[0], n_row, row):
            part = lax.dynamic_index_in_dim(panel, jnp.clip(source, 0, n_row - 1), 0, keepdims=False)
            total = total + matmul(part, v)
    chunks = total.reshape(rows, n_col, chunk).swapaxes(0, 1)
    current = -reduce_chunks(chunks, n_col, col)

    bases = [[1, 2, 4], [3, 1, 4], [6, 2, 1]]
    solved = []
    for k in range(step_count):
        value = matmul(weights[k], current.astype(BF16)).astype(BF16)
        have = [k]
        bits = [b for b in bases[k]] + [1 << i for i in range(3, 16) if (1 << i) < n_row]
        for b in bits:
            moved = lax.ppermute(value, "row", [(i, i ^ b) for i in have])
            into = jnp.zeros((), bool)
            for i in have:
                into |= row == (i ^ b)
            value = jnp.where(into, moved, value)
            have += [i ^ b for i in have]
        solved.append(value)
        current = jnp.where(row > k, current - matmul(weights[k], value), current)
    early = lax.all_to_all(jnp.stack(solved[:-1]), "col", 1, 2, tiled=True)
    late = lax.all_to_all(jnp.stack([solved[-1], current.astype(BF16)]), "col", 1, 2, tiled=True)
    return jnp.concatenate([early, late[:1]]), late[1].astype(F32)


def solution(mesh):
    shape = (mesh.shape["row"], mesh.shape["col"])

    def step(*args):
        return on_device(shape, *args)

    return jax.shard_map(
        step,
        mesh=mesh,
        in_specs=(
            P(("row", "col"), None),
            P("row", None, "col"),
            P("row", "col", None),
            P(("row", "col"), None, None),
            P(None, "col", None),
        ),
        out_specs=(P(None, "col", None), P(("row", "col"), None)),
        check_vma=False,
    )
```

```python
import functools

import jax
import jax.numpy as jnp
from jax import lax
from jax.experimental import pallas as pl
from jax.experimental.pallas import tpu as pltpu
from jax.sharding import PartitionSpec as P

F32 = jnp.float32
BF16 = jnp.bfloat16


def flip(value, axis, size, bit):
    return lax.ppermute(value, axis, [(i, i ^ bit) for i in range(size)])


def matmul(left, right):
    return jnp.dot(left, right, preferred_element_type=F32)


def halves(value, bit):
    kept = lax.dynamic_index_in_dim(value, bit, 0, keepdims=False)
    sent = lax.dynamic_index_in_dim(value, 1 - bit, 0, keepdims=False)
    return kept, sent


def gather_ordered(value, n_col, col):
    bit = n_col // 2
    bits = []
    while bit:
        bits.append(bit)
        bit //= 2
    order = [b for b in bits if b > 1] + [1]
    parts = {0: value}
    for b in order:
        moved = {f ^ b: flip(v, "col", n_col, b) for f, v in parts.items()}
        parts.update(moved)
    stacked = jnp.stack([parts[f] for f in range(n_col)])
    index = jnp.arange(n_col) ^ col
    return stacked[index].reshape(-1, value.shape[1])


def reduce_chunks(value, n_col, col):
    bit = 1
    while bit < n_col:
        rest = value.shape[0] // 2
        paired = value.reshape((rest, 2) + value.shape[1:]).swapaxes(0, 1)
        kept, sent = halves(paired, (col // bit) % 2)
        value = kept + flip(sent.astype(BF16), "col", n_col, bit).astype(F32)
        bit *= 2
    return value[0]


def gather_lines(block, n_row, row):
    per_line = 1
    while 4 * per_line * per_line <= n_row:
        per_line *= 2
    lines = n_row // per_line
    blocks = [(block, row)]
    up, down = block, block
    for s in range(1, lines):
        up = lax.ppermute(up, "row", [(i, i + per_line) for i in range((s - 1) * per_line, n_row - per_line)])
        down = lax.ppermute(down, "row", [(i, i - per_line) for i in range(per_line, n_row - (s - 1) * per_line)])
        blocks += [(up, row - s * per_line), (down, row + s * per_line)]
    for bit in range(1, per_line):
        blocks += [(flip(v, "row", n_row, bit), source ^ bit) for v, source in blocks[: 2 * lines - 1]]
    return blocks


def on_device(shape, right_side, earlier_panel, earlier_solution, window_panel, diag_inverse):
    n_row, n_col = shape
    step_count = diag_inverse.shape[0]
    row, col = lax.axis_index("row"), lax.axis_index("col")
    strip, nrhs = right_side.shape
    rows = earlier_panel.shape[0]
    chunk = nrhs // n_col
    weights = []
    for j in range(step_count):
        own = jnp.where(row == j, diag_inverse[j], window_panel[:, j, :])
        weights.append(gather_ordered(own, n_col, col))

    total = jnp.zeros((n_col, strip, nrhs), F32)
    total = lax.dynamic_update_index_in_dim(total, -right_side, col, 0).reshape(rows, nrhs)
    if n_row > 8:
        everything = lax.all_gather(earlier_solution, "row", axis=0, tiled=True)
        total = total + jnp.einsum("iqw,qwn->in", earlier_panel, everything, preferred_element_type=F32)
    else:
        panel = earlier_panel.swapaxes(0, 1)
        for v, source in gather_lines(earlier_solution[0], n_row, row):
            part = lax.dynamic_index_in_dim(panel, jnp.clip(source, 0, n_row - 1), 0, keepdims=False)
            total = total + matmul(part, v)
    chunks = total.reshape(rows, n_col, chunk).swapaxes(0, 1)
    current = -reduce_chunks(chunks, n_col, col)

    bases = [[1, 2, 4], [3, 1, 4], [6, 2, 1]]
    solved = []
    for k in range(step_count):
        value = matmul(weights[k], current.astype(BF16)).astype(BF16)
        have = [k]
        bits = [b for b in bases[k]] + [1 << i for i in range(3, 16) if (1 << i) < n_row]
        for b in bits:
            moved = lax.ppermute(value, "row", [(i, i ^ b) for i in have])
            into = jnp.zeros((), bool)
            for i in have:
                into |= row == (i ^ b)
            value = jnp.where(into, moved, value)
            have += [i ^ b for i in have]
        solved.append(value)
        current = jnp.where(row > k, current - matmul(weights[k], value), current)
    early = lax.all_to_all(jnp.stack(solved[:-1]), "col", 1, 2, tiled=True)
    late = lax.all_to_all(jnp.stack([solved[-1], current.astype(BF16)]), "col", 1, 2, tiled=True)
    return jnp.concatenate([early, late[:1]]), late[1].astype(F32)


def flat_index(*values):
    return jnp.stack([jnp.asarray(v, jnp.int32) for v in values])


PARAMS = pltpu.CompilerParams(vmem_limit_bytes=48 * 1024 * 1024)
SMEM = pl.BlockSpec(memory_space=pltpu.SMEM)
VMEM = pl.BlockSpec(memory_space=pltpu.VMEM)
ANY = pl.BlockSpec(memory_space=pl.ANY)


def shape_of(shape, dtype):
    return jax.ShapeDtypeStruct(shape, dtype)


def relayout_kernel(panel_ref, out_ref, *wide):
    tile, blocks, _ = panel_ref.shape
    for h, lanes in enumerate(wide):
        span = pl.ds(128 * h, 128)
        lanes[...] = panel_ref[:, :, span].astype(F32).reshape(tile * blocks, 128)
        for j in range(blocks):
            out_ref[j, :, span] = lanes[pl.ds(j, tile, stride=blocks), :].astype(BF16)


def relayout(panel, tile=128):
    rows, blocks, width = panel.shape
    return pl.pallas_call(
        relayout_kernel,
        grid=(rows // tile,),
        out_shape=shape_of((blocks, rows, width), BF16),
        in_specs=[pl.BlockSpec((tile, blocks, width), lambda i: (i, 0, 0))],
        out_specs=pl.BlockSpec((blocks, tile, width), lambda i: (0, i, 0)),
        scratch_shapes=[pltpu.VMEM((tile * blocks, 128), F32)] * (width // 128),
        compiler_params=PARAMS,
    )(panel)


def panel_copies(index_ref, panel_ref, held, sems, count):
    return [pltpu.make_async_copy(panel_ref.at[index_ref[b]], held.at[b], sems.at[b]) for b in range(count)]


def bulk_first_kernel(count, index_ref, panel_ref, *refs):
    blocks, (side_ref, out_ref, held, sems) = refs[:count], refs[count:]
    copies = panel_copies(index_ref, panel_ref, held, sems, count)
    for copy in copies:
        copy.start()
    for copy in copies:
        copy.wait()
    strip = side_ref.shape[0]
    col = index_ref[count]

    def tile(t, carry):
        span = pl.ds(pl.multiple_of(t * strip, strip), strip)
        total = jnp.where(t == col, -side_ref[...], 0.0)
        for b in range(count):
            total = total + matmul(held[b, span, :], blocks[b][...])
        out_ref[span, :] = total
        return carry

    lax.fori_loop(0, out_ref.shape[0] // strip, tile, 0)


def bulk_last_kernel(count, n_col, index_ref, panel_ref, *refs):
    blocks, (total_ref, kept_ref, sent_ref, held, scratch, sems) = refs[:count], refs[count:]
    copies = panel_copies(index_ref, panel_ref, held, sems, count)
    for copy in copies:
        copy.start()
    for copy in copies:
        copy.wait()
    strip = scratch.shape[0]
    chunk = kept_ref.shape[2]
    core = lax.rem(index_ref[count], 2)

    def tile(t, carry):
        span = pl.ds(pl.multiple_of(t * strip, strip), strip)
        total = total_ref[span, :]
        for b in range(count):
            total = total + matmul(held[b, span, :], blocks[b][...])
        scratch[...] = total
        for h in range(n_col // 2):
            kept_ref[h, span, :] = scratch[:, pl.ds(pl.multiple_of((2 * h + core) * chunk, chunk), chunk)]
            sent_ref[h, span, :] = scratch[:, pl.ds(pl.multiple_of((2 * h + 1 - core) * chunk, chunk), chunk)].astype(BF16)
        return carry

    lax.fori_loop(0, total_ref.shape[0] // strip, tile, 0)


def bulk(panel, blocks, sources, extra, col, n_col=None):
    count = len(blocks)
    rows, width = panel.shape[1:]
    nrhs = blocks[0].shape[1]
    index = flat_index(*sources, col)
    scratch = [pltpu.VMEM((count, rows, width), BF16)]
    if n_col is None:
        kernel = functools.partial(bulk_first_kernel, count)
        out_shape, out_specs = shape_of((rows, nrhs), F32), VMEM
    else:
        kernel = functools.partial(bulk_last_kernel, count, n_col)
        part = (n_col // 2, rows, nrhs // n_col)
        out_shape, out_specs = (shape_of(part, F32), shape_of(part, BF16)), (VMEM, VMEM)
        scratch.append(pltpu.VMEM((rows // n_col, nrhs), F32))
    return pl.pallas_call(
        kernel,
        out_shape=out_shape,
        in_specs=[SMEM, ANY] + [VMEM] * (count + 1),
        out_specs=out_specs,
        scratch_shapes=scratch + [pltpu.SemaphoreType.DMA((count,))],
        compiler_params=PARAMS,
    )(index, panel, *blocks, extra)


def reduce_kernel(bit, index_ref, kept_ref, moved_ref, keep_ref, send_ref):
    mine = lax.rem(index_ref[0] // bit, 2)
    for h in range(keep_ref.shape[0]):
        keep_ref[h] = kept_ref[2 * h + mine] + moved_ref[2 * h + mine].astype(F32)
        send_ref[h] = (kept_ref[2 * h + 1 - mine] + moved_ref[2 * h + 1 - mine].astype(F32)).astype(BF16)


def reduce_step(bit, index, kept, moved):
    part = (kept.shape[0] // 2,) + kept.shape[1:]
    return pl.pallas_call(
        functools.partial(reduce_kernel, bit),
        out_shape=(shape_of(part, F32), shape_of(part, BF16)),
        in_specs=[SMEM, VMEM, VMEM],
        out_specs=(VMEM, VMEM),
        compiler_params=PARAMS,
    )(index, kept, moved)


def apply_strips(col, strips, value, store):
    width = strips[0].shape[1]
    for f, strip in enumerate(strips):
        span = pl.ds(pl.multiple_of((col ^ f) * width, width), width)
        store(span, matmul(strip[0], value))


def start_kernel(n_col, index_ref, kept_ref, moved_ref, *refs):
    diag, (current_ref, solved_ref) = refs[:n_col], refs[n_col:]
    current = -(kept_ref[0] + moved_ref[0].astype(F32))
    current_ref[...] = current

    def store(span, product):
        solved_ref[span, :] = product.astype(BF16)

    apply_strips(index_ref[1], diag, current.astype(BF16), store)


def step_kernel(k, n_col, index_ref, current_ref, solved_ref, *refs):
    update, diag, (out_ref, next_ref) = refs[:n_col], refs[n_col : 2 * n_col], refs[2 * n_col :]
    row, col = index_ref[0], index_ref[1]
    later = row > k - 1

    def subtract(span, product):
        out_ref[span, :] = current_ref[span, :] - jnp.where(later, product, 0.0)

    apply_strips(col, update, solved_ref[...], subtract)

    def store(span, product):
        next_ref[span, :] = product.astype(BF16)

    apply_strips(col, diag, out_ref[...].astype(BF16), store)


def finish_kernel(k, n_col, index_ref, current_ref, solved_ref, *refs):
    update, (pieces_ref, scratch) = refs[:n_col], refs[n_col:]
    row, col = index_ref[0], index_ref[1]
    later = row > k

    def subtract(span, product):
        scratch[span, :] = current_ref[span, :] - jnp.where(later, product, 0.0)

    apply_strips(col, update, solved_ref[...], subtract)
    width = pieces_ref.shape[2]
    for f in range(n_col):
        span = pl.ds(pl.multiple_of((col ^ f) * width, width), width)
        pieces_ref[f, 0] = solved_ref[span, :]
        pieces_ref[f, 1] = scratch[span, :].astype(BF16)


def pieces_kernel(index_ref, *refs):
    values, pieces_ref = refs[:-1], refs[-1]
    width = pieces_ref.shape[2]
    for f in range(pieces_ref.shape[0]):
        span = pl.ds(pl.multiple_of((index_ref[1] ^ f) * width, width), width)
        for j, value in enumerate(values):
            pieces_ref[f, j] = value[span, :]


def assemble_kernel(n_col, index_ref, *refs):
    early, late, (solved_ref, remaining_ref) = refs[:n_col], refs[n_col : 2 * n_col], refs[2 * n_col :]
    chunk = early[0].shape[2]
    last = early[0].shape[0]
    for f in range(n_col):
        span = pl.ds(pl.multiple_of((index_ref[1] ^ f) * chunk, chunk), chunk)
        for j in range(last):
            solved_ref[j, :, span] = early[f][j]
        solved_ref[last, :, span] = late[f][0]
        remaining_ref[:, span] = late[f][1].astype(F32)


def local(kernel, out_shape, operands, specs=None, scratch=()):
    specs = specs or [SMEM] + [VMEM] * (len(operands) - 1)
    out_specs = jax.tree.map(lambda _: VMEM, out_shape)
    return pl.pallas_call(
        kernel, grid=(1,), out_shape=out_shape, in_specs=specs, out_specs=out_specs, scratch_shapes=list(scratch), compiler_params=PARAMS
    )(*operands)


def swap_pieces(pieces, n_col):
    return [pieces[0]] + [flip(pieces[f], "col", n_col, f) for f in range(1, n_col)]


def fast(shape, right_side, earlier_panel, earlier_solution, window_panel, diag_inverse):
    n_row, n_col = shape
    step_count = diag_inverse.shape[0]
    row, col = lax.axis_index("row"), lax.axis_index("col")
    index = flat_index(row, col)
    strip, nrhs = right_side.shape
    rows = earlier_panel.shape[0]
    chunk = nrhs // n_col

    block = earlier_solution[0]
    blocks = {0: block, 1: flip(block, "row", n_row, 1)}
    for f in (2, 4, 6):
        blocks[f] = flip(block, "row", n_row, f)
    own = jnp.stack([jnp.where(row == j, diag_inverse[j], window_panel[:, j, :]) for j in range(step_count)])
    strips = {0: own}
    for b in [1 << i for i in range(1, 8) if (1 << i) < n_col] + [1]:
        strips.update({f ^ b: flip(v, "col", n_col, b) for f, v in strips.items()})
    panel = relayout(earlier_panel)
    for f in (2, 4, 6):
        blocks[f + 1] = flip(blocks[f], "row", n_row, 1)
    early, late = (0, 1, 2, 3, 4), (5, 6, 7)
    total = bulk(panel, [blocks[f] for f in early], [row ^ f for f in early], right_side, col)
    kept, sent = bulk(panel, [blocks[f] for f in late], [row ^ f for f in late], total, col, n_col)
    moved = flip(sent, "col", n_col, 1)
    for b in [1 << i for i in range(1, 8) if (1 << i) < n_col]:
        kept, sent = reduce_step(b, flat_index(col), kept, moved)
        moved = flip(sent, "col", n_col, b)

    def slots(k):
        return [strips[f] for f in range(n_col)], [pl.BlockSpec((1,) + own.shape[1:], lambda i, k=k: (k, 0, 0))] * n_col

    value_shape = (shape_of((rows, chunk), F32), shape_of((rows, chunk), BF16))
    weights, specs = slots(0)
    current, value = local(functools.partial(start_kernel, n_col), value_shape, [index, kept, moved] + weights, [SMEM, VMEM, VMEM] + specs)
    solved = []
    for k in range(step_count):
        have = [k]
        for b in ([1, 2, 4], [3, 1, 4], [6, 2, 1])[k]:
            moved = lax.ppermute(value, "row", [(i, i ^ b) for i in have])
            into = jnp.zeros((), bool)
            for i in have:
                into |= row == (i ^ b)
            value = jnp.where(into, moved, value)
            have += [i ^ b for i in have]
        solved.append(value)
        update, specs = slots(k)
        if k < step_count - 1:
            diag, more = slots(k + 1)
            kernel = functools.partial(step_kernel, k + 1, n_col)
            current, value = local(kernel, value_shape, [index, current, value] + update + diag, [SMEM, VMEM, VMEM] + specs + more)
        else:
            pieces = shape_of((n_col, 2, rows // n_col, chunk), BF16)
            kernel = functools.partial(finish_kernel, k, n_col)
            last = local(kernel, pieces, [index, current, value] + update, [SMEM, VMEM, VMEM] + specs, [pltpu.VMEM((rows, chunk), F32)])
    first = local(pieces_kernel, shape_of((n_col, step_count - 1, rows // n_col, chunk), BF16), [index] + solved[:-1])
    first, last = swap_pieces(first, n_col), swap_pieces(last, n_col)
    outs = (shape_of((step_count, strip, nrhs), BF16), shape_of((strip, nrhs), F32))
    return local(functools.partial(assemble_kernel, n_col), outs, [index] + first + last)


def solution(mesh):
    shape = (mesh.shape["row"], mesh.shape["col"])

    def step(*args):
        chunk = args[0].shape[1] // shape[1]
        plan = fast if shape[0] == 8 and chunk % 128 == 0 else on_device
        return plan(shape, *args)

    return jax.shard_map(
        step,
        mesh=mesh,
        in_specs=(
            P(("row", "col"), None),
            P("row", None, "col"),
            P("row", "col", None),
            P(("row", "col"), None, None),
            P(None, "col", None),
        ),
        out_specs=(P(None, "col", None), P(("row", "col"), None)),
        check_vma=False,
    )
```

```python
import functools

import jax
import jax.numpy as jnp
from jax import lax
from jax.experimental import pallas as pl
from jax.experimental.pallas import tpu as pltpu
from jax.sharding import PartitionSpec as P

F32 = jnp.float32
BF16 = jnp.bfloat16


def flip(value, axis, size, bit):
    return lax.ppermute(value, axis, [(i, i ^ bit) for i in range(size)])


def matmul(left, right):
    return jnp.dot(left, right, preferred_element_type=F32)


def halves(value, bit):
    kept = lax.dynamic_index_in_dim(value, bit, 0, keepdims=False)
    sent = lax.dynamic_index_in_dim(value, 1 - bit, 0, keepdims=False)
    return kept, sent


def gather_ordered(value, n_col, col):
    bit = n_col // 2
    bits = []
    while bit:
        bits.append(bit)
        bit //= 2
    order = [b for b in bits if b > 1] + [1]
    parts = {0: value}
    for b in order:
        moved = {f ^ b: flip(v, "col", n_col, b) for f, v in parts.items()}
        parts.update(moved)
    stacked = jnp.stack([parts[f] for f in range(n_col)])
    index = jnp.arange(n_col) ^ col
    return stacked[index].reshape(-1, value.shape[1])


def reduce_chunks(value, n_col, col):
    bit = 1
    while bit < n_col:
        rest = value.shape[0] // 2
        paired = value.reshape((rest, 2) + value.shape[1:]).swapaxes(0, 1)
        kept, sent = halves(paired, (col // bit) % 2)
        value = kept + flip(sent.astype(BF16), "col", n_col, bit).astype(F32)
        bit *= 2
    return value[0]


def gather_lines(block, n_row, row):
    per_line = 1
    while 4 * per_line * per_line <= n_row:
        per_line *= 2
    lines = n_row // per_line
    blocks = [(block, row)]
    up, down = block, block
    for s in range(1, lines):
        up = lax.ppermute(up, "row", [(i, i + per_line) for i in range((s - 1) * per_line, n_row - per_line)])
        down = lax.ppermute(down, "row", [(i, i - per_line) for i in range(per_line, n_row - (s - 1) * per_line)])
        blocks += [(up, row - s * per_line), (down, row + s * per_line)]
    for bit in range(1, per_line):
        blocks += [(flip(v, "row", n_row, bit), source ^ bit) for v, source in blocks[: 2 * lines - 1]]
    return blocks


def on_device(shape, right_side, earlier_panel, earlier_solution, window_panel, diag_inverse):
    n_row, n_col = shape
    step_count = diag_inverse.shape[0]
    row, col = lax.axis_index("row"), lax.axis_index("col")
    strip, nrhs = right_side.shape
    rows = earlier_panel.shape[0]
    chunk = nrhs // n_col
    weights = []
    for j in range(step_count):
        own = jnp.where(row == j, diag_inverse[j], window_panel[:, j, :])
        weights.append(gather_ordered(own, n_col, col))

    total = jnp.zeros((n_col, strip, nrhs), F32)
    total = lax.dynamic_update_index_in_dim(total, -right_side, col, 0).reshape(rows, nrhs)
    if n_row > 8:
        everything = lax.all_gather(earlier_solution, "row", axis=0, tiled=True)
        total = total + jnp.einsum("iqw,qwn->in", earlier_panel, everything, preferred_element_type=F32)
    else:
        panel = earlier_panel.swapaxes(0, 1)
        for v, source in gather_lines(earlier_solution[0], n_row, row):
            part = lax.dynamic_index_in_dim(panel, jnp.clip(source, 0, n_row - 1), 0, keepdims=False)
            total = total + matmul(part, v)
    chunks = total.reshape(rows, n_col, chunk).swapaxes(0, 1)
    current = -reduce_chunks(chunks, n_col, col)

    bases = [[1, 2, 4], [3, 1, 4], [6, 2, 1]]
    solved = []
    for k in range(step_count):
        value = matmul(weights[k], current.astype(BF16)).astype(BF16)
        have = [k]
        bits = [b for b in bases[k]] + [1 << i for i in range(3, 16) if (1 << i) < n_row]
        for b in bits:
            moved = lax.ppermute(value, "row", [(i, i ^ b) for i in have])
            into = jnp.zeros((), bool)
            for i in have:
                into |= row == (i ^ b)
            value = jnp.where(into, moved, value)
            have += [i ^ b for i in have]
        solved.append(value)
        current = jnp.where(row > k, current - matmul(weights[k], value), current)
    early = lax.all_to_all(jnp.stack(solved[:-1]), "col", 1, 2, tiled=True)
    late = lax.all_to_all(jnp.stack([solved[-1], current.astype(BF16)]), "col", 1, 2, tiled=True)
    return jnp.concatenate([early, late[:1]]), late[1].astype(F32)


def flat_index(*values):
    return jnp.stack([jnp.asarray(v, jnp.int32) for v in values])


PARAMS = pltpu.CompilerParams(vmem_limit_bytes=24 * 1024 * 1024)
SMEM = pl.BlockSpec(memory_space=pltpu.SMEM)
VMEM = pl.BlockSpec(memory_space=pltpu.VMEM)
ANY = pl.BlockSpec(memory_space=pl.ANY)


def shape_of(shape, dtype):
    return jax.ShapeDtypeStruct(shape, dtype)


def relayout_kernel(panel_ref, out_ref, *wide):
    tile, blocks, _ = panel_ref.shape
    for h, lanes in enumerate(wide):
        span = pl.ds(128 * h, 128)
        lanes[...] = panel_ref[:, :, span].astype(F32).reshape(tile * blocks, 128)
        for j in range(blocks):
            out_ref[j, :, span] = lanes[pl.ds(j, tile, stride=blocks), :].astype(BF16)


def relayout(panel, tile=128):
    rows, blocks, width = panel.shape
    return pl.pallas_call(
        relayout_kernel,
        grid=(rows // tile,),
        out_shape=shape_of((blocks, rows, width), BF16),
        in_specs=[pl.BlockSpec((tile, blocks, width), lambda i: (i, 0, 0))],
        out_specs=pl.BlockSpec((blocks, tile, width), lambda i: (0, i, 0)),
        scratch_shapes=[pltpu.VMEM((tile * blocks, 128), F32)] * (width // 128),
        compiler_params=PARAMS,
    )(panel)


def panel_copies(index_ref, panel_ref, held, sems, count):
    return [pltpu.make_async_copy(panel_ref.at[index_ref[b]], held.at[b], sems.at[b]) for b in range(count)]


def bulk_first_kernel(count, index_ref, panel_ref, *refs):
    blocks, (side_ref, out_ref, held, sems) = refs[:count], refs[count:]
    copies = panel_copies(index_ref, panel_ref, held, sems, count)
    for copy in copies:
        copy.start()
    for copy in copies:
        copy.wait()
    strip = side_ref.shape[0]
    col = index_ref[count]

    def tile(t, carry):
        span = pl.ds(pl.multiple_of(t * strip, strip), strip)
        total = jnp.where(t == col, -side_ref[...], 0.0)
        for b in range(count):
            total = total + matmul(held[b, span, :], blocks[b][...])
        out_ref[span, :] = total
        return carry

    lax.fori_loop(0, out_ref.shape[0] // strip, tile, 0)


def bulk_last_kernel(count, n_col, index_ref, panel_ref, *refs):
    blocks, (total_ref, kept_ref, sent_ref, held, scratch, sems) = refs[:count], refs[count:]
    copies = panel_copies(index_ref, panel_ref, held, sems, count)
    for copy in copies:
        copy.start()
    for copy in copies:
        copy.wait()
    strip = scratch.shape[0]
    chunk = kept_ref.shape[2]
    core = lax.rem(index_ref[count], 2)

    def tile(t, carry):
        span = pl.ds(pl.multiple_of(t * strip, strip), strip)
        total = total_ref[span, :]
        for b in range(count):
            total = total + matmul(held[b, span, :], blocks[b][...])
        scratch[...] = total
        for h in range(n_col // 2):
            kept_ref[h, span, :] = scratch[:, pl.ds(pl.multiple_of((2 * h + core) * chunk, chunk), chunk)]
            sent_ref[h, span, :] = scratch[:, pl.ds(pl.multiple_of((2 * h + 1 - core) * chunk, chunk), chunk)].astype(BF16)
        return carry

    lax.fori_loop(0, total_ref.shape[0] // strip, tile, 0)


def bulk(panel, blocks, sources, extra, col, n_col=None):
    count = len(blocks)
    rows, width = panel.shape[1:]
    nrhs = blocks[0].shape[1]
    index = flat_index(*sources, col)
    scratch = [pltpu.VMEM((count, rows, width), BF16)]
    if n_col is None:
        kernel = functools.partial(bulk_first_kernel, count)
        out_shape, out_specs = shape_of((rows, nrhs), F32), VMEM
    else:
        kernel = functools.partial(bulk_last_kernel, count, n_col)
        part = (n_col // 2, rows, nrhs // n_col)
        out_shape, out_specs = (shape_of(part, F32), shape_of(part, BF16)), (VMEM, VMEM)
        scratch.append(pltpu.VMEM((rows // n_col, nrhs), F32))
    return pl.pallas_call(
        kernel,
        out_shape=out_shape,
        in_specs=[SMEM, ANY] + [VMEM] * (count + 1),
        out_specs=out_specs,
        scratch_shapes=scratch + [pltpu.SemaphoreType.DMA((count,))],
        compiler_params=PARAMS,
    )(index, panel, *blocks, extra)


def reduce_kernel(bit, index_ref, kept_ref, moved_ref, keep_ref, send_ref):
    mine = lax.rem(index_ref[0] // bit, 2)
    for h in range(keep_ref.shape[0]):
        keep_ref[h] = kept_ref[2 * h + mine] + moved_ref[2 * h + mine].astype(F32)
        send_ref[h] = (kept_ref[2 * h + 1 - mine] + moved_ref[2 * h + 1 - mine].astype(F32)).astype(BF16)


def reduce_step(bit, index, kept, moved):
    part = (kept.shape[0] // 2,) + kept.shape[1:]
    return pl.pallas_call(
        functools.partial(reduce_kernel, bit),
        out_shape=(shape_of(part, F32), shape_of(part, BF16)),
        in_specs=[SMEM, VMEM, VMEM],
        out_specs=(VMEM, VMEM),
        compiler_params=PARAMS,
    )(index, kept, moved)


def apply_strips(col, strips, k, value, store):
    width = strips[0].shape[1]
    for f, strip in enumerate(strips):
        span = pl.ds(pl.multiple_of((col ^ f) * width, width), width)
        store(span, matmul(strip[k], value))


def store_solved(index_ref, strips, k, current_ref, solved_ref):
    own = index_ref[0] == k

    def store(span, product):
        solved_ref[span, :] = jnp.where(own, product, 0.0).astype(BF16)

    apply_strips(index_ref[1], strips, k, current_ref[...].astype(BF16), store)


def subtract(index_ref, strips, k, value, chosen, source_ref, target_ref):
    def store(span, product):
        target_ref[span, :] = source_ref[span, :] - jnp.where(chosen, product, 0.0)

    apply_strips(index_ref[1], strips, k, value, store)


def start_kernel(n_col, index_ref, kept_ref, moved_ref, *refs):
    strips, (current_ref, solved_ref) = refs[:n_col], refs[n_col:]
    current_ref[...] = -(kept_ref[0] + moved_ref[0].astype(F32))
    store_solved(index_ref, strips, 0, current_ref, solved_ref)


def step_kernel(k, n_col, index_ref, current_ref, *refs):
    strips, refs = refs[:n_col], refs[n_col:]
    parts, (out_ref, known_ref, solved_ref) = refs[:-3], refs[-3:]
    known_ref[...] = functools.reduce(jnp.add, [part[...] for part in parts])
    subtract(index_ref, strips, k - 1, known_ref[...], index_ref[0] > k - 1, current_ref, out_ref)
    store_solved(index_ref, strips, k, out_ref, solved_ref)


def late_kernel(first, n_col, index_ref, current_ref, *refs):
    strips, refs = refs[:n_col], refs[n_col:]
    steps = strips[0].shape[0] - 1
    parts, (out_ref, pieces_ref) = refs[:-2], refs[-2:]
    each = len(parts) // steps
    width = pieces_ref.shape[2]
    for k in range(steps):
        value = functools.reduce(jnp.add, [part[...] for part in parts[k * each : (k + 1) * each]])
        subtract(index_ref, strips, k, value, index_ref[0] >= first, out_ref if k else current_ref, out_ref)
        cut(index_ref, value, pieces_ref, k)


def cut(index_ref, value, pieces_ref, k):
    width = pieces_ref.shape[2]
    col = index_ref[1]
    for f in range(pieces_ref.shape[0]):
        for owner in range(pieces_ref.shape[0]):

            @pl.when((col ^ f) == owner)
            def _():
                pieces_ref[f, k] = value[owner * width : (owner + 1) * width, :]


def finish_kernel(n_col, index_ref, current_ref, *refs):
    strips, refs = refs[:n_col], refs[n_col:]
    k = strips[0].shape[0] - 1
    parts, (pieces_ref, scratch) = refs[:-2], refs[-2:]
    value = functools.reduce(jnp.add, [part[...] for part in parts])
    subtract(index_ref, strips, k, value, index_ref[0] > k, current_ref, scratch)
    cut(index_ref, value, pieces_ref, 0)
    width = pieces_ref.shape[2]
    for f in range(n_col):
        span = pl.ds(pl.multiple_of((index_ref[1] ^ f) * width, width), width)
        pieces_ref[f, 1] = scratch[span, :].astype(BF16)


def assemble_kernel(n_col, index_ref, *refs):
    early, late, (solved_ref, remaining_ref) = refs[:n_col], refs[n_col : 2 * n_col], refs[2 * n_col :]
    chunk = early[0].shape[2]
    last = early[0].shape[0]
    for f in range(n_col):
        span = pl.ds(pl.multiple_of((index_ref[1] ^ f) * chunk, chunk), chunk)
        for j in range(last):
            solved_ref[j, :, span] = early[f][j]
        solved_ref[last, :, span] = late[f][0]
        remaining_ref[:, span] = late[f][1].astype(F32)


def local(kernel, out_shape, operands, scratch=()):
    out_specs = jax.tree.map(lambda _: VMEM, out_shape)
    return pl.pallas_call(
        kernel,
        out_shape=out_shape,
        in_specs=[SMEM] + [VMEM] * (len(operands) - 1),
        out_specs=out_specs,
        scratch_shapes=list(scratch),
        compiler_params=PARAMS,
    )(*operands)


def hop(value, *pairs):
    return lax.ppermute(value, "row", pairs)


def after(value, *others):
    return lax.optimization_barrier((value,) + others)[0]


def swap_pieces(pieces, n_col):
    return [pieces[0]] + [flip(pieces[f], "col", n_col, f) for f in range(1, n_col)]


def fast(shape, right_side, earlier_panel, earlier_solution, window_panel, diag_inverse):
    n_row, n_col = shape
    step_count = diag_inverse.shape[0]
    row, col = lax.axis_index("row"), lax.axis_index("col")
    index = flat_index(row, col)
    strip, nrhs = right_side.shape
    rows = earlier_panel.shape[0]
    chunk = nrhs // n_col

    block = earlier_solution[0]
    blocks = {0: block}
    for f in (6, 4, 2, 1):
        blocks[f] = flip(block, "row", n_row, f)
    own = jnp.stack([jnp.where(row == j, diag_inverse[j], window_panel[:, j, :]) for j in range(step_count)])
    strips = {0: own}
    strips[1] = flip(own, "col", n_col, 1)
    strips[2] = flip(own, "col", n_col, 2)
    panel = relayout(earlier_panel)
    for f in (2, 4, 6):
        blocks[f + 1] = flip(blocks[f], "row", n_row, 1)
    early, late = (0, 1, 2, 3, 4), (5, 6, 7)
    total = bulk(panel, [blocks[f] for f in early], [row ^ f for f in early], right_side, col)
    kept, sent = bulk(panel, [blocks[f] for f in late], [row ^ f for f in late], total, col, n_col)
    strips[3] = flip(after(strips[2], sent), "col", n_col, 1)
    moved = flip(sent, "col", n_col, 1)
    kept, sent = reduce_step(2, flat_index(col), kept, moved)
    moved = flip(sent, "col", n_col, 2)
    strips = [strips[f] for f in range(n_col)]

    wide, narrow = shape_of((rows, chunk), F32), shape_of((rows, chunk), BF16)
    current, own0 = local(functools.partial(start_kernel, n_col), (wide, narrow), [index, kept, moved] + strips)
    at1, at2 = hop(own0, (0, 1)), hop(own0, (0, 2))
    step = functools.partial(step_kernel, 1, n_col)
    current, known0, own1 = local(step, (wide, narrow, narrow), [index, current] + strips + [own0, at1, at2])
    up2 = hop(own1, (1, 2))
    up3 = hop(own1, (1, 3))
    on0 = hop(known0, (1, 3), (2, 4))
    step = functools.partial(step_kernel, 2, n_col)
    current, known1, own2 = local(step, (wide, narrow, narrow), [index, current] + strips + [own1, up2])
    z4 = hop(own2, (2, 4))
    z6 = hop(own2, (2, 6))
    z0 = hop(own2, (2, 0))
    further0 = hop(on0, (3, 5), (4, 6))
    up5 = hop(up3, (3, 5))
    last0 = hop(further0, (5, 7))
    up7 = hop(up5, (5, 7))
    line1 = known1 + up3 + up5 + up7
    across1 = hop(line1, (1, 0), (5, 4), (7, 6))
    line2 = own2 + z0 + z4 + z6
    across2 = hop(line2, (0, 1), (2, 3), (4, 5), (6, 7))

    first = shape_of((n_col, step_count - 1, strip, chunk), BF16)
    parts = [known0 + on0, further0 + last0] + [line1, across1]
    current, first = local(functools.partial(late_kernel, step_count, n_col), (wide, first), [index, current] + strips + parts)
    last = shape_of((n_col, 2, strip, chunk), BF16)
    last = local(functools.partial(finish_kernel, n_col), last, [index, current] + strips + [line2, across2], [pltpu.VMEM((rows, chunk), F32)])
    first, last = swap_pieces(first, n_col), swap_pieces(last, n_col)
    outs = (shape_of((step_count, strip, nrhs), BF16), shape_of((strip, nrhs), F32))
    return local(functools.partial(assemble_kernel, n_col), outs, [index] + first + last)


def solution(mesh):
    shape = (mesh.shape["row"], mesh.shape["col"])

    def step(*args):
        chunk = args[0].shape[1] // shape[1]
        plan = fast if shape == (8, 4) and chunk % 128 == 0 and args[4].shape[0] == 3 else on_device
        return plan(shape, *args)

    return jax.shard_map(
        step,
        mesh=mesh,
        in_specs=(
            P(("row", "col"), None),
            P("row", None, "col"),
            P("row", "col", None),
            P(("row", "col"), None, None),
            P(None, "col", None),
        ),
        out_specs=(P(None, "col", None), P(("row", "col"), None)),
        check_vma=False,
    )
```

```python
import functools

import jax
import jax.numpy as jnp
from jax import lax
from jax.experimental import pallas as pl
from jax.experimental.pallas import tpu as pltpu
from jax.sharding import PartitionSpec as P

F32 = jnp.float32
BF16 = jnp.bfloat16


def flip(value, axis, size, bit):
    return lax.ppermute(value, axis, [(i, i ^ bit) for i in range(size)])


def matmul(left, right):
    return jnp.dot(left, right, preferred_element_type=F32)


def halves(value, bit):
    kept = lax.dynamic_index_in_dim(value, bit, 0, keepdims=False)
    sent = lax.dynamic_index_in_dim(value, 1 - bit, 0, keepdims=False)
    return kept, sent


def gather_ordered(value, n_col, col):
    bit = n_col // 2
    bits = []
    while bit:
        bits.append(bit)
        bit //= 2
    order = [b for b in bits if b > 1] + [1]
    parts = {0: value}
    for b in order:
        moved = {f ^ b: flip(v, "col", n_col, b) for f, v in parts.items()}
        parts.update(moved)
    stacked = jnp.stack([parts[f] for f in range(n_col)])
    index = jnp.arange(n_col) ^ col
    return stacked[index].reshape(-1, value.shape[1])


def reduce_chunks(value, n_col, col):
    bit = 1
    while bit < n_col:
        rest = value.shape[0] // 2
        paired = value.reshape((rest, 2) + value.shape[1:]).swapaxes(0, 1)
        kept, sent = halves(paired, (col // bit) % 2)
        value = kept + flip(sent.astype(BF16), "col", n_col, bit).astype(F32)
        bit *= 2
    return value[0]


def gather_lines(block, n_row, row):
    per_line = 1
    while 4 * per_line * per_line <= n_row:
        per_line *= 2
    lines = n_row // per_line
    blocks = [(block, row)]
    up, down = block, block
    for s in range(1, lines):
        up = lax.ppermute(up, "row", [(i, i + per_line) for i in range((s - 1) * per_line, n_row - per_line)])
        down = lax.ppermute(down, "row", [(i, i - per_line) for i in range(per_line, n_row - (s - 1) * per_line)])
        blocks += [(up, row - s * per_line), (down, row + s * per_line)]
    for bit in range(1, per_line):
        blocks += [(flip(v, "row", n_row, bit), source ^ bit) for v, source in blocks[: 2 * lines - 1]]
    return blocks


def on_device(shape, right_side, earlier_panel, earlier_solution, window_panel, diag_inverse):
    n_row, n_col = shape
    step_count = diag_inverse.shape[0]
    row, col = lax.axis_index("row"), lax.axis_index("col")
    strip, nrhs = right_side.shape
    rows = earlier_panel.shape[0]
    chunk = nrhs // n_col
    weights = []
    for j in range(step_count):
        own = jnp.where(row == j, diag_inverse[j], window_panel[:, j, :])
        weights.append(gather_ordered(own, n_col, col))

    total = jnp.zeros((n_col, strip, nrhs), F32)
    total = lax.dynamic_update_index_in_dim(total, -right_side, col, 0).reshape(rows, nrhs)
    if n_row > 8:
        everything = lax.all_gather(earlier_solution, "row", axis=0, tiled=True)
        total = total + jnp.einsum("iqw,qwn->in", earlier_panel, everything, preferred_element_type=F32)
    else:
        panel = earlier_panel.swapaxes(0, 1)
        for v, source in gather_lines(earlier_solution[0], n_row, row):
            part = lax.dynamic_index_in_dim(panel, jnp.clip(source, 0, n_row - 1), 0, keepdims=False)
            total = total + matmul(part, v)
    chunks = total.reshape(rows, n_col, chunk).swapaxes(0, 1)
    current = -reduce_chunks(chunks, n_col, col)

    bases = [[1, 2, 4], [3, 1, 4], [6, 2, 1]]
    solved = []
    for k in range(step_count):
        value = matmul(weights[k], current.astype(BF16)).astype(BF16)
        have = [k]
        bits = [b for b in bases[k]] + [1 << i for i in range(3, 16) if (1 << i) < n_row]
        for b in bits:
            moved = lax.ppermute(value, "row", [(i, i ^ b) for i in have])
            into = jnp.zeros((), bool)
            for i in have:
                into |= row == (i ^ b)
            value = jnp.where(into, moved, value)
            have += [i ^ b for i in have]
        solved.append(value)
        current = jnp.where(row > k, current - matmul(weights[k], value), current)
    early = lax.all_to_all(jnp.stack(solved[:-1]), "col", 1, 2, tiled=True)
    late = lax.all_to_all(jnp.stack([solved[-1], current.astype(BF16)]), "col", 1, 2, tiled=True)
    return jnp.concatenate([early, late[:1]]), late[1].astype(F32)


def flat_index(*values):
    return jnp.stack([jnp.asarray(v, jnp.int32) for v in values])


PARAMS = pltpu.CompilerParams(vmem_limit_bytes=20 * 1024 * 1024)


def cost(us):
    return pl.CostEstimate(flops=0, bytes_accessed=int(us * 3.6e6), transcendentals=0)

SMEM = pl.BlockSpec(memory_space=pltpu.SMEM)
VMEM = pl.BlockSpec(memory_space=pltpu.VMEM)
HBM = pl.BlockSpec(memory_space=pltpu.HBM)


def shape_of(shape, dtype):
    return jax.ShapeDtypeStruct(shape, dtype)


def order_kernel(index_ref, panel_ref, out_ref, held, sems, *wide):
    tiles, tile, sources, width = held.shape
    row = index_ref[0]
    copies = [pltpu.make_async_copy(panel_ref.at[pl.ds(t * tile, tile)], held.at[t], sems.at[t]) for t in range(tiles)]
    for copy in copies:
        copy.start()
    for t, copy in enumerate(copies):
        copy.wait()
        for h, lanes in enumerate(wide):
            lanes[...] = held[t, :, :, h * 128 : (h + 1) * 128].astype(F32).reshape(tile * sources, 128)
            for j in range(sources):
                start = (j ^ row) * width + h * 128
                span = pl.ds(pl.multiple_of(start, 128), 128)
                out_ref[t * tile : (t + 1) * tile, span] = lanes[pl.ds(j, tile, stride=sources), :].astype(BF16)


def order_panel(index, panel, tiles=4):
    rows, sources, width = panel.shape
    tile = rows // tiles
    return pl.pallas_call(
        order_kernel,
        out_shape=shape_of((rows, sources * width), BF16),
        in_specs=[SMEM, HBM],
        out_specs=VMEM,
        scratch_shapes=[pltpu.VMEM((tiles, tile, sources, width), BF16), pltpu.SemaphoreType.DMA((tiles,))]
        + [pltpu.VMEM((tile * sources, 128), F32)] * (width // 128),
        compiler_params=PARAMS,
        cost_estimate=cost(8),
    )(index, panel)


def bulk_kernel(count, index_ref, panel_ref, side_ref, *refs):
    blocks, (total_ref, stacked) = refs[:count], refs[count:]
    width = blocks[0].shape[0]
    strip = side_ref.shape[0]
    for f in range(count):
        stacked[f * width : (f + 1) * width, :] = blocks[f][...]
    for t in range(total_ref.shape[0] // strip):
        span = slice(t * strip, (t + 1) * strip)
        total_ref[span, :] = matmul(panel_ref[span, : count * width], stacked[...])
    own = pl.ds(pl.multiple_of(index_ref[1] * strip, strip), strip)
    total_ref[own, :] = total_ref[own, :] - side_ref[...]


def bulk(index, panel, side, blocks):
    count = len(blocks)
    width, nrhs = blocks[0].shape
    scratch = [pltpu.VMEM((count * width, nrhs), BF16)]
    kernel = functools.partial(bulk_kernel, count)
    return local(kernel, shape_of((panel.shape[0], nrhs), F32), [index, panel, side] + blocks, scratch, us=8)


def split_kernel(n_col, index_ref, panel_ref, block_ref, total_ref, kept_ref, sent_ref, scratch):
    chunk = kept_ref.shape[2]
    strip = scratch.shape[0]
    core = lax.rem(index_ref[1], 2)

    def tile(t, carry):
        span = pl.ds(pl.multiple_of(t * strip, strip), strip)
        scratch[...] = total_ref[span, :] + matmul(panel_ref[span, panel_ref.shape[1] - block_ref.shape[0] :], block_ref[...])
        for h in range(n_col // 2):
            kept_ref[h, span, :] = scratch[:, pl.ds(pl.multiple_of((2 * h + core) * chunk, chunk), chunk)]
            sent_ref[h, span, :] = scratch[:, pl.ds(pl.multiple_of((2 * h + 1 - core) * chunk, chunk), chunk)].astype(BF16)
        return carry

    lax.fori_loop(0, total_ref.shape[0] // strip, tile, 0)


def reduce_kernel(bit, index_ref, kept_ref, moved_ref, keep_ref, send_ref):
    mine = lax.rem(index_ref[0] // bit, 2)
    for h in range(keep_ref.shape[0]):
        keep_ref[h] = kept_ref[2 * h + mine] + moved_ref[2 * h + mine].astype(F32)
        send_ref[h] = (kept_ref[2 * h + 1 - mine] + moved_ref[2 * h + 1 - mine].astype(F32)).astype(BF16)


def reduce_step(bit, index, kept, moved):
    part = (kept.shape[0] // 2,) + kept.shape[1:]
    return pl.pallas_call(
        functools.partial(reduce_kernel, bit),
        out_shape=(shape_of(part, F32), shape_of(part, BF16)),
        in_specs=[SMEM, VMEM, VMEM],
        out_specs=(VMEM, VMEM),
        compiler_params=PARAMS,
        cost_estimate=cost(1),
    )(index, kept, moved)


def apply_strips(col, strips, value, store):
    refs, slot = strips
    width = refs[0].shape[1]
    for f, strip in enumerate(refs):
        span = pl.ds(pl.multiple_of((col ^ f) * width, width), width)
        store(span, matmul(strip[slot], value))


def store_solved(index_ref, strips, k, current_ref, solved_ref):
    def store(span, product):
        solved_ref[span, :] = product.astype(BF16)

    @pl.when(index_ref[0] == k)
    def _():
        apply_strips(index_ref[1], strips, current_ref[...].astype(BF16), store)

    @pl.when(index_ref[0] != k)
    def _():
        solved_ref[...] = jnp.zeros_like(solved_ref)


def subtract(index_ref, strips, value, chosen, source_ref, target_ref):
    def store(span, product):
        target_ref[span, :] = source_ref[span, :] - product

    @pl.when(chosen)
    def _():
        apply_strips(index_ref[1], strips, value, store)

    @pl.when(jnp.logical_not(chosen))
    def _():
        target_ref[...] = source_ref[...]


def added(parts):
    return functools.reduce(jnp.add, [part[...] for part in parts])


def start_kernel(n_col, index_ref, kept_ref, moved_ref, *refs):
    strips, (current_ref, solved_ref) = refs[:n_col], refs[n_col:]
    current_ref[...] = -(kept_ref[0] + moved_ref[0].astype(F32))
    store_solved(index_ref, (strips, 0), 0, current_ref, solved_ref)


def first_step_kernel(n_col, index_ref, current_ref, own_ref, value_ref, *refs):
    strips, (out_ref, solved_ref) = refs[:n_col], refs[n_col:]
    subtract(index_ref, (strips, 0), value_ref[...], index_ref[0] == 1, current_ref, out_ref)
    store_solved(index_ref, (strips, 1), 1, out_ref, solved_ref)

    @pl.when(index_ref[0] == 0)
    def _():
        solved_ref[...] = own_ref[...]


def between_kernel(n_col, index_ref, current_ref, value_ref, *refs):
    strips, (out_ref,) = refs[:n_col], refs[n_col:]
    subtract(index_ref, (strips, 0), value_ref[...], index_ref[0] == 2, current_ref, out_ref)


def copy_where(chosen, source_ref, target_ref):
    @pl.when(chosen)
    def _():
        target_ref[...] = source_ref[...]


def second_step_kernel(n_col, index_ref, current_ref, own_ref, first_ref, second_ref, *refs):
    strips, (out_ref, solved_ref, line_ref) = refs[:n_col], refs[n_col:]
    row = index_ref[0]
    subtract(index_ref, (strips, 1), first_ref[...], row == 2, current_ref, out_ref)
    store_solved(index_ref, (strips, 2), 2, out_ref, solved_ref)
    copy_where(row == 0, own_ref, solved_ref)
    copy_where(row == 3, second_ref, solved_ref)
    copy_where(row != 6, first_ref, line_ref)
    copy_where(row == 6, second_ref, line_ref)


def line_kernel(index_ref, own1_ref, own2_ref, z6_ref, z4_ref, z0_ref, out_ref):
    row = index_ref[0]
    copy_where(row == 0, z0_ref, out_ref)
    copy_where(row == 1, own1_ref, out_ref)
    copy_where((row == 2) | (row == 3), own2_ref, out_ref)
    copy_where((row == 4) | (row == 7), z4_ref, out_ref)
    copy_where((row == 5) | (row == 6), z6_ref, out_ref)


def update_either(index_ref, first, strips, value, source_ref, target_ref):
    row = index_ref[0]

    @pl.when((row > 2) & first)
    def _():
        subtract(index_ref, (strips, 1), value, row > 2, source_ref, target_ref)

    @pl.when((row > 2) & jnp.logical_not(first))
    def _():
        subtract(index_ref, (strips, 2), value, row > 2, source_ref, target_ref)

    @pl.when(row <= 2)
    def _():
        target_ref[...] = source_ref[...]


def middle_kernel(n_col, index_ref, current_ref, own0_ref, at1_ref, at2_ref, z0_ref, line0_ref, across0_ref, line_ref, *refs):
    strips, (out_ref, pieces_ref, known, between) = refs[:n_col], refs[n_col:]
    row = index_ref[0]
    for holder, part in enumerate((own0_ref, at1_ref, at2_ref, z0_ref, line0_ref, across0_ref, line0_ref, across0_ref)):
        copy_where(row == holder, part, known)
    subtract(index_ref, (strips, 0), known[...], row > 2, current_ref, between)
    update_either(index_ref, lax.rem(row, 2) == 1, strips, line_ref[...], between, out_ref)
    cut(index_ref, known, pieces_ref, 0)
    cut(index_ref, line_ref, pieces_ref, 1)


def finish_kernel(n_col, index_ref, current_ref, value_ref, *refs):
    strips, (pieces_ref, scratch) = refs[:n_col], refs[n_col:]
    update_either(index_ref, lax.rem(index_ref[0], 2) == 0, strips, value_ref[...], current_ref, scratch)
    cut(index_ref, value_ref, pieces_ref, 0)
    cut(index_ref, scratch, pieces_ref, 1)


def cut(index_ref, value_ref, pieces_ref, k):
    width = pieces_ref.shape[2]
    for f in range(pieces_ref.shape[0]):
        span = pl.ds(pl.multiple_of((index_ref[1] ^ f) * width, width), width)
        pieces_ref[f, k] = value_ref[span, :].astype(BF16)


def assemble_kernel(n_col, index_ref, *refs):
    groups, (solved_ref, remaining_ref) = refs[: 2 * n_col], refs[2 * n_col :]
    middle, late = groups[:n_col], groups[n_col:]
    chunk = middle[0].shape[2]
    odd = lax.rem(index_ref[0], 2)
    for f in range(n_col):
        span = pl.ds(pl.multiple_of((index_ref[1] ^ f) * chunk, chunk), chunk)
        solved_ref[0, :, span] = middle[f][0]
        solved_ref[2 - odd, :, span] = middle[f][1]
        solved_ref[1 + odd, :, span] = late[f][0]
        remaining_ref[:, span] = late[f][1].astype(F32)


def local(kernel, out_shape, operands, scratch=(), us=1):
    out_specs = jax.tree.map(lambda _: VMEM, out_shape)
    return pl.pallas_call(
        kernel,
        out_shape=out_shape,
        in_specs=[SMEM] + [VMEM] * (len(operands) - 1),
        out_specs=out_specs,
        scratch_shapes=list(scratch),
        compiler_params=PARAMS,
        cost_estimate=cost(us),
    )(*operands)


def hop(value, *pairs):
    return lax.ppermute(value, "row", pairs)


def gate(*values):
    return lax.optimization_barrier(values)


def swap_pieces(pieces, n_col):
    return [pieces[0]] + [flip(pieces[f], "col", n_col, f) for f in range(1, n_col)]


def fast(shape, right_side, earlier_panel, earlier_solution, window_panel, diag_inverse):
    n_row, n_col = shape
    step_count = diag_inverse.shape[0]
    row, col = lax.axis_index("row"), lax.axis_index("col")
    index = flat_index(row, col)
    strip, nrhs = right_side.shape
    rows = earlier_panel.shape[0]
    chunk = nrhs // n_col

    block = earlier_solution[0]
    own = jnp.stack([jnp.where(row == j, diag_inverse[j], window_panel[:, j, :]) for j in range(step_count)])
    over = flip(own, "col", n_col, 2)
    b4 = flip(block, "row", n_row, 4)
    b2 = flip(block, "row", n_row, 2)
    b1 = flip(block, "row", n_row, 1)
    b1, b2, again, panel = gate(b1, b2, block, earlier_panel)
    b6 = flip(again, "row", n_row, 6)
    b3 = flip(b2, "row", n_row, 1)
    panel = order_panel(index, panel)
    b3, b4, panel = gate(b3, b4, panel)
    b5 = flip(b4, "row", n_row, 1)
    b7 = flip(b6, "row", n_row, 1)
    total = bulk(index, panel, right_side, [block, b1, b2, b3, b4, b5, b6])
    total, b7 = gate(total, b7)
    part = (n_col // 2, rows, chunk)
    split = functools.partial(split_kernel, n_col)
    kept, sent = local(split, (shape_of(part, F32), shape_of(part, BF16)), [index, panel, b7, total], [pltpu.VMEM((strip, nrhs), F32)])
    moved = flip(sent, "col", n_col, 1)
    moved, over = gate(moved, over)
    kept, sent = reduce_step(2, flat_index(col), kept, moved)
    moved = flip(sent, "col", n_col, 2)
    slots = [own, flip(own, "col", n_col, 1), over, flip(over, "col", n_col, 1)]

    wide, narrow = shape_of((rows, chunk), F32), shape_of((rows, chunk), BF16)
    current, own0 = local(functools.partial(start_kernel, n_col), (wide, narrow), [index, kept, moved] + slots)
    at1, at2 = hop(own0, (0, 1)), hop(own0, (0, 2))
    step = functools.partial(first_step_kernel, n_col)
    current, own1 = local(step, (wide, narrow), [index, current, own0, at1] + slots)
    first, second = hop(own1, (1, 2), (0, 4)), hop(own1, (1, 3), (0, 6))
    current = local(functools.partial(between_kernel, n_col), wide, [index, current, at2] + slots, us=8)
    step = functools.partial(second_step_kernel, n_col)
    current, own2, line0 = local(step, (wide, narrow, narrow), [index, current, own0, first, second] + slots)
    z6 = hop(own2, (2, 6), (3, 5))
    z4 = hop(own2, (2, 4), (3, 7))
    z0 = hop(own2, (2, 0), (0, 3))
    across0 = hop(line0, (4, 5), (6, 7))
    line = local(line_kernel, narrow, [index, own1, own2, z6, z4, z0])
    across = flip(line, "row", n_row, 1)
    pieces = shape_of((n_col, 2, strip, chunk), BF16)
    middle = functools.partial(middle_kernel, n_col)
    parts = [own0, at1, at2, z0, line0, across0, line]
    scratch = [pltpu.VMEM((rows, chunk), BF16), pltpu.VMEM((rows, chunk), F32)]
    current, middle = local(middle, (wide, pieces), [index, current] + parts + slots, scratch, us=8)
    middle = swap_pieces(middle, n_col)
    across, *middle = gate(across, *middle)
    finish = functools.partial(finish_kernel, n_col)
    late = local(finish, pieces, [index, current, across] + slots, [pltpu.VMEM((rows, chunk), F32)])
    late = swap_pieces(late, n_col)
    outs = (shape_of((step_count, strip, nrhs), BF16), shape_of((strip, nrhs), F32))
    return local(functools.partial(assemble_kernel, n_col), outs, [index] + middle + late)


def solution(mesh):
    shape = (mesh.shape["row"], mesh.shape["col"])

    def step(*args):
        chunk = args[0].shape[1] // shape[1]
        plan = fast if shape == (8, 4) and chunk % 128 == 0 and args[4].shape[0] == 3 else on_device
        return plan(shape, *args)

    return jax.shard_map(
        step,
        mesh=mesh,
        in_specs=(
            P(("row", "col"), None),
            P("row", None, "col"),
            P("row", "col", None),
            P(("row", "col"), None, None),
            P(None, "col", None),
        ),
        out_specs=(P(None, "col", None), P(("row", "col"), None)),
        check_vma=False,
    )
```

```python
import functools

import jax
import jax.numpy as jnp
from jax import lax
from jax.experimental import pallas as pl
from jax.experimental.pallas import tpu as pltpu
from jax.sharding import PartitionSpec as P

F32 = jnp.float32
BF16 = jnp.bfloat16


def flip(value, axis, size, bit):
    return lax.ppermute(value, axis, [(i, i ^ bit) for i in range(size)])


def matmul(left, right):
    return jnp.dot(left, right, preferred_element_type=F32)


def halves(value, bit):
    kept = lax.dynamic_index_in_dim(value, bit, 0, keepdims=False)
    sent = lax.dynamic_index_in_dim(value, 1 - bit, 0, keepdims=False)
    return kept, sent


def gather_ordered(value, n_col, col):
    bit = n_col // 2
    bits = []
    while bit:
        bits.append(bit)
        bit //= 2
    order = [b for b in bits if b > 1] + [1]
    parts = {0: value}
    for b in order:
        moved = {f ^ b: flip(v, "col", n_col, b) for f, v in parts.items()}
        parts.update(moved)
    stacked = jnp.stack([parts[f] for f in range(n_col)])
    index = jnp.arange(n_col) ^ col
    return stacked[index].reshape(-1, value.shape[1])


def reduce_chunks(value, n_col, col):
    bit = 1
    while bit < n_col:
        rest = value.shape[0] // 2
        paired = value.reshape((rest, 2) + value.shape[1:]).swapaxes(0, 1)
        kept, sent = halves(paired, (col // bit) % 2)
        value = kept + flip(sent.astype(BF16), "col", n_col, bit).astype(F32)
        bit *= 2
    return value[0]


def gather_lines(block, n_row, row):
    per_line = 1
    while 4 * per_line * per_line <= n_row:
        per_line *= 2
    lines = n_row // per_line
    blocks = [(block, row)]
    up, down = block, block
    for s in range(1, lines):
        up = lax.ppermute(up, "row", [(i, i + per_line) for i in range((s - 1) * per_line, n_row - per_line)])
        down = lax.ppermute(down, "row", [(i, i - per_line) for i in range(per_line, n_row - (s - 1) * per_line)])
        blocks += [(up, row - s * per_line), (down, row + s * per_line)]
    for bit in range(1, per_line):
        blocks += [(flip(v, "row", n_row, bit), source ^ bit) for v, source in blocks[: 2 * lines - 1]]
    return blocks


def on_device(shape, right_side, earlier_panel, earlier_solution, window_panel, diag_inverse):
    n_row, n_col = shape
    step_count = diag_inverse.shape[0]
    row, col = lax.axis_index("row"), lax.axis_index("col")
    strip, nrhs = right_side.shape
    rows = earlier_panel.shape[0]
    chunk = nrhs // n_col
    weights = []
    for j in range(step_count):
        own = jnp.where(row == j, diag_inverse[j], window_panel[:, j, :])
        weights.append(gather_ordered(own, n_col, col))

    total = jnp.zeros((n_col, strip, nrhs), F32)
    total = lax.dynamic_update_index_in_dim(total, -right_side, col, 0).reshape(rows, nrhs)
    if n_row > 8:
        everything = lax.all_gather(earlier_solution, "row", axis=0, tiled=True)
        total = total + jnp.einsum("iqw,qwn->in", earlier_panel, everything, preferred_element_type=F32)
    else:
        panel = earlier_panel.swapaxes(0, 1)
        for v, source in gather_lines(earlier_solution[0], n_row, row):
            part = lax.dynamic_index_in_dim(panel, jnp.clip(source, 0, n_row - 1), 0, keepdims=False)
            total = total + matmul(part, v)
    chunks = total.reshape(rows, n_col, chunk).swapaxes(0, 1)
    current = -reduce_chunks(chunks, n_col, col)

    bases = [[1, 2, 4], [3, 1, 4], [6, 2, 1]]
    solved = []
    for k in range(step_count):
        value = matmul(weights[k], current.astype(BF16)).astype(BF16)
        have = [k]
        bits = [b for b in bases[k]] + [1 << i for i in range(3, 16) if (1 << i) < n_row]
        for b in bits:
            moved = lax.ppermute(value, "row", [(i, i ^ b) for i in have])
            into = jnp.zeros((), bool)
            for i in have:
                into |= row == (i ^ b)
            value = jnp.where(into, moved, value)
            have += [i ^ b for i in have]
        solved.append(value)
        current = jnp.where(row > k, current - matmul(weights[k], value), current)
    early = lax.all_to_all(jnp.stack(solved[:-1]), "col", 1, 2, tiled=True)
    late = lax.all_to_all(jnp.stack([solved[-1], current.astype(BF16)]), "col", 1, 2, tiled=True)
    return jnp.concatenate([early, late[:1]]), late[1].astype(F32)


def flat_index(*values):
    return jnp.stack([jnp.asarray(v, jnp.int32) for v in values])


PARAMS = pltpu.CompilerParams(vmem_limit_bytes=20 * 1024 * 1024)


def cost(us):
    return pl.CostEstimate(flops=0, bytes_accessed=int(us * 3.6e6), transcendentals=0)

SMEM = pl.BlockSpec(memory_space=pltpu.SMEM)
VMEM = pl.BlockSpec(memory_space=pltpu.VMEM)
HBM = pl.BlockSpec(memory_space=pltpu.HBM)


def shape_of(shape, dtype):
    return jax.ShapeDtypeStruct(shape, dtype)


def order_kernel(index_ref, panel_ref, out_ref, held, sems, *wide):
    tiles, tile, sources, width = held.shape
    row = index_ref[0]
    copies = [pltpu.make_async_copy(panel_ref.at[pl.ds(t * tile, tile)], held.at[t], sems.at[t]) for t in range(tiles)]
    for copy in copies:
        copy.start()
    for t, copy in enumerate(copies):
        copy.wait()
        for h, lanes in enumerate(wide):
            lanes[...] = held[t, :, :, h * 128 : (h + 1) * 128].astype(F32).reshape(tile * sources, 128)
            for j in range(sources):
                start = (j ^ row) * width + h * 128
                span = pl.ds(pl.multiple_of(start, 128), 128)
                out_ref[t * tile : (t + 1) * tile, span] = lanes[pl.ds(j, tile, stride=sources), :].astype(BF16)


def order_panel(index, panel, tiles=4):
    rows, sources, width = panel.shape
    tile = rows // tiles
    return pl.pallas_call(
        order_kernel,
        out_shape=shape_of((rows, sources * width), BF16),
        in_specs=[SMEM, HBM],
        out_specs=VMEM,
        scratch_shapes=[pltpu.VMEM((tiles, tile, sources, width), BF16), pltpu.SemaphoreType.DMA((tiles,))]
        + [pltpu.VMEM((tile * sources, 128), F32)] * (width // 128),
        compiler_params=PARAMS,
        cost_estimate=cost(8),
    )(index, panel)


def bulk_kernel(count, index_ref, panel_ref, side_ref, *refs):
    blocks, (total_ref, stacked) = refs[:count], refs[count:]
    width = blocks[0].shape[0]
    strip = side_ref.shape[0]
    for f in range(count):
        stacked[f * width : (f + 1) * width, :] = blocks[f][...]
    for t in range(total_ref.shape[0] // strip):
        span = slice(t * strip, (t + 1) * strip)
        total_ref[span, :] = matmul(panel_ref[span, : count * width], stacked[...])
    own = pl.ds(pl.multiple_of(index_ref[1] * strip, strip), strip)
    total_ref[own, :] = total_ref[own, :] - side_ref[...]


def bulk(index, panel, side, blocks):
    count = len(blocks)
    width, nrhs = blocks[0].shape
    scratch = [pltpu.VMEM((count * width, nrhs), BF16)]
    kernel = functools.partial(bulk_kernel, count)
    return local(kernel, shape_of((panel.shape[0], nrhs), F32), [index, panel, side] + blocks, scratch, us=8)


def split_kernel(n_col, index_ref, panel_ref, block_ref, total_ref, kept_ref, sent_ref, scratch):
    chunk = kept_ref.shape[2]
    strip = scratch.shape[0]
    core = lax.rem(index_ref[1], 2)

    def tile(t, carry):
        span = pl.ds(pl.multiple_of(t * strip, strip), strip)
        scratch[...] = total_ref[span, :] + matmul(panel_ref[span, panel_ref.shape[1] - block_ref.shape[0] :], block_ref[...])
        for h in range(n_col // 2):
            kept_ref[h, span, :] = scratch[:, pl.ds(pl.multiple_of((2 * h + core) * chunk, chunk), chunk)]
            sent_ref[h, span, :] = scratch[:, pl.ds(pl.multiple_of((2 * h + 1 - core) * chunk, chunk), chunk)].astype(BF16)
        return carry

    lax.fori_loop(0, total_ref.shape[0] // strip, tile, 0)


def reduce_kernel(bit, index_ref, kept_ref, moved_ref, keep_ref, also_ref, send_ref):
    mine = lax.rem(index_ref[1] // bit, 2)
    keep = kept_ref[mine] + moved_ref[mine].astype(F32)
    keep_ref[...] = keep
    also_ref[...] = keep.astype(BF16)
    send_ref[...] = (kept_ref[1 - mine] + moved_ref[1 - mine].astype(F32)).astype(BF16)


def apply_strips(col, strips, value, store):
    refs, slot = strips
    width = refs[0].shape[1]
    for f, strip in enumerate(refs):
        span = pl.ds(pl.multiple_of((col ^ f) * width, width), width)
        store(span, matmul(strip[slot], value))


def store_solved(index_ref, strips, k, current_ref, solved_ref):
    def store(span, product):
        solved_ref[span, :] = product.astype(BF16)

    @pl.when(index_ref[0] == k)
    def _():
        apply_strips(index_ref[1], strips, current_ref[...].astype(BF16), store)

    @pl.when(index_ref[0] != k)
    def _():
        solved_ref[...] = jnp.zeros_like(solved_ref)


def subtract(index_ref, strips, value, chosen, source_ref, target_ref):
    def store(span, product):
        target_ref[span, :] = source_ref[span, :] - product

    @pl.when(chosen)
    def _():
        apply_strips(index_ref[1], strips, value, store)

    @pl.when(jnp.logical_not(chosen))
    def _():
        target_ref[...] = source_ref[...]


def added(parts):
    return functools.reduce(jnp.add, [part[...] for part in parts])


def copy_where(chosen, source_ref, target_ref):
    @pl.when(chosen)
    def _():
        target_ref[...] = source_ref[...]


def product_kernel(n_col, index_ref, *refs):
    strips, (out_ref, right, last) = refs[:n_col], refs[n_col:]
    row, col = index_ref[0], index_ref[1]
    width = strips[0].shape[1]
    spans = [pl.ds(pl.multiple_of((col ^ f) * width, width), width) for f in range(n_col)]

    @pl.when(row == 1)
    def _():
        for span, strip in zip(spans, strips):
            right[span, :] = strip[0]
            last[span, :] = strip[2]
        for span, strip in zip(spans, strips):
            part = matmul(strip[1], right[...]).astype(BF16)
            out_ref[span, :] = matmul(part, last[...]).astype(BF16)

    @pl.when(row == 2)
    def _():
        for span, strip in zip(spans, strips):
            right[span, :] = strip[1]
        for span, strip in zip(spans, strips):
            out_ref[span, :] = matmul(strip[2], right[...]).astype(BF16)

    @pl.when((row < 1) | (row > 2))
    def _():
        out_ref[...] = jnp.zeros_like(out_ref)


def start_kernel(n_col, index_ref, kept_ref, moved_ref, *refs):
    strips, (current_ref, solved_ref, ahead_ref) = refs[:n_col], refs[n_col:]
    current_ref[...] = -(kept_ref[...] + moved_ref[...].astype(F32))
    store_solved(index_ref, (strips, 0), 0, current_ref, solved_ref)

    def store(span, product):
        ahead_ref[span, :] = product

    @pl.when(index_ref[0] == 1)
    def _():
        apply_strips(index_ref[1], (strips, 1), current_ref[...].astype(BF16), store)


def first_step_kernel(index_ref, own_ref, ahead_ref, product_ref, at1a_ref, at1b_ref, solved_ref):
    row = index_ref[0]

    @pl.when(row == 1)
    def _():
        rows0 = -(at1a_ref[...].astype(F32) + at1b_ref[...].astype(F32))
        solved_ref[...] = (ahead_ref[...] - matmul(product_ref[...], rows0.astype(BF16))).astype(BF16)

    copy_where(row == 0, own_ref, solved_ref)

    @pl.when(row > 1)
    def _():
        solved_ref[...] = jnp.zeros_like(solved_ref)


def between_kernel(n_col, index_ref, current_ref, value_ref, *refs):
    strips, (out_ref, ahead_ref) = refs[:n_col], refs[n_col:]
    row = index_ref[0]
    subtract(index_ref, (strips, 0), value_ref[...], row == 2, current_ref, out_ref)

    def store(span, product):
        ahead_ref[span, :] = product

    @pl.when(row == 2)
    def _():
        apply_strips(index_ref[1], (strips, 2), out_ref[...].astype(BF16), store)


def second_step_kernel(index_ref, own_ref, ahead_ref, product_ref, first_ref, second_ref, solved_ref, line_ref):
    row = index_ref[0]

    @pl.when(row == 2)
    def _():
        solved_ref[...] = (ahead_ref[...] - matmul(product_ref[...], first_ref[...])).astype(BF16)

    copy_where(row == 0, own_ref, solved_ref)
    copy_where(row == 3, second_ref, solved_ref)

    @pl.when((row == 1) | (row > 3))
    def _():
        solved_ref[...] = jnp.zeros_like(solved_ref)

    copy_where(row == 0, own_ref, line_ref)
    copy_where(row == 4, second_ref, line_ref)
    copy_where((row != 0) & (row != 4), first_ref, line_ref)


def line_kernel(index_ref, own1_ref, own2_ref, z6_ref, z4_ref, z0_ref, out_ref):
    row = index_ref[0]
    copy_where(row == 0, z0_ref, out_ref)
    copy_where(row == 1, own1_ref, out_ref)
    copy_where((row == 2) | (row == 3), own2_ref, out_ref)
    copy_where((row == 4) | (row == 7), z4_ref, out_ref)
    copy_where((row == 5) | (row == 6), z6_ref, out_ref)


def update_either(index_ref, first, strips, value, source_ref, target_ref):
    row = index_ref[0]

    @pl.when((row > 2) & first)
    def _():
        subtract(index_ref, (strips, 1), value, row > 2, source_ref, target_ref)

    @pl.when((row > 2) & jnp.logical_not(first))
    def _():
        subtract(index_ref, (strips, 2), value, row > 2, source_ref, target_ref)

    @pl.when(row <= 2)
    def _():
        target_ref[...] = source_ref[...]


def middle_kernel(n_col, index_ref, current_ref, own0_ref, at2_ref, z0_ref, line0_ref, across0_ref, first_ref, line_ref, *refs):
    strips, (out_ref, pieces_ref, known, between) = refs[:n_col], refs[n_col:]
    row = index_ref[0]
    for holder, part in enumerate((own0_ref, across0_ref, at2_ref, z0_ref, line0_ref, across0_ref, line0_ref, across0_ref)):
        copy_where(row == holder, part, known)
    subtract(index_ref, (strips, 0), known[...], (row == 1) | (row > 2), current_ref, between)
    update_either(index_ref, lax.rem(row, 2) == 1, strips, line_ref[...], between, out_ref)

    @pl.when(row == 2)
    def _():
        subtract(index_ref, (strips, 1), first_ref[...], row == 2, between, out_ref)

    cut(index_ref, known, pieces_ref, 0)
    cut(index_ref, line_ref, pieces_ref, 1)


def finish_kernel(n_col, index_ref, current_ref, value_ref, *refs):
    strips, (pieces_ref, scratch) = refs[:n_col], refs[n_col:]
    update_either(index_ref, lax.rem(index_ref[0], 2) == 0, strips, value_ref[...], current_ref, scratch)
    cut(index_ref, value_ref, pieces_ref, 0)
    cut(index_ref, scratch, pieces_ref, 1)


def cut(index_ref, value_ref, pieces_ref, k):
    width = pieces_ref.shape[2]
    for f in range(pieces_ref.shape[0]):
        span = pl.ds(pl.multiple_of((index_ref[1] ^ f) * width, width), width)
        pieces_ref[f, k] = value_ref[span, :].astype(BF16)


def assemble_kernel(n_col, index_ref, *refs):
    groups, (solved_ref, remaining_ref) = refs[: 2 * n_col], refs[2 * n_col :]
    middle, late = groups[:n_col], groups[n_col:]
    chunk = middle[0].shape[2]
    odd = lax.rem(index_ref[0], 2)
    for f in range(n_col):
        span = pl.ds(pl.multiple_of((index_ref[1] ^ f) * chunk, chunk), chunk)
        solved_ref[0, :, span] = middle[f][0]
        solved_ref[2 - odd, :, span] = middle[f][1]
        solved_ref[1 + odd, :, span] = late[f][0]
        remaining_ref[:, span] = late[f][1].astype(F32)


def local(kernel, out_shape, operands, scratch=(), us=1):
    out_specs = jax.tree.map(lambda _: VMEM, out_shape)
    return pl.pallas_call(
        kernel,
        out_shape=out_shape,
        in_specs=[SMEM] + [VMEM] * (len(operands) - 1),
        out_specs=out_specs,
        scratch_shapes=list(scratch),
        compiler_params=PARAMS,
        cost_estimate=cost(us),
    )(*operands)


def hop(value, *pairs):
    return lax.ppermute(value, "row", pairs)


def gate(*values):
    return lax.optimization_barrier(values)


def swap_pieces(pieces, n_col):
    return [pieces[0]] + [flip(pieces[f], "col", n_col, f) for f in range(1, n_col)]


def fast(shape, right_side, earlier_panel, earlier_solution, window_panel, diag_inverse):
    n_row, n_col = shape
    step_count = diag_inverse.shape[0]
    row, col = lax.axis_index("row"), lax.axis_index("col")
    index = flat_index(row, col)
    strip, nrhs = right_side.shape
    rows = earlier_panel.shape[0]
    chunk = nrhs // n_col

    block = earlier_solution[0]
    own = [jnp.where(row == j, diag_inverse[j], window_panel[:, j, :]) for j in range(step_count)]
    own = jnp.stack(own[:2] + [jnp.where(row == 1, diag_inverse[0], own[2])])
    over = flip(own, "col", n_col, 2)
    b4 = flip(block, "row", n_row, 4)
    b2 = flip(block, "row", n_row, 2)
    b1 = flip(block, "row", n_row, 1)
    panel = order_panel(index, earlier_panel)
    b1, b2, again, panel = gate(b1, b2, block, panel)
    b6 = flip(again, "row", n_row, 6)
    b3 = flip(b2, "row", n_row, 1)
    b5 = flip(b4, "row", n_row, 1)
    b7 = flip(b6, "row", n_row, 1)
    total = bulk(index, panel, right_side, [block, b1, b2, b3, b4, b5, b6])
    total, b7 = gate(total, b7)
    part = (n_col // 2, rows, chunk)
    split = functools.partial(split_kernel, n_col)
    kept, sent = local(split, (shape_of(part, F32), shape_of(part, BF16)), [index, panel, b7, total], [pltpu.VMEM((strip, nrhs), F32)])
    moved = flip(sent, "col", n_col, 1)
    moved, over = gate(moved, over)
    slots = [own, flip(own, "col", n_col, 1), over, flip(over, "col", n_col, 1)]
    wide, narrow = shape_of((rows, chunk), F32), shape_of((rows, chunk), BF16)
    kept, also, sent = local(functools.partial(reduce_kernel, 2), (wide, narrow, narrow), [index, kept, moved])
    at1a = hop(also, (0, 1))
    at1b = lax.ppermute(sent, ("row", "col"), [(c, n_col + (c ^ 2)) for c in range(n_col)])
    moved = flip(sent, "col", n_col, 2)
    scratch = [pltpu.VMEM((rows, rows), BF16)] * 2
    product = local(functools.partial(product_kernel, n_col), shape_of((rows, rows), BF16), [index] + slots, scratch, us=8)

    kept, product = gate(kept, product)
    start = functools.partial(start_kernel, n_col)
    current, own0, ahead = local(start, (wide, narrow, wide), [index, kept, moved] + slots)
    at2 = hop(own0, (0, 2))
    own1 = local(first_step_kernel, narrow, [index, own0, ahead, product, at1a, at1b])
    first, second = hop(own1, (1, 2), (0, 6)), hop(own1, (1, 3), (0, 4))
    between = functools.partial(between_kernel, n_col)
    current, ahead = local(between, (wide, wide), [index, current, at2] + slots, us=8)
    own2, line0 = local(second_step_kernel, (narrow, narrow), [index, own0, ahead, product, first, second])
    z6 = hop(own2, (2, 6), (3, 5))
    z4 = hop(own2, (2, 4), (3, 7))
    z0 = hop(own2, (2, 0), (0, 3))
    across0 = hop(line0, (0, 1), (4, 5), (6, 7))
    line = local(line_kernel, narrow, [index, own1, own2, z6, z4, z0])
    across = flip(line, "row", n_row, 1)
    pieces = shape_of((n_col, 2, strip, chunk), BF16)
    middle = functools.partial(middle_kernel, n_col)
    parts = [own0, at2, z0, line0, across0, first, line]
    scratch = [pltpu.VMEM((rows, chunk), BF16), pltpu.VMEM((rows, chunk), F32)]
    current, middle = local(middle, (wide, pieces), [index, current] + parts + slots, scratch, us=8)
    middle = swap_pieces(middle, n_col)
    across, *middle = gate(across, *middle)
    finish = functools.partial(finish_kernel, n_col)
    late = local(finish, pieces, [index, current, across] + slots, [pltpu.VMEM((rows, chunk), F32)])
    late = swap_pieces(late, n_col)
    outs = (shape_of((step_count, strip, nrhs), BF16), shape_of((strip, nrhs), F32))
    return local(functools.partial(assemble_kernel, n_col), outs, [index] + middle + late)


def solution(mesh):
    shape = (mesh.shape["row"], mesh.shape["col"])

    def step(*args):
        chunk = args[0].shape[1] // shape[1]
        plan = fast if shape == (8, 4) and chunk % 128 == 0 and args[4].shape[0] == 3 else on_device
        return plan(shape, *args)

    return jax.shard_map(
        step,
        mesh=mesh,
        in_specs=(
            P(("row", "col"), None),
            P("row", None, "col"),
            P("row", "col", None),
            P(("row", "col"), None, None),
            P(None, "col", None),
        ),
        out_specs=(P(None, "col", None), P(("row", "col"), None)),
        check_vma=False,
    )
```

```python
import functools

import jax
import jax.numpy as jnp
from jax import lax
from jax.experimental import pallas as pl
from jax.experimental.pallas import tpu as pltpu
from jax.sharding import PartitionSpec as P

F32 = jnp.float32
BF16 = jnp.bfloat16


def flip(value, axis, size, bit):
    return lax.ppermute(value, axis, [(i, i ^ bit) for i in range(size)])


def matmul(left, right):
    return jnp.dot(left, right, preferred_element_type=F32)


def halves(value, bit):
    kept = lax.dynamic_index_in_dim(value, bit, 0, keepdims=False)
    sent = lax.dynamic_index_in_dim(value, 1 - bit, 0, keepdims=False)
    return kept, sent


def gather_ordered(value, n_col, col):
    bit = n_col // 2
    bits = []
    while bit:
        bits.append(bit)
        bit //= 2
    order = [b for b in bits if b > 1] + [1]
    parts = {0: value}
    for b in order:
        moved = {f ^ b: flip(v, "col", n_col, b) for f, v in parts.items()}
        parts.update(moved)
    stacked = jnp.stack([parts[f] for f in range(n_col)])
    index = jnp.arange(n_col) ^ col
    return stacked[index].reshape(-1, value.shape[1])


def reduce_chunks(value, n_col, col):
    bit = 1
    while bit < n_col:
        rest = value.shape[0] // 2
        paired = value.reshape((rest, 2) + value.shape[1:]).swapaxes(0, 1)
        kept, sent = halves(paired, (col // bit) % 2)
        value = kept + flip(sent.astype(BF16), "col", n_col, bit).astype(F32)
        bit *= 2
    return value[0]


def gather_lines(block, n_row, row):
    per_line = 1
    while 4 * per_line * per_line <= n_row:
        per_line *= 2
    lines = n_row // per_line
    blocks = [(block, row)]
    up, down = block, block
    for s in range(1, lines):
        up = lax.ppermute(up, "row", [(i, i + per_line) for i in range((s - 1) * per_line, n_row - per_line)])
        down = lax.ppermute(down, "row", [(i, i - per_line) for i in range(per_line, n_row - (s - 1) * per_line)])
        blocks += [(up, row - s * per_line), (down, row + s * per_line)]
    for bit in range(1, per_line):
        blocks += [(flip(v, "row", n_row, bit), source ^ bit) for v, source in blocks[: 2 * lines - 1]]
    return blocks


def on_device(shape, right_side, earlier_panel, earlier_solution, window_panel, diag_inverse):
    n_row, n_col = shape
    step_count = diag_inverse.shape[0]
    row, col = lax.axis_index("row"), lax.axis_index("col")
    strip, nrhs = right_side.shape
    rows = earlier_panel.shape[0]
    chunk = nrhs // n_col
    weights = []
    for j in range(step_count):
        own = jnp.where(row == j, diag_inverse[j], window_panel[:, j, :])
        weights.append(gather_ordered(own, n_col, col))

    total = jnp.zeros((n_col, strip, nrhs), F32)
    total = lax.dynamic_update_index_in_dim(total, -right_side, col, 0).reshape(rows, nrhs)
    if n_row > 8:
        everything = lax.all_gather(earlier_solution, "row", axis=0, tiled=True)
        total = total + jnp.einsum("iqw,qwn->in", earlier_panel, everything, preferred_element_type=F32)
    else:
        panel = earlier_panel.swapaxes(0, 1)
        for v, source in gather_lines(earlier_solution[0], n_row, row):
            part = lax.dynamic_index_in_dim(panel, jnp.clip(source, 0, n_row - 1), 0, keepdims=False)
            total = total + matmul(part, v)
    chunks = total.reshape(rows, n_col, chunk).swapaxes(0, 1)
    current = -reduce_chunks(chunks, n_col, col)

    bases = [[1, 2, 4], [3, 1, 4], [6, 2, 1]]
    solved = []
    for k in range(step_count):
        value = matmul(weights[k], current.astype(BF16)).astype(BF16)
        have = [k]
        bits = [b for b in bases[k]] + [1 << i for i in range(3, 16) if (1 << i) < n_row]
        for b in bits:
            moved = lax.ppermute(value, "row", [(i, i ^ b) for i in have])
            into = jnp.zeros((), bool)
            for i in have:
                into |= row == (i ^ b)
            value = jnp.where(into, moved, value)
            have += [i ^ b for i in have]
        solved.append(value)
        current = jnp.where(row > k, current - matmul(weights[k], value), current)
    early = lax.all_to_all(jnp.stack(solved[:-1]), "col", 1, 2, tiled=True)
    late = lax.all_to_all(jnp.stack([solved[-1], current.astype(BF16)]), "col", 1, 2, tiled=True)
    return jnp.concatenate([early, late[:1]]), late[1].astype(F32)


def flat_index(*values):
    return jnp.stack([jnp.asarray(v, jnp.int32) for v in values])


PARAMS = pltpu.CompilerParams(vmem_limit_bytes=20 * 1024 * 1024)


def cost(us):
    return pl.CostEstimate(flops=0, bytes_accessed=int(us * 3.6e6), transcendentals=0)

SMEM = pl.BlockSpec(memory_space=pltpu.SMEM)
VMEM = pl.BlockSpec(memory_space=pltpu.VMEM)
HBM = pl.BlockSpec(memory_space=pltpu.HBM)


def shape_of(shape, dtype):
    return jax.ShapeDtypeStruct(shape, dtype)


def order_kernel(index_ref, panel_ref, out_ref, held, sems, *wide):
    tiles, tile, sources, width = held.shape
    row = index_ref[0]
    copies = [pltpu.make_async_copy(panel_ref.at[pl.ds(t * tile, tile)], held.at[t], sems.at[t]) for t in range(tiles)]
    for copy in copies:
        copy.start()
    for t, copy in enumerate(copies):
        copy.wait()
        for h, lanes in enumerate(wide):
            lanes[...] = held[t, :, :, h * 128 : (h + 1) * 128].astype(F32).reshape(tile * sources, 128)
            for j in range(sources):
                start = (j ^ row) * width + h * 128
                span = pl.ds(pl.multiple_of(start, 128), 128)
                out_ref[t * tile : (t + 1) * tile, span] = lanes[pl.ds(j, tile, stride=sources), :].astype(BF16)


def order_panel(index, panel, tiles=4):
    rows, sources, width = panel.shape
    tile = rows // tiles
    return pl.pallas_call(
        order_kernel,
        out_shape=shape_of((rows, sources * width), BF16),
        in_specs=[SMEM, HBM],
        out_specs=VMEM,
        scratch_shapes=[pltpu.VMEM((tiles, tile, sources, width), BF16), pltpu.SemaphoreType.DMA((tiles,))]
        + [pltpu.VMEM((tile * sources, 128), F32)] * (width // 128),
        compiler_params=PARAMS,
        cost_estimate=cost(8),
    )(index, panel)


def bulk_kernel(count, index_ref, panel_ref, side_ref, *refs):
    blocks, (total_ref, stacked) = refs[:count], refs[count:]
    width = blocks[0].shape[0]
    strip = side_ref.shape[0]
    for f in range(count):
        stacked[f * width : (f + 1) * width, :] = blocks[f][...]
    for t in range(total_ref.shape[0] // strip):
        span = slice(t * strip, (t + 1) * strip)
        total_ref[span, :] = matmul(panel_ref[span, : count * width], stacked[...])
    own = pl.ds(pl.multiple_of(index_ref[1] * strip, strip), strip)
    total_ref[own, :] = total_ref[own, :] - side_ref[...]


def bulk(index, panel, side, blocks):
    count = len(blocks)
    width, nrhs = blocks[0].shape
    scratch = [pltpu.VMEM((count * width, nrhs), BF16)]
    kernel = functools.partial(bulk_kernel, count)
    return local(kernel, shape_of((panel.shape[0], nrhs), F32), [index, panel, side] + blocks, scratch, us=8)


def split_kernel(n_col, index_ref, panel_ref, block_ref, total_ref, kept_ref, sent_ref, scratch):
    chunk = kept_ref.shape[2]
    strip = scratch.shape[0]
    core = lax.rem(index_ref[1], 2)

    def tile(t, carry):
        span = pl.ds(pl.multiple_of(t * strip, strip), strip)
        scratch[...] = total_ref[span, :] + matmul(panel_ref[span, panel_ref.shape[1] - block_ref.shape[0] :], block_ref[...])
        for h in range(n_col // 2):
            kept_ref[h, span, :] = scratch[:, pl.ds(pl.multiple_of((2 * h + core) * chunk, chunk), chunk)]
            sent_ref[h, span, :] = scratch[:, pl.ds(pl.multiple_of((2 * h + 1 - core) * chunk, chunk), chunk)].astype(BF16)
        return carry

    lax.fori_loop(0, total_ref.shape[0] // strip, tile, 0)


def reduce_kernel(bit, index_ref, kept_ref, moved_ref, keep_ref, also_ref, send_ref):
    mine = lax.rem(index_ref[1] // bit, 2)
    keep = kept_ref[mine] + moved_ref[mine].astype(F32)
    keep_ref[...] = keep
    also_ref[...] = keep.astype(BF16)
    send_ref[...] = (kept_ref[1 - mine] + moved_ref[1 - mine].astype(F32)).astype(BF16)


def apply_strips(col, strips, value, store):
    refs, slot = strips
    width = refs[0].shape[1]
    for f, strip in enumerate(refs):
        span = pl.ds(pl.multiple_of((col ^ f) * width, width), width)
        store(span, matmul(strip[slot], value))


def store_solved(index_ref, strips, k, current_ref, solved_ref):
    def store(span, product):
        solved_ref[span, :] = product.astype(BF16)

    @pl.when(index_ref[0] == k)
    def _():
        apply_strips(index_ref[1], strips, current_ref[...].astype(BF16), store)

    @pl.when(index_ref[0] != k)
    def _():
        solved_ref[...] = jnp.zeros_like(solved_ref)


def subtract(index_ref, strips, value, chosen, source_ref, target_ref):
    def store(span, product):
        target_ref[span, :] = source_ref[span, :] - product

    @pl.when(chosen)
    def _():
        apply_strips(index_ref[1], strips, value, store)

    @pl.when(jnp.logical_not(chosen))
    def _():
        target_ref[...] = source_ref[...]


def added(parts):
    return functools.reduce(jnp.add, [part[...] for part in parts])


def copy_where(chosen, source_ref, target_ref):
    @pl.when(chosen)
    def _():
        target_ref[...] = source_ref[...]


def product_kernel(n_col, index_ref, *refs):
    strips, (out_ref, right, last) = refs[:n_col], refs[n_col:]
    row, col = index_ref[0], index_ref[1]
    width = strips[0].shape[1]
    spans = [pl.ds(pl.multiple_of((col ^ f) * width, width), width) for f in range(n_col)]

    @pl.when(row == 1)
    def _():
        for span, strip in zip(spans, strips):
            right[span, :] = strip[0]
            last[span, :] = strip[2]
        for span, strip in zip(spans, strips):
            part = matmul(strip[1], right[...]).astype(BF16)
            out_ref[span, :] = matmul(part, last[...]).astype(BF16)

    @pl.when(row == 2)
    def _():
        for span, strip in zip(spans, strips):
            right[span, :] = strip[1]
        for span, strip in zip(spans, strips):
            out_ref[span, :] = matmul(strip[2], right[...]).astype(BF16)

    @pl.when((row < 1) | (row > 2))
    def _():
        out_ref[...] = jnp.zeros_like(out_ref)


def start_kernel(n_col, index_ref, kept_ref, moved_ref, *refs):
    strips, (current_ref, solved_ref, ahead_ref) = refs[:n_col], refs[n_col:]
    current_ref[...] = -(kept_ref[...] + moved_ref[...].astype(F32))
    store_solved(index_ref, (strips, 0), 0, current_ref, solved_ref)

    def store(span, product):
        ahead_ref[span, :] = product

    @pl.when(index_ref[0] == 1)
    def _():
        apply_strips(index_ref[1], (strips, 1), current_ref[...].astype(BF16), store)


def first_step_kernel(index_ref, own_ref, ahead_ref, product_ref, at1a_ref, at1b_ref, solved_ref):
    row = index_ref[0]

    @pl.when(row == 1)
    def _():
        rows0 = -(at1a_ref[...].astype(F32) + at1b_ref[...].astype(F32))
        solved_ref[...] = (ahead_ref[...] - matmul(product_ref[...], rows0.astype(BF16))).astype(BF16)

    copy_where(row == 0, own_ref, solved_ref)

    @pl.when(row > 1)
    def _():
        solved_ref[...] = jnp.zeros_like(solved_ref)


def between_kernel(n_col, index_ref, current_ref, value_ref, *refs):
    strips, (out_ref, ahead_ref) = refs[:n_col], refs[n_col:]
    row = index_ref[0]
    subtract(index_ref, (strips, 0), value_ref[...], row == 2, current_ref, out_ref)

    def store(span, product):
        ahead_ref[span, :] = product

    @pl.when(row == 2)
    def _():
        apply_strips(index_ref[1], (strips, 2), out_ref[...].astype(BF16), store)


def second_step_kernel(index_ref, own_ref, ahead_ref, product_ref, first_ref, second_ref, solved_ref):
    row = index_ref[0]

    @pl.when(row == 2)
    def _():
        solved_ref[...] = (ahead_ref[...] - matmul(product_ref[...], first_ref[...])).astype(BF16)

    copy_where(row == 0, own_ref, solved_ref)
    copy_where(row == 3, second_ref, solved_ref)

    @pl.when((row == 1) | (row > 3))
    def _():
        solved_ref[...] = jnp.zeros_like(solved_ref)


def pick_kernel(holders, index_ref, *refs):
    parts, (out_ref,) = refs[:-1], refs[-1:]
    for row, part in enumerate(holders):
        copy_where(index_ref[0] == row, parts[part], out_ref)


def pick(index, holders, *parts):
    return local(functools.partial(pick_kernel, holders), shape_of(parts[0].shape, BF16), [index] + list(parts))


def update_either(index_ref, first, strips, value, source_ref, target_ref):
    row = index_ref[0]

    @pl.when((row > 2) & first)
    def _():
        subtract(index_ref, (strips, 1), value, row > 2, source_ref, target_ref)

    @pl.when((row > 2) & jnp.logical_not(first))
    def _():
        subtract(index_ref, (strips, 2), value, row > 2, source_ref, target_ref)

    @pl.when(row <= 2)
    def _():
        target_ref[...] = source_ref[...]


def middle_kernel(n_col, index_ref, current_ref, own0_ref, at2_ref, fourth_ref, line0_ref, across0_ref, first_ref, line_ref, *refs):
    strips, (out_ref, pieces_ref, known, between) = refs[:n_col], refs[n_col:]
    row = index_ref[0]
    for holder, part in enumerate((own0_ref, across0_ref, at2_ref, fourth_ref, line0_ref, across0_ref, line0_ref, across0_ref)):
        copy_where(row == holder, part, known)
    subtract(index_ref, (strips, 0), known[...], (row == 1) | (row > 2), current_ref, between)
    update_either(index_ref, lax.rem(row, 2) == 1, strips, line_ref[...], between, out_ref)

    @pl.when(row == 2)
    def _():
        subtract(index_ref, (strips, 1), first_ref[...], row == 2, between, out_ref)

    cut(index_ref, known, pieces_ref, 0)
    cut(index_ref, line_ref, pieces_ref, 1)


def finish_kernel(n_col, index_ref, current_ref, value_ref, *refs):
    strips, (pieces_ref, scratch) = refs[:n_col], refs[n_col:]
    update_either(index_ref, lax.rem(index_ref[0], 2) == 0, strips, value_ref[...], current_ref, scratch)
    cut(index_ref, value_ref, pieces_ref, 0)
    cut(index_ref, scratch, pieces_ref, 1)


def cut(index_ref, value_ref, pieces_ref, k):
    width = pieces_ref.shape[2]
    for f in range(pieces_ref.shape[0]):
        span = pl.ds(pl.multiple_of((index_ref[1] ^ f) * width, width), width)
        pieces_ref[f, k] = value_ref[span, :].astype(BF16)


def assemble_kernel(n_col, index_ref, *refs):
    groups, (solved_ref, remaining_ref, remaining, sems, last_sem) = refs[: 2 * n_col], refs[2 * n_col :]
    middle, late = groups[:n_col], groups[n_col:]
    chunk = middle[0].shape[2]
    odd = lax.rem(index_ref[0], 2)
    spans = [pl.ds(pl.multiple_of((index_ref[1] ^ f) * chunk, chunk), chunk) for f in range(n_col)]
    copies = []
    for f, span in enumerate(spans):
        for part, k in ((middle[f].at[0], 0), (middle[f].at[1], 2 - odd), (late[f].at[0], 1 + odd)):
            copies.append(pltpu.make_async_copy(part, solved_ref.at[k, :, span], sems.at[len(copies)]))
            copies[-1].start()
    for f, span in enumerate(spans):
        remaining[:, span] = late[f][1].astype(F32)
    copies.append(pltpu.make_async_copy(remaining, remaining_ref, last_sem))
    copies[-1].start()
    for copy in copies:
        copy.wait()


def assemble(index, middle, late, outs):
    n_col = len(middle)
    return pl.pallas_call(
        functools.partial(assemble_kernel, n_col),
        out_shape=outs,
        in_specs=[SMEM] + [VMEM] * (2 * n_col),
        out_specs=(HBM, HBM),
        scratch_shapes=[pltpu.VMEM(outs[1].shape, F32), pltpu.SemaphoreType.DMA((3 * n_col,)), pltpu.SemaphoreType.DMA],
        compiler_params=PARAMS,
        cost_estimate=cost(1),
    )(index, *middle, *late)


def local(kernel, out_shape, operands, scratch=(), us=1):
    out_specs = jax.tree.map(lambda _: VMEM, out_shape)
    return pl.pallas_call(
        kernel,
        out_shape=out_shape,
        in_specs=[SMEM] + [VMEM] * (len(operands) - 1),
        out_specs=out_specs,
        scratch_shapes=list(scratch),
        compiler_params=PARAMS,
        cost_estimate=cost(us),
    )(*operands)


def hop(value, *pairs):
    return lax.ppermute(value, "row", pairs)


def gate(*values):
    return lax.optimization_barrier(values)


def swap_pieces(pieces, n_col):
    return [pieces[0]] + [flip(pieces[f], "col", n_col, f) for f in range(1, n_col)]


def fast(shape, right_side, earlier_panel, earlier_solution, window_panel, diag_inverse):
    n_row, n_col = shape
    step_count = diag_inverse.shape[0]
    row, col = lax.axis_index("row"), lax.axis_index("col")
    index = flat_index(row, col)
    strip, nrhs = right_side.shape
    rows = earlier_panel.shape[0]
    chunk = nrhs // n_col

    block = earlier_solution[0]
    own = [jnp.where(row == j, diag_inverse[j], window_panel[:, j, :]) for j in range(step_count)]
    own = jnp.stack(own[:2] + [jnp.where(row == 1, diag_inverse[0], own[2])])
    over = flip(own, "col", n_col, 2)
    b4 = flip(block, "row", n_row, 4)
    b2 = flip(block, "row", n_row, 2)
    b1 = flip(block, "row", n_row, 1)
    panel = order_panel(index, earlier_panel)
    b2, again, panel = gate(b2, block, panel)
    b4, b1 = gate(b4, b1)
    b6 = flip(again, "row", n_row, 6)
    b3 = flip(b2, "row", n_row, 1)
    b5 = flip(b4, "row", n_row, 1)
    b7 = flip(b6, "row", n_row, 1)
    total = bulk(index, panel, right_side, [block, b1, b2, b3, b4, b5, b6])
    total, b7 = gate(total, b7)
    part = (n_col // 2, rows, chunk)
    split = functools.partial(split_kernel, n_col)
    kept, sent = local(split, (shape_of(part, F32), shape_of(part, BF16)), [index, panel, b7, total], [pltpu.VMEM((strip, nrhs), F32)])
    moved = flip(sent, "col", n_col, 1)
    moved, over = gate(moved, over)
    slots = [own, flip(own, "col", n_col, 1), over, flip(over, "col", n_col, 1)]
    wide, narrow = shape_of((rows, chunk), F32), shape_of((rows, chunk), BF16)
    kept, also, sent = local(functools.partial(reduce_kernel, 2), (wide, narrow, narrow), [index, kept, moved])
    at1a = hop(also, (0, 1))
    at1b = lax.ppermute(sent, ("row", "col"), [(c, n_col + (c ^ 2)) for c in range(n_col)])
    moved = flip(sent, "col", n_col, 2)
    scratch = [pltpu.VMEM((rows, rows), BF16)] * 2
    product = local(functools.partial(product_kernel, n_col), shape_of((rows, rows), BF16), [index] + slots, scratch, us=8)

    kept, product = gate(kept, product)
    start = functools.partial(start_kernel, n_col)
    current, own0, ahead = local(start, (wide, narrow, wide), [index, kept, moved] + slots)
    at2 = hop(own0, (0, 2))
    own1 = local(first_step_kernel, narrow, [index, own0, ahead, product, at1a, at1b])
    first, second = hop(own1, (1, 2), (0, 6)), hop(own1, (1, 3))
    third, fourth = hop(own1, (0, 4)), hop(own1, (1, 5), (0, 3))
    between = functools.partial(between_kernel, n_col)
    current, ahead = local(between, (wide, wide), [index, current, at2] + slots, us=8)
    own2 = local(second_step_kernel, narrow, [index, own0, ahead, product, first, second])
    z6 = hop(own2, (2, 6))
    z4 = hop(own2, (2, 4), (3, 7))
    z0 = hop(own2, (2, 0))
    line0 = pick(index, (0, 0, 0, 0, 1, 0, 2, 0), own0, third, first)
    across0 = hop(line0, (0, 1), (4, 5), (6, 7))
    line = pick(index, (5, 0, 1, 1, 3, 4, 2, 3), own1, own2, z6, z4, fourth, z0)
    across = flip(line, "row", n_row, 1)
    pieces = shape_of((n_col, 2, strip, chunk), BF16)
    middle = functools.partial(middle_kernel, n_col)
    parts = [own0, at2, fourth, line0, across0, first, line]
    scratch = [pltpu.VMEM((rows, chunk), BF16), pltpu.VMEM((rows, chunk), F32)]
    current, middle = local(middle, (wide, pieces), [index, current] + parts + slots, scratch, us=8)
    middle = swap_pieces(middle, n_col)
    across, *middle = gate(across, *middle)
    finish = functools.partial(finish_kernel, n_col)
    late = local(finish, pieces, [index, current, across] + slots, [pltpu.VMEM((rows, chunk), F32)])
    late = swap_pieces(late, n_col)
    outs = (shape_of((step_count, strip, nrhs), BF16), shape_of((strip, nrhs), F32))
    return assemble(index, middle, late, outs)


def solution(mesh):
    shape = (mesh.shape["row"], mesh.shape["col"])

    def step(*args):
        chunk = args[0].shape[1] // shape[1]
        plan = fast if shape == (8, 4) and chunk % 128 == 0 and args[4].shape[0] == 3 else on_device
        return plan(shape, *args)

    return jax.shard_map(
        step,
        mesh=mesh,
        in_specs=(
            P(("row", "col"), None),
            P("row", None, "col"),
            P("row", "col", None),
            P(("row", "col"), None, None),
            P(None, "col", None),
        ),
        out_specs=(P(None, "col", None), P(("row", "col"), None)),
        check_vma=False,
    )
```

```python
import functools

import jax
import jax.numpy as jnp
from jax import lax
from jax.experimental import pallas as pl
from jax.experimental.pallas import tpu as pltpu
from jax.sharding import PartitionSpec as P

F32 = jnp.float32
BF16 = jnp.bfloat16


def flip(value, axis, size, bit):
    return lax.ppermute(value, axis, [(i, i ^ bit) for i in range(size)])


def matmul(left, right):
    return jnp.dot(left, right, preferred_element_type=F32)


def halves(value, bit):
    kept = lax.dynamic_index_in_dim(value, bit, 0, keepdims=False)
    sent = lax.dynamic_index_in_dim(value, 1 - bit, 0, keepdims=False)
    return kept, sent


def gather_ordered(value, n_col, col):
    bit = n_col // 2
    bits = []
    while bit:
        bits.append(bit)
        bit //= 2
    order = [b for b in bits if b > 1] + [1]
    parts = {0: value}
    for b in order:
        moved = {f ^ b: flip(v, "col", n_col, b) for f, v in parts.items()}
        parts.update(moved)
    stacked = jnp.stack([parts[f] for f in range(n_col)])
    index = jnp.arange(n_col) ^ col
    return stacked[index].reshape(-1, value.shape[1])


def reduce_chunks(value, n_col, col):
    bit = 1
    while bit < n_col:
        rest = value.shape[0] // 2
        paired = value.reshape((rest, 2) + value.shape[1:]).swapaxes(0, 1)
        kept, sent = halves(paired, (col // bit) % 2)
        value = kept + flip(sent.astype(BF16), "col", n_col, bit).astype(F32)
        bit *= 2
    return value[0]


def gather_lines(block, n_row, row):
    per_line = 1
    while 4 * per_line * per_line <= n_row:
        per_line *= 2
    lines = n_row // per_line
    blocks = [(block, row)]
    up, down = block, block
    for s in range(1, lines):
        up = lax.ppermute(up, "row", [(i, i + per_line) for i in range((s - 1) * per_line, n_row - per_line)])
        down = lax.ppermute(down, "row", [(i, i - per_line) for i in range(per_line, n_row - (s - 1) * per_line)])
        blocks += [(up, row - s * per_line), (down, row + s * per_line)]
    for bit in range(1, per_line):
        blocks += [(flip(v, "row", n_row, bit), source ^ bit) for v, source in blocks[: 2 * lines - 1]]
    return blocks


def on_device(shape, right_side, earlier_panel, earlier_solution, window_panel, diag_inverse):
    n_row, n_col = shape
    step_count = diag_inverse.shape[0]
    row, col = lax.axis_index("row"), lax.axis_index("col")
    strip, nrhs = right_side.shape
    rows = earlier_panel.shape[0]
    chunk = nrhs // n_col
    weights = []
    for j in range(step_count):
        own = jnp.where(row == j, diag_inverse[j], window_panel[:, j, :])
        weights.append(gather_ordered(own, n_col, col))

    total = jnp.zeros((n_col, strip, nrhs), F32)
    total = lax.dynamic_update_index_in_dim(total, -right_side, col, 0).reshape(rows, nrhs)
    if n_row > 8:
        everything = lax.all_gather(earlier_solution, "row", axis=0, tiled=True)
        total = total + jnp.einsum("iqw,qwn->in", earlier_panel, everything, preferred_element_type=F32)
    else:
        panel = earlier_panel.swapaxes(0, 1)
        for v, source in gather_lines(earlier_solution[0], n_row, row):
            part = lax.dynamic_index_in_dim(panel, jnp.clip(source, 0, n_row - 1), 0, keepdims=False)
            total = total + matmul(part, v)
    chunks = total.reshape(rows, n_col, chunk).swapaxes(0, 1)
    current = -reduce_chunks(chunks, n_col, col)

    bases = [[1, 2, 4], [3, 1, 4], [6, 2, 1]]
    solved = []
    for k in range(step_count):
        value = matmul(weights[k], current.astype(BF16)).astype(BF16)
        have = [k]
        bits = [b for b in bases[k]] + [1 << i for i in range(3, 16) if (1 << i) < n_row]
        for b in bits:
            moved = lax.ppermute(value, "row", [(i, i ^ b) for i in have])
            into = jnp.zeros((), bool)
            for i in have:
                into |= row == (i ^ b)
            value = jnp.where(into, moved, value)
            have += [i ^ b for i in have]
        solved.append(value)
        current = jnp.where(row > k, current - matmul(weights[k], value), current)
    early = lax.all_to_all(jnp.stack(solved[:-1]), "col", 1, 2, tiled=True)
    late = lax.all_to_all(jnp.stack([solved[-1], current.astype(BF16)]), "col", 1, 2, tiled=True)
    return jnp.concatenate([early, late[:1]]), late[1].astype(F32)


def flat_index(*values):
    return jnp.stack([jnp.asarray(v, jnp.int32) for v in values])


PARAMS = pltpu.CompilerParams(vmem_limit_bytes=20 * 1024 * 1024)


def cost(us):
    return pl.CostEstimate(flops=0, bytes_accessed=int(us * 3.6e6), transcendentals=0)

SMEM = pl.BlockSpec(memory_space=pltpu.SMEM)
VMEM = pl.BlockSpec(memory_space=pltpu.VMEM)
HBM = pl.BlockSpec(memory_space=pltpu.HBM)


def shape_of(shape, dtype):
    return jax.ShapeDtypeStruct(shape, dtype)


def order_kernel(index_ref, panel_ref, out_ref, held, sems, *wide):
    tiles, tile, sources, width = held.shape
    row = index_ref[0]
    copies = [pltpu.make_async_copy(panel_ref.at[pl.ds(t * tile, tile)], held.at[t], sems.at[t]) for t in range(tiles)]
    for copy in copies:
        copy.start()
    for t, copy in enumerate(copies):
        copy.wait()
        for h, lanes in enumerate(wide):
            lanes[...] = held[t, :, :, h * 128 : (h + 1) * 128].astype(F32).reshape(tile * sources, 128)
            for j in range(sources):
                start = (j ^ row) * width + h * 128
                span = pl.ds(pl.multiple_of(start, 128), 128)
                out_ref[t * tile : (t + 1) * tile, span] = lanes[pl.ds(j, tile, stride=sources), :].astype(BF16)


def order_panel(index, panel, tiles=4):
    rows, sources, width = panel.shape
    tile = rows // tiles
    return pl.pallas_call(
        order_kernel,
        out_shape=shape_of((rows, sources * width), BF16),
        in_specs=[SMEM, HBM],
        out_specs=VMEM,
        scratch_shapes=[pltpu.VMEM((tiles, tile, sources, width), BF16), pltpu.SemaphoreType.DMA((tiles,))]
        + [pltpu.VMEM((tile * sources, 128), F32)] * (width // 128),
        compiler_params=PARAMS,
        cost_estimate=cost(8),
    )(index, panel)


def bulk_kernel(count, index_ref, panel_ref, side_ref, *refs):
    blocks, (total_ref, stacked) = refs[:count], refs[count:]
    width = blocks[0].shape[0]
    strip = side_ref.shape[0]
    for f in range(count):
        stacked[f * width : (f + 1) * width, :] = blocks[f][...]
    for t in range(total_ref.shape[0] // strip):
        span = slice(t * strip, (t + 1) * strip)
        total_ref[span, :] = matmul(panel_ref[span, : count * width], stacked[...])
    own = pl.ds(pl.multiple_of(index_ref[1] * strip, strip), strip)
    total_ref[own, :] = total_ref[own, :] - side_ref[...]


def bulk(index, panel, side, blocks):
    count = len(blocks)
    width, nrhs = blocks[0].shape
    scratch = [pltpu.VMEM((count * width, nrhs), BF16)]
    kernel = functools.partial(bulk_kernel, count)
    return local(kernel, shape_of((panel.shape[0], nrhs), F32), [index, panel, side] + blocks, scratch, us=8)


def split_kernel(n_col, index_ref, panel_ref, block_ref, total_ref, kept_ref, sent_ref, scratch):
    chunk = kept_ref.shape[2]
    strip = scratch.shape[0]
    core = lax.rem(index_ref[1], 2)

    def tile(t, carry):
        span = pl.ds(pl.multiple_of(t * strip, strip), strip)
        scratch[...] = total_ref[span, :] + matmul(panel_ref[span, panel_ref.shape[1] - block_ref.shape[0] :], block_ref[...])
        for h in range(n_col // 2):
            kept_ref[h, span, :] = scratch[:, pl.ds(pl.multiple_of((2 * h + core) * chunk, chunk), chunk)]
            sent_ref[h, span, :] = scratch[:, pl.ds(pl.multiple_of((2 * h + 1 - core) * chunk, chunk), chunk)].astype(BF16)
        return carry

    lax.fori_loop(0, total_ref.shape[0] // strip, tile, 0)


def reduce_kernel(bit, index_ref, kept_ref, moved_ref, keep_ref, also_ref, send_ref):
    mine = lax.rem(index_ref[1] // bit, 2)
    keep = kept_ref[mine] + moved_ref[mine].astype(F32)
    keep_ref[...] = keep
    also_ref[...] = keep.astype(BF16)
    send_ref[...] = (kept_ref[1 - mine] + moved_ref[1 - mine].astype(F32)).astype(BF16)


def apply_strips(col, strips, value, store):
    refs, slot = strips
    width = refs[0].shape[1]
    for f, strip in enumerate(refs):
        span = pl.ds(pl.multiple_of((col ^ f) * width, width), width)
        store(span, matmul(strip[slot], value))


def store_solved(index_ref, strips, k, current_ref, solved_ref):
    def store(span, product):
        solved_ref[span, :] = product.astype(BF16)

    @pl.when(index_ref[0] == k)
    def _():
        apply_strips(index_ref[1], strips, current_ref[...].astype(BF16), store)

    @pl.when(index_ref[0] != k)
    def _():
        solved_ref[...] = jnp.zeros_like(solved_ref)


def subtract(index_ref, strips, value, chosen, source_ref, target_ref):
    def store(span, product):
        target_ref[span, :] = source_ref[span, :] - product

    @pl.when(chosen)
    def _():
        apply_strips(index_ref[1], strips, value, store)

    @pl.when(jnp.logical_not(chosen))
    def _():
        target_ref[...] = source_ref[...]


def added(parts):
    return functools.reduce(jnp.add, [part[...] for part in parts])


def copy_where(chosen, source_ref, target_ref):
    @pl.when(chosen)
    def _():
        target_ref[...] = source_ref[...]


def product_kernel(n_col, index_ref, *refs):
    strips, (out_ref, right, last) = refs[:n_col], refs[n_col:]
    row, col = index_ref[0], index_ref[1]
    width = strips[0].shape[1]
    spans = [pl.ds(pl.multiple_of((col ^ f) * width, width), width) for f in range(n_col)]

    @pl.when(row == 1)
    def _():
        for span, strip in zip(spans, strips):
            right[span, :] = strip[0]
            last[span, :] = strip[2]
        for span, strip in zip(spans, strips):
            part = matmul(strip[1], right[...]).astype(BF16)
            out_ref[span, :] = matmul(part, last[...]).astype(BF16)

    @pl.when(row == 2)
    def _():
        for span, strip in zip(spans, strips):
            right[span, :] = strip[1]
        for span, strip in zip(spans, strips):
            out_ref[span, :] = matmul(strip[2], right[...]).astype(BF16)

    @pl.when((row < 1) | (row > 2))
    def _():
        out_ref[...] = jnp.zeros_like(out_ref)


def start_kernel(n_col, index_ref, kept_ref, moved_ref, *refs):
    strips, (current_ref, solved_ref, ahead_ref) = refs[:n_col], refs[n_col:]
    current_ref[...] = -(kept_ref[...] + moved_ref[...].astype(F32))
    store_solved(index_ref, (strips, 0), 0, current_ref, solved_ref)

    def store(span, product):
        ahead_ref[span, :] = product

    @pl.when(index_ref[0] == 1)
    def _():
        apply_strips(index_ref[1], (strips, 1), current_ref[...].astype(BF16), store)


def first_step_kernel(index_ref, own_ref, ahead_ref, product_ref, at1a_ref, at1b_ref, solved_ref):
    row = index_ref[0]

    @pl.when(row == 1)
    def _():
        rows0 = -(at1a_ref[...].astype(F32) + at1b_ref[...].astype(F32))
        solved_ref[...] = (ahead_ref[...] - matmul(product_ref[...], rows0.astype(BF16))).astype(BF16)

    copy_where(row == 0, own_ref, solved_ref)

    @pl.when(row > 1)
    def _():
        solved_ref[...] = jnp.zeros_like(solved_ref)


def between_kernel(n_col, index_ref, current_ref, value_ref, *refs):
    strips, (out_ref, ahead_ref) = refs[:n_col], refs[n_col:]
    row = index_ref[0]
    subtract(index_ref, (strips, 0), value_ref[...], row == 2, current_ref, out_ref)

    def store(span, product):
        ahead_ref[span, :] = product

    @pl.when(row == 2)
    def _():
        apply_strips(index_ref[1], (strips, 2), out_ref[...].astype(BF16), store)


def second_step_kernel(index_ref, own_ref, ahead_ref, product_ref, first_ref, second_ref, solved_ref):
    row = index_ref[0]

    @pl.when(row == 2)
    def _():
        solved_ref[...] = (ahead_ref[...] - matmul(product_ref[...], first_ref[...])).astype(BF16)

    copy_where(row == 0, own_ref, solved_ref)
    copy_where(row == 3, second_ref, solved_ref)

    @pl.when((row == 1) | (row > 3))
    def _():
        solved_ref[...] = jnp.zeros_like(solved_ref)


def pick_kernel(holders, index_ref, *refs):
    parts, (out_ref,) = refs[:-1], refs[-1:]
    for row, part in enumerate(holders):
        copy_where(index_ref[0] == row, parts[part], out_ref)


def pick(index, holders, *parts):
    return local(functools.partial(pick_kernel, holders), shape_of(parts[0].shape, BF16), [index] + list(parts))


def update_either(index_ref, first, strips, value, source_ref, target_ref):
    row = index_ref[0]

    @pl.when((row > 2) & first)
    def _():
        subtract(index_ref, (strips, 1), value, row > 2, source_ref, target_ref)

    @pl.when((row > 2) & jnp.logical_not(first))
    def _():
        subtract(index_ref, (strips, 2), value, row > 2, source_ref, target_ref)

    @pl.when(row <= 2)
    def _():
        target_ref[...] = source_ref[...]


def middle_kernel(n_col, index_ref, current_ref, own0_ref, at2_ref, fourth_ref, line0_ref, across0_ref, first_ref, line_ref, *refs):
    strips, (out_ref, pieces_ref, known, between) = refs[:n_col], refs[n_col:]
    row = index_ref[0]
    for holder, part in enumerate((own0_ref, across0_ref, at2_ref, fourth_ref, line0_ref, across0_ref, line0_ref, across0_ref)):
        copy_where(row == holder, part, known)
    subtract(index_ref, (strips, 0), known[...], (row == 1) | (row > 2), current_ref, between)
    update_either(index_ref, lax.rem(row, 2) == 1, strips, line_ref[...], between, out_ref)

    @pl.when(row == 2)
    def _():
        subtract(index_ref, (strips, 1), first_ref[...], row == 2, between, out_ref)

    cut(index_ref, known, pieces_ref, 0)
    cut(index_ref, line_ref, pieces_ref, 1)


def finish_kernel(n_col, index_ref, current_ref, value_ref, *refs):
    strips, (pieces_ref, scratch) = refs[:n_col], refs[n_col:]
    update_either(index_ref, lax.rem(index_ref[0], 2) == 0, strips, value_ref[...], current_ref, scratch)
    cut(index_ref, value_ref, pieces_ref, 0)
    cut(index_ref, scratch, pieces_ref, 1)


def cut(index_ref, value_ref, pieces_ref, k):
    width = pieces_ref.shape[2]
    for f in range(pieces_ref.shape[0]):
        span = pl.ds(pl.multiple_of((index_ref[1] ^ f) * width, width), width)
        pieces_ref[f, k] = value_ref[span, :].astype(BF16)


def assemble_kernel(n_col, index_ref, *refs):
    groups, (solved_ref, remaining_ref, remaining, sems, last_sem) = refs[: 2 * n_col], refs[2 * n_col :]
    middle, late = groups[:n_col], groups[n_col:]
    chunk = middle[0].shape[2]
    odd = lax.rem(index_ref[0], 2)
    spans = [pl.ds(pl.multiple_of((index_ref[1] ^ f) * chunk, chunk), chunk) for f in range(n_col)]
    copies = []
    for f, span in enumerate(spans):
        for part, k in ((middle[f].at[0], 0), (middle[f].at[1], 2 - odd), (late[f].at[0], 1 + odd)):
            copies.append(pltpu.make_async_copy(part, solved_ref.at[k, :, span], sems.at[len(copies)]))
            copies[-1].start()
    for f, span in enumerate(spans):
        remaining[:, span] = late[f][1].astype(F32)
    copies.append(pltpu.make_async_copy(remaining, remaining_ref, last_sem))
    copies[-1].start()
    for copy in copies:
        copy.wait()


def assemble(index, middle, late, outs):
    n_col = len(middle)
    return pl.pallas_call(
        functools.partial(assemble_kernel, n_col),
        out_shape=outs,
        in_specs=[SMEM] + [VMEM] * (2 * n_col),
        out_specs=(HBM, HBM),
        scratch_shapes=[pltpu.VMEM(outs[1].shape, F32), pltpu.SemaphoreType.DMA((3 * n_col,)), pltpu.SemaphoreType.DMA],
        compiler_params=PARAMS,
        cost_estimate=cost(1),
    )(index, *middle, *late)


def local(kernel, out_shape, operands, scratch=(), us=1):
    out_specs = jax.tree.map(lambda _: VMEM, out_shape)
    return pl.pallas_call(
        kernel,
        out_shape=out_shape,
        in_specs=[SMEM] + [VMEM] * (len(operands) - 1),
        out_specs=out_specs,
        scratch_shapes=list(scratch),
        compiler_params=PARAMS,
        cost_estimate=cost(us),
    )(*operands)


def hop(value, *pairs):
    return lax.ppermute(value, "row", pairs)


def gate(*values):
    return lax.optimization_barrier(values)


def swap_pieces(pieces, n_col):
    return [pieces[0]] + [flip(pieces[f], "col", n_col, f) for f in range(1, n_col)]


def fast(shape, right_side, earlier_panel, earlier_solution, window_panel, diag_inverse):
    n_row, n_col = shape
    step_count = diag_inverse.shape[0]
    row, col = lax.axis_index("row"), lax.axis_index("col")
    index = flat_index(row, col)
    strip, nrhs = right_side.shape
    rows = earlier_panel.shape[0]
    chunk = nrhs // n_col

    block = earlier_solution[0]
    own = [jnp.where(row == j, diag_inverse[j], window_panel[:, j, :]) for j in range(step_count)]
    own = jnp.stack(own[:2] + [jnp.where(row == 1, diag_inverse[0], own[2])])
    over = flip(own, "col", n_col, 2)
    b4 = flip(block, "row", n_row, 4)
    b2 = flip(block, "row", n_row, 2)
    b1 = flip(block, "row", n_row, 1)
    panel = order_panel(index, earlier_panel)
    b2, again, panel = gate(b2, block, panel)
    b4, b1 = gate(b4, b1)
    b6 = flip(again, "row", n_row, 6)
    b3 = flip(b2, "row", n_row, 1)
    b5 = flip(b4, "row", n_row, 1)
    b7 = flip(b6, "row", n_row, 1)
    total = bulk(index, panel, right_side, [block, b1, b2, b3, b4, b5, b6])
    total, b7 = gate(total, b7)
    part = (n_col // 2, rows, chunk)
    split = functools.partial(split_kernel, n_col)
    kept, sent = local(split, (shape_of(part, F32), shape_of(part, BF16)), [index, panel, b7, total], [pltpu.VMEM((strip, nrhs), F32)])
    moved = flip(sent, "col", n_col, 1)
    moved, over = gate(moved, over)
    slots = [own, flip(own, "col", n_col, 1), over, flip(over, "col", n_col, 1)]
    wide, narrow = shape_of((rows, chunk), F32), shape_of((rows, chunk), BF16)
    kept, also, sent = local(functools.partial(reduce_kernel, 2), (wide, narrow, narrow), [index, kept, moved])
    at1a = hop(also, (0, 1))
    at1b = lax.ppermute(sent, ("row", "col"), [(c, n_col + (c ^ 2)) for c in range(n_col)])
    moved = flip(sent, "col", n_col, 2)
    scratch = [pltpu.VMEM((rows, rows), BF16)] * 2
    product = local(functools.partial(product_kernel, n_col), shape_of((rows, rows), BF16), [index] + slots, scratch, us=8)

    kept, product = gate(kept, product)
    start = functools.partial(start_kernel, n_col)
    current, own0, ahead = local(start, (wide, narrow, wide), [index, kept, moved] + slots)
    at2 = hop(own0, (0, 2))
    own1 = local(first_step_kernel, narrow, [index, own0, ahead, product, at1a, at1b])
    first, second = hop(own1, (1, 2), (0, 6)), hop(own1, (1, 3))
    third, fourth = hop(own1, (0, 4)), hop(own1, (1, 5), (0, 3))
    between = functools.partial(between_kernel, n_col)
    current, ahead = local(between, (wide, wide), [index, current, at2] + slots, us=8)
    own2 = local(second_step_kernel, narrow, [index, own0, ahead, product, first, second])
    z6 = hop(own2, (2, 6))
    z4 = hop(own2, (2, 4), (3, 7))
    z0 = hop(own2, (2, 0))
    line0 = pick(index, (0, 0, 0, 0, 1, 0, 2, 0), own0, third, first)
    across0 = hop(line0, (0, 1), (4, 5), (6, 7))
    line = pick(index, (5, 0, 1, 1, 3, 4, 2, 3), own1, own2, z6, z4, fourth, z0)
    across = flip(line, "row", n_row, 1)
    pieces = shape_of((n_col, 2, strip, chunk), BF16)
    middle = functools.partial(middle_kernel, n_col)
    parts = [own0, at2, fourth, line0, across0, first, line]
    scratch = [pltpu.VMEM((rows, chunk), BF16), pltpu.VMEM((rows, chunk), F32)]
    current, middle = local(middle, (wide, pieces), [index, current] + parts + slots, scratch, us=8)
    middle = swap_pieces(middle, n_col)
    finish = functools.partial(finish_kernel, n_col)
    late = local(finish, pieces, [index, current, across] + slots, [pltpu.VMEM((rows, chunk), F32)])
    late = swap_pieces(late, n_col)
    outs = (shape_of((step_count, strip, nrhs), BF16), shape_of((strip, nrhs), F32))
    return assemble(index, middle, late, outs)


def solution(mesh):
    shape = (mesh.shape["row"], mesh.shape["col"])

    def step(*args):
        chunk = args[0].shape[1] // shape[1]
        plan = fast if shape == (8, 4) and chunk % 128 == 0 and args[4].shape[0] == 3 else on_device
        return plan(shape, *args)

    return jax.shard_map(
        step,
        mesh=mesh,
        in_specs=(
            P(("row", "col"), None),
            P("row", None, "col"),
            P("row", "col", None),
            P(("row", "col"), None, None),
            P(None, "col", None),
        ),
        out_specs=(P(None, "col", None), P(("row", "col"), None)),
        check_vma=False,
    )
```

```python
import functools

import jax
import jax.numpy as jnp
from jax import lax
from jax.experimental import pallas as pl
from jax.experimental.pallas import tpu as pltpu
from jax.sharding import PartitionSpec as P

F32 = jnp.float32
BF16 = jnp.bfloat16


def flip(value, axis, size, bit):
    return lax.ppermute(value, axis, [(i, i ^ bit) for i in range(size)])


def matmul(left, right):
    return jnp.dot(left, right, preferred_element_type=F32)


def halves(value, bit):
    kept = lax.dynamic_index_in_dim(value, bit, 0, keepdims=False)
    sent = lax.dynamic_index_in_dim(value, 1 - bit, 0, keepdims=False)
    return kept, sent


def gather_ordered(value, n_col, col):
    bit = n_col // 2
    bits = []
    while bit:
        bits.append(bit)
        bit //= 2
    order = [b for b in bits if b > 1] + [1]
    parts = {0: value}
    for b in order:
        moved = {f ^ b: flip(v, "col", n_col, b) for f, v in parts.items()}
        parts.update(moved)
    stacked = jnp.stack([parts[f] for f in range(n_col)])
    index = jnp.arange(n_col) ^ col
    return stacked[index].reshape(-1, value.shape[1])


def reduce_chunks(value, n_col, col):
    bit = 1
    while bit < n_col:
        rest = value.shape[0] // 2
        paired = value.reshape((rest, 2) + value.shape[1:]).swapaxes(0, 1)
        kept, sent = halves(paired, (col // bit) % 2)
        value = kept + flip(sent.astype(BF16), "col", n_col, bit).astype(F32)
        bit *= 2
    return value[0]


def gather_lines(block, n_row, row):
    per_line = 1
    while 4 * per_line * per_line <= n_row:
        per_line *= 2
    lines = n_row // per_line
    blocks = [(block, row)]
    up, down = block, block
    for s in range(1, lines):
        up = lax.ppermute(up, "row", [(i, i + per_line) for i in range((s - 1) * per_line, n_row - per_line)])
        down = lax.ppermute(down, "row", [(i, i - per_line) for i in range(per_line, n_row - (s - 1) * per_line)])
        blocks += [(up, row - s * per_line), (down, row + s * per_line)]
    for bit in range(1, per_line):
        blocks += [(flip(v, "row", n_row, bit), source ^ bit) for v, source in blocks[: 2 * lines - 1]]
    return blocks


def on_device(shape, right_side, earlier_panel, earlier_solution, window_panel, diag_inverse):
    n_row, n_col = shape
    step_count = diag_inverse.shape[0]
    row, col = lax.axis_index("row"), lax.axis_index("col")
    strip, nrhs = right_side.shape
    rows = earlier_panel.shape[0]
    chunk = nrhs // n_col
    weights = []
    for j in range(step_count):
        own = jnp.where(row == j, diag_inverse[j], window_panel[:, j, :])
        weights.append(gather_ordered(own, n_col, col))

    total = jnp.zeros((n_col, strip, nrhs), F32)
    total = lax.dynamic_update_index_in_dim(total, -right_side, col, 0).reshape(rows, nrhs)
    if n_row > 8:
        everything = lax.all_gather(earlier_solution, "row", axis=0, tiled=True)
        total = total + jnp.einsum("iqw,qwn->in", earlier_panel, everything, preferred_element_type=F32)
    else:
        panel = earlier_panel.swapaxes(0, 1)
        for v, source in gather_lines(earlier_solution[0], n_row, row):
            part = lax.dynamic_index_in_dim(panel, jnp.clip(source, 0, n_row - 1), 0, keepdims=False)
            total = total + matmul(part, v)
    chunks = total.reshape(rows, n_col, chunk).swapaxes(0, 1)
    current = -reduce_chunks(chunks, n_col, col)

    bases = [[1, 2, 4], [3, 1, 4], [6, 2, 1]]
    solved = []
    for k in range(step_count):
        value = matmul(weights[k], current.astype(BF16)).astype(BF16)
        have = [k]
        bits = [b for b in bases[k]] + [1 << i for i in range(3, 16) if (1 << i) < n_row]
        for b in bits:
            moved = lax.ppermute(value, "row", [(i, i ^ b) for i in have])
            into = jnp.zeros((), bool)
            for i in have:
                into |= row == (i ^ b)
            value = jnp.where(into, moved, value)
            have += [i ^ b for i in have]
        solved.append(value)
        current = jnp.where(row > k, current - matmul(weights[k], value), current)
    early = lax.all_to_all(jnp.stack(solved[:-1]), "col", 1, 2, tiled=True)
    late = lax.all_to_all(jnp.stack([solved[-1], current.astype(BF16)]), "col", 1, 2, tiled=True)
    return jnp.concatenate([early, late[:1]]), late[1].astype(F32)


def flat_index(*values):
    return jnp.stack([jnp.asarray(v, jnp.int32) for v in values])


PARAMS = pltpu.CompilerParams(vmem_limit_bytes=20 * 1024 * 1024)


def cost(us):
    return pl.CostEstimate(flops=0, bytes_accessed=int(us * 3.6e6), transcendentals=0)

SMEM = pl.BlockSpec(memory_space=pltpu.SMEM)
VMEM = pl.BlockSpec(memory_space=pltpu.VMEM)
HBM = pl.BlockSpec(memory_space=pltpu.HBM)


def shape_of(shape, dtype):
    return jax.ShapeDtypeStruct(shape, dtype)


def order_kernel(index_ref, panel_ref, out_ref, held, sems, *wide):
    tiles, tile, sources, width = held.shape
    row = index_ref[0]
    copies = [pltpu.make_async_copy(panel_ref.at[pl.ds(t * tile, tile)], held.at[t], sems.at[t]) for t in range(tiles)]
    for copy in copies:
        copy.start()
    for t, copy in enumerate(copies):
        copy.wait()
        for h, lanes in enumerate(wide):
            lanes[...] = held[t, :, :, h * 128 : (h + 1) * 128].astype(F32).reshape(tile * sources, 128)
            for j in range(sources):
                start = (j ^ row) * width + h * 128
                span = pl.ds(pl.multiple_of(start, 128), 128)
                out_ref[t * tile : (t + 1) * tile, span] = lanes[pl.ds(j, tile, stride=sources), :].astype(BF16)


def order_panel(index, panel, tiles=4):
    rows, sources, width = panel.shape
    tile = rows // tiles
    return pl.pallas_call(
        order_kernel,
        out_shape=shape_of((rows, sources * width), BF16),
        in_specs=[SMEM, HBM],
        out_specs=VMEM,
        scratch_shapes=[pltpu.VMEM((tiles, tile, sources, width), BF16), pltpu.SemaphoreType.DMA((tiles,))]
        + [pltpu.VMEM((tile * sources, 128), F32)] * (width // 128),
        compiler_params=PARAMS,
        cost_estimate=cost(8),
    )(index, panel)


def bulk_kernel(count, index_ref, panel_ref, side_ref, *refs):
    blocks, (total_ref, stacked) = refs[:count], refs[count:]
    width = blocks[0].shape[0]
    strip = side_ref.shape[0]
    for f in range(count):
        stacked[f * width : (f + 1) * width, :] = blocks[f][...]
    for t in range(total_ref.shape[0] // strip):
        span = slice(t * strip, (t + 1) * strip)
        total_ref[span, :] = matmul(panel_ref[span, : count * width], stacked[...])
    own = pl.ds(pl.multiple_of(index_ref[1] * strip, strip), strip)
    total_ref[own, :] = total_ref[own, :] - side_ref[...]


def bulk(index, panel, side, blocks):
    count = len(blocks)
    width, nrhs = blocks[0].shape
    scratch = [pltpu.VMEM((count * width, nrhs), BF16)]
    kernel = functools.partial(bulk_kernel, count)
    return local(kernel, shape_of((panel.shape[0], nrhs), F32), [index, panel, side] + blocks, scratch, us=8)


def split_kernel(n_col, index_ref, panel_ref, *refs):
    blocks, (total_ref, kept_ref, sent_ref) = refs[:-3], refs[-3:]
    chunk = kept_ref.shape[2]
    width = blocks[0].shape[0]
    strip = total_ref.shape[0] // n_col
    core = lax.rem(index_ref[1], 2)
    first = panel_ref.shape[1] - len(blocks) * width

    def tile(t, carry):
        span = pl.ds(pl.multiple_of(t * strip, strip), strip)
        total = total_ref[span, :]
        for b, block in enumerate(blocks):
            total = total + matmul(panel_ref[span, first + b * width : first + (b + 1) * width], block[...])
        for parity in range(2):

            @pl.when(core == parity)
            def _():
                for h in range(n_col // 2):
                    mine, other = 2 * h + parity, 2 * h + 1 - parity
                    kept_ref[h, span, :] = total[:, mine * chunk : (mine + 1) * chunk]
                    sent_ref[h, span, :] = total[:, other * chunk : (other + 1) * chunk].astype(BF16)

        return carry

    lax.fori_loop(0, n_col, tile, 0)


def reduce_kernel(bit, index_ref, kept_ref, moved_ref, keep_ref, also_ref, send_ref):
    mine = lax.rem(index_ref[1] // bit, 2)
    keep = kept_ref[mine] + moved_ref[mine].astype(F32)
    keep_ref[...] = keep
    also_ref[...] = keep.astype(BF16)
    send_ref[...] = (kept_ref[1 - mine] + moved_ref[1 - mine].astype(F32)).astype(BF16)


def apply_strips(col, strips, value, store):
    refs, slot = strips
    width = refs[0].shape[1]
    for f, strip in enumerate(refs):
        span = pl.ds(pl.multiple_of((col ^ f) * width, width), width)
        store(span, matmul(strip[slot], value))


def store_solved(index_ref, strips, k, current_ref, solved_ref):
    def store(span, product):
        solved_ref[span, :] = product.astype(BF16)

    @pl.when(index_ref[0] == k)
    def _():
        apply_strips(index_ref[1], strips, current_ref[...].astype(BF16), store)

    @pl.when(index_ref[0] != k)
    def _():
        solved_ref[...] = jnp.zeros_like(solved_ref)


def subtract(index_ref, strips, value, chosen, source_ref, target_ref):
    def store(span, product):
        target_ref[span, :] = source_ref[span, :] - product

    @pl.when(chosen)
    def _():
        apply_strips(index_ref[1], strips, value, store)

    @pl.when(jnp.logical_not(chosen))
    def _():
        target_ref[...] = source_ref[...]


def added(parts):
    return functools.reduce(jnp.add, [part[...] for part in parts])


def copy_where(chosen, source_ref, target_ref):
    @pl.when(chosen)
    def _():
        target_ref[...] = source_ref[...]


def product_kernel(n_col, index_ref, *refs):
    strips, (out_ref, right, last) = refs[:n_col], refs[n_col:]
    row, col = index_ref[0], index_ref[1]
    width = strips[0].shape[1]
    spans = [pl.ds(pl.multiple_of((col ^ f) * width, width), width) for f in range(n_col)]

    @pl.when(row == 1)
    def _():
        for span, strip in zip(spans, strips):
            right[span, :] = strip[0]
            last[span, :] = strip[2]
        for span, strip in zip(spans, strips):
            part = matmul(strip[1], right[...]).astype(BF16)
            out_ref[span, :] = matmul(part, last[...]).astype(BF16)

    @pl.when(row == 2)
    def _():
        for span, strip in zip(spans, strips):
            right[span, :] = strip[1]
        for span, strip in zip(spans, strips):
            out_ref[span, :] = matmul(strip[2], right[...]).astype(BF16)

    @pl.when((row < 1) | (row > 2))
    def _():
        out_ref[...] = jnp.zeros_like(out_ref)


def start_kernel(n_col, index_ref, kept_ref, moved_ref, *refs):
    strips, (current_ref, solved_ref, ahead_ref) = refs[:n_col], refs[n_col:]
    current_ref[...] = -(kept_ref[...] + moved_ref[...].astype(F32))
    store_solved(index_ref, (strips, 0), 0, current_ref, solved_ref)

    def store(span, product):
        ahead_ref[span, :] = product

    @pl.when(index_ref[0] == 1)
    def _():
        apply_strips(index_ref[1], (strips, 1), current_ref[...].astype(BF16), store)


def first_step_kernel(index_ref, own_ref, ahead_ref, product_ref, at1a_ref, at1b_ref, solved_ref):
    row = index_ref[0]

    @pl.when(row == 1)
    def _():
        rows0 = -(at1a_ref[...].astype(F32) + at1b_ref[...].astype(F32))
        solved_ref[...] = (ahead_ref[...] - matmul(product_ref[...], rows0.astype(BF16))).astype(BF16)

    copy_where(row == 0, own_ref, solved_ref)

    @pl.when(row > 1)
    def _():
        solved_ref[...] = jnp.zeros_like(solved_ref)


def between_kernel(n_col, index_ref, current_ref, value_ref, *refs):
    strips, (out_ref, ahead_ref) = refs[:n_col], refs[n_col:]
    row = index_ref[0]
    subtract(index_ref, (strips, 0), value_ref[...], row == 2, current_ref, out_ref)

    def store(span, product):
        ahead_ref[span, :] = product

    @pl.when(row == 2)
    def _():
        apply_strips(index_ref[1], (strips, 2), out_ref[...].astype(BF16), store)


def second_step_kernel(index_ref, own_ref, ahead_ref, product_ref, first_ref, second_ref, solved_ref):
    row = index_ref[0]

    @pl.when(row == 2)
    def _():
        solved_ref[...] = (ahead_ref[...] - matmul(product_ref[...], first_ref[...])).astype(BF16)

    copy_where(row == 0, own_ref, solved_ref)
    copy_where(row == 3, second_ref, solved_ref)

    @pl.when((row == 1) | (row > 3))
    def _():
        solved_ref[...] = jnp.zeros_like(solved_ref)


def pick_kernel(holders, index_ref, *refs):
    parts, (out_ref,) = refs[:-1], refs[-1:]
    for row, part in enumerate(holders):
        copy_where(index_ref[0] == row, parts[part], out_ref)


def pick(index, holders, *parts):
    return local(functools.partial(pick_kernel, holders), shape_of(parts[0].shape, BF16), [index] + list(parts))


def known_kernel(index_ref, own0_ref, at2_ref, fourth_ref, line0_ref, across0_ref, line_ref, known_ref, pieces_ref):
    row = index_ref[0]
    for holder, part in enumerate((own0_ref, across0_ref, at2_ref, fourth_ref, line0_ref, across0_ref, line0_ref, across0_ref)):
        copy_where(row == holder, part, known_ref)
    cut(index_ref, known_ref, pieces_ref, 0)
    cut(index_ref, line_ref, pieces_ref, 1)


def middle_kernel(n_col, index_ref, current_ref, known_ref, first_ref, line_ref, *refs):
    strips, (out_ref, between) = refs[:n_col], refs[n_col:]
    row = index_ref[0]
    odd = lax.rem(row, 2) == 1
    subtract(index_ref, (strips, 0), known_ref[...], (row == 1) | (row > 2), current_ref, between)
    copy_where(row < 2, between, out_ref)

    @pl.when(row == 2)
    def _():
        subtract(index_ref, (strips, 1), first_ref[...], row == 2, between, out_ref)

    for slot, mine in ((1, odd), (2, jnp.logical_not(odd))):

        @pl.when((row > 2) & mine)
        def _():
            subtract(index_ref, (strips, slot), line_ref[...], row > 2, between, out_ref)


def finish_kernel(distances, index_ref, current_ref, value_ref, *refs):
    strips, (pieces_ref,) = refs[:-1], refs[-1:]
    row, col = index_ref[0], index_ref[1]
    odd = lax.rem(row, 2) == 1
    width = pieces_ref.shape[2]
    for i, (f, strip) in enumerate(zip(distances, strips)):
        span = pl.ds(pl.multiple_of((col ^ f) * width, width), width)
        pieces_ref[i, 0] = value_ref[span, :]

        @pl.when(row <= 2)
        def _():
            pieces_ref[i, 1] = current_ref[span, :].astype(BF16)

        for slot, mine in ((2, odd), (1, jnp.logical_not(odd))):

            @pl.when((row > 2) & mine)
            def _():
                pieces_ref[i, 1] = (current_ref[span, :] - matmul(strip[slot], value_ref[...])).astype(BF16)


def cut(index_ref, value_ref, pieces_ref, k):
    width = pieces_ref.shape[2]
    for f in range(pieces_ref.shape[0]):
        span = pl.ds(pl.multiple_of((index_ref[1] ^ f) * width, width), width)
        pieces_ref[f, k] = value_ref[span, :].astype(BF16)


def assemble_kernel(n_col, index_ref, *refs):
    groups, (solved_ref, remaining_ref, remaining, sems, last_sem) = refs[: 2 * n_col], refs[2 * n_col :]
    middle, late = groups[:n_col], groups[n_col:]
    chunk = middle[0].shape[2]
    odd = lax.rem(index_ref[0], 2)
    spans = [pl.ds(pl.multiple_of((index_ref[1] ^ f) * chunk, chunk), chunk) for f in range(n_col)]
    copies = []
    for f, span in enumerate(spans):
        for part, k in ((middle[f].at[0], 0), (middle[f].at[1], 2 - odd), (late[f].at[0], 1 + odd)):
            copies.append(pltpu.make_async_copy(part, solved_ref.at[k, :, span], sems.at[len(copies)]))
            copies[-1].start()
    for f, span in enumerate(spans):
        remaining[:, span] = late[f][1].astype(F32)
    copies.append(pltpu.make_async_copy(remaining, remaining_ref, last_sem))
    copies[-1].start()
    for copy in copies:
        copy.wait()


def assemble(index, middle, late, outs):
    n_col = len(middle)
    return pl.pallas_call(
        functools.partial(assemble_kernel, n_col),
        out_shape=outs,
        in_specs=[SMEM] + [VMEM] * (2 * n_col),
        out_specs=(HBM, HBM),
        scratch_shapes=[pltpu.VMEM(outs[1].shape, F32), pltpu.SemaphoreType.DMA((3 * n_col,)), pltpu.SemaphoreType.DMA],
        compiler_params=PARAMS,
        cost_estimate=cost(1),
    )(index, *middle, *late)


def local(kernel, out_shape, operands, scratch=(), us=1):
    out_specs = jax.tree.map(lambda _: VMEM, out_shape)
    return pl.pallas_call(
        kernel,
        out_shape=out_shape,
        in_specs=[SMEM] + [VMEM] * (len(operands) - 1),
        out_specs=out_specs,
        scratch_shapes=list(scratch),
        compiler_params=PARAMS,
        cost_estimate=cost(us),
    )(*operands)


def hop(value, *pairs):
    return lax.ppermute(value, "row", pairs)


def gate(*values):
    return lax.optimization_barrier(values)


def swap_pieces(pieces, n_col):
    return [pieces[0]] + [flip(pieces[f], "col", n_col, f) for f in range(1, n_col)]


def fast(shape, right_side, earlier_panel, earlier_solution, window_panel, diag_inverse):
    n_row, n_col = shape
    step_count = diag_inverse.shape[0]
    row, col = lax.axis_index("row"), lax.axis_index("col")
    index = flat_index(row, col)
    strip, nrhs = right_side.shape
    rows = earlier_panel.shape[0]
    chunk = nrhs // n_col

    block = earlier_solution[0]
    own = [jnp.where(row == j, diag_inverse[j], window_panel[:, j, :]) for j in range(step_count)]
    own = jnp.stack(own[:2] + [jnp.where(row == 1, diag_inverse[0], own[2])])
    over = flip(own, "col", n_col, 2)
    b4 = flip(block, "row", n_row, 4)
    b2 = flip(block, "row", n_row, 2)
    b1 = flip(block, "row", n_row, 1)
    panel = order_panel(index, earlier_panel)
    b2, again, panel = gate(b2, block, panel)
    b4, b1 = gate(b4, b1)
    b6 = flip(again, "row", n_row, 6)
    b3 = flip(b2, "row", n_row, 1)
    b5 = flip(b4, "row", n_row, 1)
    b7 = flip(b6, "row", n_row, 1)
    total = bulk(index, panel, right_side, [block, b1, b2, b3, b4, b5, b6])
    total, b7 = gate(total, b7)
    part = (n_col // 2, rows, chunk)
    split = functools.partial(split_kernel, n_col)
    kept, sent = local(split, (shape_of(part, F32), shape_of(part, BF16)), [index, panel, b7, total])
    moved = flip(sent, "col", n_col, 1)
    moved, over = gate(moved, over)
    slots = [own, flip(own, "col", n_col, 1), over, flip(over, "col", n_col, 1)]
    wide, narrow = shape_of((rows, chunk), F32), shape_of((rows, chunk), BF16)
    kept, also, sent = local(functools.partial(reduce_kernel, 2), (wide, narrow, narrow), [index, kept, moved])
    at1a = hop(also, (0, 1))
    at1b = lax.ppermute(sent, ("row", "col"), [(c, n_col + (c ^ 2)) for c in range(n_col)])
    moved = flip(sent, "col", n_col, 2)
    scratch = [pltpu.VMEM((rows, rows), BF16)] * 2
    product = local(functools.partial(product_kernel, n_col), shape_of((rows, rows), BF16), [index] + slots, scratch, us=8)

    kept, product = gate(kept, product)
    start = functools.partial(start_kernel, n_col)
    current, own0, ahead = local(start, (wide, narrow, wide), [index, kept, moved] + slots)
    at2 = hop(own0, (0, 2))
    own1 = local(first_step_kernel, narrow, [index, own0, ahead, product, at1a, at1b])
    first, second = hop(own1, (1, 2), (0, 6)), hop(own1, (1, 3))
    third, fourth = hop(own1, (0, 4)), hop(own1, (1, 5), (0, 3))
    between = functools.partial(between_kernel, n_col)
    current, ahead = local(between, (wide, wide), [index, current, at2] + slots, us=8)
    own2 = local(second_step_kernel, narrow, [index, own0, ahead, product, first, second])
    z6 = hop(own2, (2, 6))
    z4 = hop(own2, (2, 4), (3, 7))
    z0 = hop(own2, (2, 0))
    line0 = pick(index, (0, 0, 0, 0, 1, 0, 2, 0), own0, third, first)
    across0 = hop(line0, (0, 1), (4, 5), (6, 7))
    line = pick(index, (5, 0, 1, 1, 3, 4, 2, 3), own1, own2, z6, z4, fourth, z0)
    across = flip(line, "row", n_row, 1)
    pieces = shape_of((n_col, 2, strip, chunk), BF16)
    known, middle = local(known_kernel, (narrow, pieces), [index, own0, at2, fourth, line0, across0, line])
    middle = swap_pieces(middle, n_col)
    scratch = [pltpu.VMEM((rows, chunk), F32)]
    current = local(functools.partial(middle_kernel, n_col), wide, [index, current, known, first, line] + slots, scratch, us=8)
    late = {}
    for distances, us in (((2, 3), 1), ((0, 1), 8)):
        part = shape_of((2, 2, strip, chunk), BF16)
        finish = functools.partial(finish_kernel, distances)
        part = local(finish, part, [index, current, across] + [slots[f] for f in distances], us=us)
        late.update(zip(distances, (part[0], part[1])))
    late = swap_pieces([late[f] for f in range(n_col)], n_col)
    outs = (shape_of((step_count, strip, nrhs), BF16), shape_of((strip, nrhs), F32))
    return assemble(index, middle, late, outs)


def solution(mesh):
    shape = (mesh.shape["row"], mesh.shape["col"])

    def step(*args):
        chunk = args[0].shape[1] // shape[1]
        plan = fast if shape == (8, 4) and chunk % 128 == 0 and args[4].shape[0] == 3 else on_device
        return plan(shape, *args)

    return jax.shard_map(
        step,
        mesh=mesh,
        in_specs=(
            P(("row", "col"), None),
            P("row", None, "col"),
            P("row", "col", None),
            P(("row", "col"), None, None),
            P(None, "col", None),
        ),
        out_specs=(P(None, "col", None), P(("row", "col"), None)),
        check_vma=False,
    )
```

```python
import functools

import jax
import jax.numpy as jnp
from jax import lax
from jax.experimental import pallas as pl
from jax.experimental.pallas import tpu as pltpu
from jax.sharding import PartitionSpec as P

F32 = jnp.float32
BF16 = jnp.bfloat16


def flip(value, axis, size, bit):
    return lax.ppermute(value, axis, [(i, i ^ bit) for i in range(size)])


def matmul(left, right):
    return jnp.dot(left, right, preferred_element_type=F32)


def halves(value, bit):
    kept = lax.dynamic_index_in_dim(value, bit, 0, keepdims=False)
    sent = lax.dynamic_index_in_dim(value, 1 - bit, 0, keepdims=False)
    return kept, sent


def gather_ordered(value, n_col, col):
    bit = n_col // 2
    bits = []
    while bit:
        bits.append(bit)
        bit //= 2
    order = [b for b in bits if b > 1] + [1]
    parts = {0: value}
    for b in order:
        moved = {f ^ b: flip(v, "col", n_col, b) for f, v in parts.items()}
        parts.update(moved)
    stacked = jnp.stack([parts[f] for f in range(n_col)])
    index = jnp.arange(n_col) ^ col
    return stacked[index].reshape(-1, value.shape[1])


def reduce_chunks(value, n_col, col):
    bit = 1
    while bit < n_col:
        rest = value.shape[0] // 2
        paired = value.reshape((rest, 2) + value.shape[1:]).swapaxes(0, 1)
        kept, sent = halves(paired, (col // bit) % 2)
        value = kept + flip(sent.astype(BF16), "col", n_col, bit).astype(F32)
        bit *= 2
    return value[0]


def gather_lines(block, n_row, row):
    per_line = 1
    while 4 * per_line * per_line <= n_row:
        per_line *= 2
    lines = n_row // per_line
    blocks = [(block, row)]
    up, down = block, block
    for s in range(1, lines):
        up = lax.ppermute(up, "row", [(i, i + per_line) for i in range((s - 1) * per_line, n_row - per_line)])
        down = lax.ppermute(down, "row", [(i, i - per_line) for i in range(per_line, n_row - (s - 1) * per_line)])
        blocks += [(up, row - s * per_line), (down, row + s * per_line)]
    for bit in range(1, per_line):
        blocks += [(flip(v, "row", n_row, bit), source ^ bit) for v, source in blocks[: 2 * lines - 1]]
    return blocks


def on_device(shape, right_side, earlier_panel, earlier_solution, window_panel, diag_inverse):
    n_row, n_col = shape
    step_count = diag_inverse.shape[0]
    row, col = lax.axis_index("row"), lax.axis_index("col")
    strip, nrhs = right_side.shape
    rows = earlier_panel.shape[0]
    chunk = nrhs // n_col
    weights = []
    for j in range(step_count):
        own = jnp.where(row == j, diag_inverse[j], window_panel[:, j, :])
        weights.append(gather_ordered(own, n_col, col))

    total = jnp.zeros((n_col, strip, nrhs), F32)
    total = lax.dynamic_update_index_in_dim(total, -right_side, col, 0).reshape(rows, nrhs)
    if n_row > 8:
        everything = lax.all_gather(earlier_solution, "row", axis=0, tiled=True)
        total = total + jnp.einsum("iqw,qwn->in", earlier_panel, everything, preferred_element_type=F32)
    else:
        panel = earlier_panel.swapaxes(0, 1)
        for v, source in gather_lines(earlier_solution[0], n_row, row):
            part = lax.dynamic_index_in_dim(panel, jnp.clip(source, 0, n_row - 1), 0, keepdims=False)
            total = total + matmul(part, v)
    chunks = total.reshape(rows, n_col, chunk).swapaxes(0, 1)
    current = -reduce_chunks(chunks, n_col, col)

    bases = [[1, 2, 4], [3, 1, 4], [6, 2, 1]]
    solved = []
    for k in range(step_count):
        value = matmul(weights[k], current.astype(BF16)).astype(BF16)
        have = [k]
        bits = [b for b in bases[k]] + [1 << i for i in range(3, 16) if (1 << i) < n_row]
        for b in bits:
            moved = lax.ppermute(value, "row", [(i, i ^ b) for i in have])
            into = jnp.zeros((), bool)
            for i in have:
                into |= row == (i ^ b)
            value = jnp.where(into, moved, value)
            have += [i ^ b for i in have]
        solved.append(value)
        current = jnp.where(row > k, current - matmul(weights[k], value), current)
    early = lax.all_to_all(jnp.stack(solved[:-1]), "col", 1, 2, tiled=True)
    late = lax.all_to_all(jnp.stack([solved[-1], current.astype(BF16)]), "col", 1, 2, tiled=True)
    return jnp.concatenate([early, late[:1]]), late[1].astype(F32)


def flat_index(*values):
    return jnp.stack([jnp.asarray(v, jnp.int32) for v in values])


PARAMS = pltpu.CompilerParams(vmem_limit_bytes=20 * 1024 * 1024)


def cost(us):
    return pl.CostEstimate(flops=0, bytes_accessed=int(us * 3.6e6), transcendentals=0)

SMEM = pl.BlockSpec(memory_space=pltpu.SMEM)
VMEM = pl.BlockSpec(memory_space=pltpu.VMEM)
HBM = pl.BlockSpec(memory_space=pltpu.HBM)


def shape_of(shape, dtype):
    return jax.ShapeDtypeStruct(shape, dtype)


def order_kernel(index_ref, panel_ref, out_ref, held, sems, *wide):
    tiles, tile, sources, width = held.shape
    row = index_ref[0]
    copies = [pltpu.make_async_copy(panel_ref.at[pl.ds(t * tile, tile)], held.at[t], sems.at[t]) for t in range(tiles)]
    for copy in copies:
        copy.start()
    for t, copy in enumerate(copies):
        copy.wait()
        for h, lanes in enumerate(wide):
            lanes[...] = held[t, :, :, h * 128 : (h + 1) * 128].astype(F32).reshape(tile * sources, 128)
            for j in range(sources):
                start = (j ^ row) * width + h * 128
                span = pl.ds(pl.multiple_of(start, 128), 128)
                out_ref[t * tile : (t + 1) * tile, span] = lanes[pl.ds(j, tile, stride=sources), :].astype(BF16)


def order_panel(index, panel, tiles=4):
    rows, sources, width = panel.shape
    tile = rows // tiles
    return pl.pallas_call(
        order_kernel,
        out_shape=shape_of((rows, sources * width), BF16),
        in_specs=[SMEM, HBM],
        out_specs=VMEM,
        scratch_shapes=[pltpu.VMEM((tiles, tile, sources, width), BF16), pltpu.SemaphoreType.DMA((tiles,))]
        + [pltpu.VMEM((tile * sources, 128), F32)] * (width // 128),
        compiler_params=PARAMS,
        cost_estimate=cost(8),
    )(index, panel)


def bulk_kernel(count, index_ref, panel_ref, side_ref, *refs):
    blocks, (total_ref, stacked) = refs[:count], refs[count:]
    width = blocks[0].shape[0]
    strip = side_ref.shape[0]
    for f in range(count):
        stacked[f * width : (f + 1) * width, :] = blocks[f][...]
    for t in range(total_ref.shape[0] // strip):
        span = slice(t * strip, (t + 1) * strip)
        total_ref[span, :] = matmul(panel_ref[span, : count * width], stacked[...])
    own = pl.ds(pl.multiple_of(index_ref[1] * strip, strip), strip)
    total_ref[own, :] = total_ref[own, :] - side_ref[...]


def bulk(index, panel, side, blocks):
    count = len(blocks)
    width, nrhs = blocks[0].shape
    scratch = [pltpu.VMEM((count * width, nrhs), BF16)]
    kernel = functools.partial(bulk_kernel, count)
    return local(kernel, shape_of((panel.shape[0], nrhs), F32), [index, panel, side] + blocks, scratch, us=8)


def split_kernel(n_col, index_ref, panel_ref, *refs):
    blocks, (total_ref, kept_ref, sent_ref) = refs[:-3], refs[-3:]
    chunk = kept_ref.shape[2]
    width = blocks[0].shape[0]
    strip = total_ref.shape[0] // n_col
    core = lax.rem(index_ref[1], 2)
    first = panel_ref.shape[1] - len(blocks) * width

    def tile(t, carry):
        span = pl.ds(pl.multiple_of(t * strip, strip), strip)
        total = total_ref[span, :]
        for b, block in enumerate(blocks):
            total = total + matmul(panel_ref[span, first + b * width : first + (b + 1) * width], block[...])
        for parity in range(2):

            @pl.when(core == parity)
            def _():
                for h in range(n_col // 2):
                    mine, other = 2 * h + parity, 2 * h + 1 - parity
                    kept_ref[h, span, :] = total[:, mine * chunk : (mine + 1) * chunk]
                    sent_ref[h, span, :] = total[:, other * chunk : (other + 1) * chunk].astype(BF16)

        return carry

    lax.fori_loop(0, n_col, tile, 0)


def reduce_kernel(bit, index_ref, kept_ref, moved_ref, keep_ref, also_ref, send_ref):
    mine = lax.rem(index_ref[1] // bit, 2)
    keep = kept_ref[mine] + moved_ref[mine].astype(F32)
    keep_ref[...] = keep
    also_ref[...] = keep.astype(BF16)
    send_ref[...] = (kept_ref[1 - mine] + moved_ref[1 - mine].astype(F32)).astype(BF16)


def apply_strips(col, strips, value, store):
    refs, slot = strips
    width = refs[0].shape[1]
    for f, strip in enumerate(refs):
        span = pl.ds(pl.multiple_of((col ^ f) * width, width), width)
        store(span, matmul(strip[slot], value))


def store_solved(index_ref, strips, k, current_ref, solved_ref):
    def store(span, product):
        solved_ref[span, :] = product.astype(BF16)

    @pl.when(index_ref[0] == k)
    def _():
        apply_strips(index_ref[1], strips, current_ref[...].astype(BF16), store)

    @pl.when(index_ref[0] != k)
    def _():
        solved_ref[...] = jnp.zeros_like(solved_ref)


def subtract(index_ref, strips, value, chosen, source_ref, target_ref):
    def store(span, product):
        target_ref[span, :] = source_ref[span, :] - product

    @pl.when(chosen)
    def _():
        apply_strips(index_ref[1], strips, value, store)

    @pl.when(jnp.logical_not(chosen))
    def _():
        target_ref[...] = source_ref[...]


def added(parts):
    return functools.reduce(jnp.add, [part[...] for part in parts])


def copy_where(chosen, source_ref, target_ref):
    @pl.when(chosen)
    def _():
        target_ref[...] = source_ref[...]


def product_kernel(n_col, index_ref, *refs):
    strips, (out_ref, right, last) = refs[:n_col], refs[n_col:]
    row, col = index_ref[0], index_ref[1]
    width = strips[0].shape[1]
    spans = [pl.ds(pl.multiple_of((col ^ f) * width, width), width) for f in range(n_col)]

    @pl.when(row == 1)
    def _():
        for span, strip in zip(spans, strips):
            right[span, :] = strip[0]
            last[span, :] = strip[2]
        for span, strip in zip(spans, strips):
            part = matmul(strip[1], right[...]).astype(BF16)
            out_ref[span, :] = matmul(part, last[...]).astype(BF16)

    @pl.when(row == 2)
    def _():
        for span, strip in zip(spans, strips):
            right[span, :] = strip[1]
        for span, strip in zip(spans, strips):
            out_ref[span, :] = matmul(strip[2], right[...]).astype(BF16)

    @pl.when((row < 1) | (row > 2))
    def _():
        out_ref[...] = jnp.zeros_like(out_ref)


def start_kernel(n_col, index_ref, kept_ref, moved_ref, *refs):
    strips, (current_ref, solved_ref, ahead_ref) = refs[:n_col], refs[n_col:]
    current_ref[...] = -(kept_ref[...] + moved_ref[...].astype(F32))
    store_solved(index_ref, (strips, 0), 0, current_ref, solved_ref)

    def store(span, product):
        ahead_ref[span, :] = product

    @pl.when(index_ref[0] == 1)
    def _():
        apply_strips(index_ref[1], (strips, 1), current_ref[...].astype(BF16), store)


def first_step_kernel(index_ref, own_ref, ahead_ref, product_ref, at1a_ref, at1b_ref, solved_ref):
    row = index_ref[0]

    @pl.when(row == 1)
    def _():
        rows0 = -(at1a_ref[...].astype(F32) + at1b_ref[...].astype(F32))
        solved_ref[...] = (ahead_ref[...] - matmul(product_ref[...], rows0.astype(BF16))).astype(BF16)

    copy_where(row == 0, own_ref, solved_ref)

    @pl.when(row > 1)
    def _():
        solved_ref[...] = jnp.zeros_like(solved_ref)


def between_kernel(n_col, index_ref, current_ref, value_ref, *refs):
    strips, (out_ref, ahead_ref) = refs[:n_col], refs[n_col:]
    row = index_ref[0]
    subtract(index_ref, (strips, 0), value_ref[...], row == 2, current_ref, out_ref)

    def store(span, product):
        ahead_ref[span, :] = product

    @pl.when(row == 2)
    def _():
        apply_strips(index_ref[1], (strips, 2), out_ref[...].astype(BF16), store)


def second_step_kernel(index_ref, own_ref, ahead_ref, product_ref, first_ref, second_ref, solved_ref):
    row = index_ref[0]

    @pl.when(row == 2)
    def _():
        solved_ref[...] = (ahead_ref[...] - matmul(product_ref[...], first_ref[...])).astype(BF16)

    copy_where(row == 0, own_ref, solved_ref)
    copy_where(row == 3, second_ref, solved_ref)

    @pl.when((row == 1) | (row > 3))
    def _():
        solved_ref[...] = jnp.zeros_like(solved_ref)


def pick_kernel(holders, index_ref, *refs):
    parts, (out_ref,) = refs[:-1], refs[-1:]
    for row, part in enumerate(holders):
        copy_where(index_ref[0] == row, parts[part], out_ref)


def pick(index, holders, *parts):
    return local(functools.partial(pick_kernel, holders), shape_of(parts[0].shape, BF16), [index] + list(parts))


def known_kernel(index_ref, own0_ref, z0_ref, at2_ref, fourth_ref, line0_ref, across0_ref, line_ref, known_ref, pieces_ref):
    row = index_ref[0]
    for holder, part in enumerate((own0_ref, z0_ref, at2_ref, fourth_ref, line0_ref, across0_ref, line0_ref, across0_ref)):
        copy_where(row == holder, part, known_ref)
    cut(index_ref, known_ref, pieces_ref, 0)
    cut(index_ref, line_ref, pieces_ref, 1)


def middle_kernel(n_col, index_ref, current_ref, known_ref, first_ref, line_ref, *refs):
    strips, (out_ref, between) = refs[:n_col], refs[n_col:]
    row = index_ref[0]
    odd = lax.rem(row, 2) == 1
    subtract(index_ref, (strips, 0), known_ref[...], (row == 1) | (row > 2), current_ref, between)
    copy_where(row < 2, between, out_ref)

    @pl.when(row == 2)
    def _():
        subtract(index_ref, (strips, 1), first_ref[...], row == 2, between, out_ref)

    for slot, mine in ((1, odd), (2, jnp.logical_not(odd))):

        @pl.when((row > 2) & mine)
        def _():
            subtract(index_ref, (strips, slot), line_ref[...], row > 2, between, out_ref)


def finish_kernel(distances, index_ref, current_ref, value_ref, *refs):
    strips, (pieces_ref,) = refs[:-1], refs[-1:]
    row, col = index_ref[0], index_ref[1]
    odd = lax.rem(row, 2) == 1
    width = pieces_ref.shape[2]
    for i, (f, strip) in enumerate(zip(distances, strips)):
        span = pl.ds(pl.multiple_of((col ^ f) * width, width), width)
        pieces_ref[i, 0] = value_ref[span, :]

        @pl.when(row <= 2)
        def _():
            pieces_ref[i, 1] = current_ref[span, :].astype(BF16)

        for slot, mine in ((2, odd), (1, jnp.logical_not(odd))):

            @pl.when((row > 2) & mine)
            def _():
                pieces_ref[i, 1] = (current_ref[span, :] - matmul(strip[slot], value_ref[...])).astype(BF16)


def cut(index_ref, value_ref, pieces_ref, k):
    width = pieces_ref.shape[2]
    for f in range(pieces_ref.shape[0]):
        span = pl.ds(pl.multiple_of((index_ref[1] ^ f) * width, width), width)
        pieces_ref[f, k] = value_ref[span, :].astype(BF16)


def assemble_kernel(n_col, index_ref, *refs):
    groups, (solved_ref, remaining_ref, remaining, sems, last_sem) = refs[: 2 * n_col], refs[2 * n_col :]
    middle, late = groups[:n_col], groups[n_col:]
    chunk = middle[0].shape[2]
    odd = lax.rem(index_ref[0], 2)
    spans = [pl.ds(pl.multiple_of((index_ref[1] ^ f) * chunk, chunk), chunk) for f in range(n_col)]
    copies = []
    for f, span in enumerate(spans):
        for part, k in ((middle[f].at[0], 0), (middle[f].at[1], 2 - odd), (late[f].at[0], 1 + odd)):
            copies.append(pltpu.make_async_copy(part, solved_ref.at[k, :, span], sems.at[len(copies)]))
            copies[-1].start()
    for f, span in enumerate(spans):
        remaining[:, span] = late[f][1].astype(F32)
    copies.append(pltpu.make_async_copy(remaining, remaining_ref, last_sem))
    copies[-1].start()
    for copy in copies:
        copy.wait()


def assemble(index, middle, late, outs):
    n_col = len(middle)
    return pl.pallas_call(
        functools.partial(assemble_kernel, n_col),
        out_shape=outs,
        in_specs=[SMEM] + [VMEM] * (2 * n_col),
        out_specs=(HBM, HBM),
        scratch_shapes=[pltpu.VMEM(outs[1].shape, F32), pltpu.SemaphoreType.DMA((3 * n_col,)), pltpu.SemaphoreType.DMA],
        compiler_params=PARAMS,
        cost_estimate=cost(1),
    )(index, *middle, *late)


def local(kernel, out_shape, operands, scratch=(), us=1):
    out_specs = jax.tree.map(lambda _: VMEM, out_shape)
    return pl.pallas_call(
        kernel,
        out_shape=out_shape,
        in_specs=[SMEM] + [VMEM] * (len(operands) - 1),
        out_specs=out_specs,
        scratch_shapes=list(scratch),
        compiler_params=PARAMS,
        cost_estimate=cost(us),
    )(*operands)


def hop(value, *pairs):
    return lax.ppermute(value, "row", pairs)


def gate(*values):
    return lax.optimization_barrier(values)


def swap_pieces(pieces, n_col):
    return [pieces[0]] + [flip(pieces[f], "col", n_col, f) for f in range(1, n_col)]


def fast(shape, right_side, earlier_panel, earlier_solution, window_panel, diag_inverse):
    n_row, n_col = shape
    step_count = diag_inverse.shape[0]
    row, col = lax.axis_index("row"), lax.axis_index("col")
    index = flat_index(row, col)
    strip, nrhs = right_side.shape
    rows = earlier_panel.shape[0]
    chunk = nrhs // n_col

    block = earlier_solution[0]
    own = [jnp.where(row == j, diag_inverse[j], window_panel[:, j, :]) for j in range(step_count)]
    own = jnp.stack(own[:2] + [jnp.where(row == 1, diag_inverse[0], own[2])])
    over = flip(own, "col", n_col, 2)
    b4 = flip(block, "row", n_row, 4)
    b2 = flip(block, "row", n_row, 2)
    b1 = flip(block, "row", n_row, 1)
    panel = order_panel(index, earlier_panel)
    b2, again, panel = gate(b2, block, panel)
    b4, b1 = gate(b4, b1)
    b6 = flip(again, "row", n_row, 6)
    b3 = flip(b2, "row", n_row, 1)
    b5 = flip(b4, "row", n_row, 1)
    b7 = flip(b6, "row", n_row, 1)
    total = bulk(index, panel, right_side, [block, b1, b2, b3, b4, b5, b6])
    total, b7 = gate(total, b7)
    part = (n_col // 2, rows, chunk)
    split = functools.partial(split_kernel, n_col)
    kept, sent = local(split, (shape_of(part, F32), shape_of(part, BF16)), [index, panel, b7, total])
    moved = flip(sent, "col", n_col, 1)
    moved, over = gate(moved, over)
    slots = [own, flip(own, "col", n_col, 1), over, flip(over, "col", n_col, 1)]
    wide, narrow = shape_of((rows, chunk), F32), shape_of((rows, chunk), BF16)
    kept, also, sent = local(functools.partial(reduce_kernel, 2), (wide, narrow, narrow), [index, kept, moved])
    at1a = hop(also, (0, 1))
    at1b = lax.ppermute(sent, ("row", "col"), [(c, n_col + (c ^ 2)) for c in range(n_col)])
    moved = flip(sent, "col", n_col, 2)
    scratch = [pltpu.VMEM((rows, rows), BF16)] * 2
    product = local(functools.partial(product_kernel, n_col), shape_of((rows, rows), BF16), [index] + slots, scratch, us=8)

    kept, product = gate(kept, product)
    start = functools.partial(start_kernel, n_col)
    current, own0, ahead = local(start, (wide, narrow, wide), [index, kept, moved] + slots)
    at2 = hop(own0, (0, 2))
    own1 = local(first_step_kernel, narrow, [index, own0, ahead, product, at1a, at1b])
    first, second = hop(own1, (1, 2), (0, 6)), hop(own1, (1, 3))
    third, fourth = hop(own1, (0, 4)), hop(own1, (1, 5), (0, 3))
    between = functools.partial(between_kernel, n_col)
    current, ahead = local(between, (wide, wide), [index, current, at2] + slots, us=8)
    own2 = local(second_step_kernel, narrow, [index, own0, ahead, product, first, second])
    z6 = hop(own2, (2, 6))
    z4 = hop(own2, (2, 4), (3, 7))
    z0 = hop(own2, (2, 0), (0, 1))
    line0 = pick(index, (0, 0, 0, 0, 1, 0, 2, 0), own0, third, first)
    across0 = hop(line0, (4, 5), (6, 7))
    line = pick(index, (5, 0, 1, 1, 3, 4, 2, 3), own1, own2, z6, z4, fourth, z0)
    across = flip(line, "row", n_row, 1)
    pieces = shape_of((n_col, 2, strip, chunk), BF16)
    known, middle = local(known_kernel, (narrow, pieces), [index, own0, z0, at2, fourth, line0, across0, line])
    middle = swap_pieces(middle, n_col)
    scratch = [pltpu.VMEM((rows, chunk), F32)]
    current = local(functools.partial(middle_kernel, n_col), wide, [index, current, known, first, line] + slots, scratch, us=8)
    late = {}
    for distances, us in (((2, 3), 1), ((0, 1), 8)):
        part = shape_of((2, 2, strip, chunk), BF16)
        finish = functools.partial(finish_kernel, distances)
        part = local(finish, part, [index, current, across] + [slots[f] for f in distances], us=us)
        late.update(zip(distances, (part[0], part[1])))
    late = swap_pieces([late[f] for f in range(n_col)], n_col)
    outs = (shape_of((step_count, strip, nrhs), BF16), shape_of((strip, nrhs), F32))
    return assemble(index, middle, late, outs)


def solution(mesh):
    shape = (mesh.shape["row"], mesh.shape["col"])

    def step(*args):
        chunk = args[0].shape[1] // shape[1]
        plan = fast if shape == (8, 4) and chunk % 128 == 0 and args[4].shape[0] == 3 else on_device
        return plan(shape, *args)

    return jax.shard_map(
        step,
        mesh=mesh,
        in_specs=(
            P(("row", "col"), None),
            P("row", None, "col"),
            P("row", "col", None),
            P(("row", "col"), None, None),
            P(None, "col", None),
        ),
        out_specs=(P(None, "col", None), P(("row", "col"), None)),
        check_vma=False,
    )
```

```python
import functools

import jax
import jax.numpy as jnp
from jax import lax
from jax.experimental import pallas as pl
from jax.experimental.pallas import tpu as pltpu
from jax.sharding import PartitionSpec as P

F32 = jnp.float32
BF16 = jnp.bfloat16


def flip(value, axis, size, bit):
    return lax.ppermute(value, axis, [(i, i ^ bit) for i in range(size)])


def matmul(left, right):
    return jnp.dot(left, right, preferred_element_type=F32)


def halves(value, bit):
    kept = lax.dynamic_index_in_dim(value, bit, 0, keepdims=False)
    sent = lax.dynamic_index_in_dim(value, 1 - bit, 0, keepdims=False)
    return kept, sent


def gather_ordered(value, n_col, col):
    bit = n_col // 2
    bits = []
    while bit:
        bits.append(bit)
        bit //= 2
    order = [b for b in bits if b > 1] + [1]
    parts = {0: value}
    for b in order:
        moved = {f ^ b: flip(v, "col", n_col, b) for f, v in parts.items()}
        parts.update(moved)
    stacked = jnp.stack([parts[f] for f in range(n_col)])
    index = jnp.arange(n_col) ^ col
    return stacked[index].reshape(-1, value.shape[1])


def reduce_chunks(value, n_col, col):
    bit = 1
    while bit < n_col:
        rest = value.shape[0] // 2
        paired = value.reshape((rest, 2) + value.shape[1:]).swapaxes(0, 1)
        kept, sent = halves(paired, (col // bit) % 2)
        value = kept + flip(sent.astype(BF16), "col", n_col, bit).astype(F32)
        bit *= 2
    return value[0]


def gather_lines(block, n_row, row):
    per_line = 1
    while 4 * per_line * per_line <= n_row:
        per_line *= 2
    lines = n_row // per_line
    blocks = [(block, row)]
    up, down = block, block
    for s in range(1, lines):
        up = lax.ppermute(up, "row", [(i, i + per_line) for i in range((s - 1) * per_line, n_row - per_line)])
        down = lax.ppermute(down, "row", [(i, i - per_line) for i in range(per_line, n_row - (s - 1) * per_line)])
        blocks += [(up, row - s * per_line), (down, row + s * per_line)]
    for bit in range(1, per_line):
        blocks += [(flip(v, "row", n_row, bit), source ^ bit) for v, source in blocks[: 2 * lines - 1]]
    return blocks


def on_device(shape, right_side, earlier_panel, earlier_solution, window_panel, diag_inverse):
    n_row, n_col = shape
    step_count = diag_inverse.shape[0]
    row, col = lax.axis_index("row"), lax.axis_index("col")
    strip, nrhs = right_side.shape
    rows = earlier_panel.shape[0]
    chunk = nrhs // n_col
    weights = []
    for j in range(step_count):
        own = jnp.where(row == j, diag_inverse[j], window_panel[:, j, :])
        weights.append(gather_ordered(own, n_col, col))

    total = jnp.zeros((n_col, strip, nrhs), F32)
    total = lax.dynamic_update_index_in_dim(total, -right_side, col, 0).reshape(rows, nrhs)
    if n_row > 8:
        everything = lax.all_gather(earlier_solution, "row", axis=0, tiled=True)
        total = total + jnp.einsum("iqw,qwn->in", earlier_panel, everything, preferred_element_type=F32)
    else:
        panel = earlier_panel.swapaxes(0, 1)
        for v, source in gather_lines(earlier_solution[0], n_row, row):
            part = lax.dynamic_index_in_dim(panel, jnp.clip(source, 0, n_row - 1), 0, keepdims=False)
            total = total + matmul(part, v)
    chunks = total.reshape(rows, n_col, chunk).swapaxes(0, 1)
    current = -reduce_chunks(chunks, n_col, col)

    bases = [[1, 2, 4], [3, 1, 4], [6, 2, 1]]
    solved = []
    for k in range(step_count):
        value = matmul(weights[k], current.astype(BF16)).astype(BF16)
        have = [k]
        bits = [b for b in bases[k]] + [1 << i for i in range(3, 16) if (1 << i) < n_row]
        for b in bits:
            moved = lax.ppermute(value, "row", [(i, i ^ b) for i in have])
            into = jnp.zeros((), bool)
            for i in have:
                into |= row == (i ^ b)
            value = jnp.where(into, moved, value)
            have += [i ^ b for i in have]
        solved.append(value)
        current = jnp.where(row > k, current - matmul(weights[k], value), current)
    early = lax.all_to_all(jnp.stack(solved[:-1]), "col", 1, 2, tiled=True)
    late = lax.all_to_all(jnp.stack([solved[-1], current.astype(BF16)]), "col", 1, 2, tiled=True)
    return jnp.concatenate([early, late[:1]]), late[1].astype(F32)


def flat_index(*values):
    return jnp.stack([jnp.asarray(v, jnp.int32) for v in values])


PARAMS = pltpu.CompilerParams(vmem_limit_bytes=20 * 1024 * 1024)


def cost(us):
    return pl.CostEstimate(flops=0, bytes_accessed=int(us * 3.6e6), transcendentals=0)

SMEM = pl.BlockSpec(memory_space=pltpu.SMEM)
VMEM = pl.BlockSpec(memory_space=pltpu.VMEM)
HBM = pl.BlockSpec(memory_space=pltpu.HBM)


def shape_of(shape, dtype):
    return jax.ShapeDtypeStruct(shape, dtype)


def order_kernel(index_ref, panel_ref, out_ref, held, sems, *wide):
    tiles, tile, sources, width = held.shape
    row = index_ref[0]
    copies = [pltpu.make_async_copy(panel_ref.at[pl.ds(t * tile, tile)], held.at[t], sems.at[t]) for t in range(tiles)]
    for copy in copies:
        copy.start()
    for t, copy in enumerate(copies):
        copy.wait()
        for h, lanes in enumerate(wide):
            lanes[...] = held[t, :, :, h * 128 : (h + 1) * 128].astype(F32).reshape(tile * sources, 128)
            for j in range(sources):
                start = (j ^ row) * width + h * 128
                span = pl.ds(pl.multiple_of(start, 128), 128)
                out_ref[t * tile : (t + 1) * tile, span] = lanes[pl.ds(j, tile, stride=sources), :].astype(BF16)


def order_panel(index, panel, tiles=4):
    rows, sources, width = panel.shape
    tile = rows // tiles
    return pl.pallas_call(
        order_kernel,
        out_shape=shape_of((rows, sources * width), BF16),
        in_specs=[SMEM, HBM],
        out_specs=VMEM,
        scratch_shapes=[pltpu.VMEM((tiles, tile, sources, width), BF16), pltpu.SemaphoreType.DMA((tiles,))]
        + [pltpu.VMEM((tile * sources, 128), F32)] * (width // 128),
        compiler_params=PARAMS,
        cost_estimate=cost(8),
    )(index, panel)


def bulk_kernel(count, index_ref, panel_ref, side_ref, *refs):
    blocks, (total_ref, stacked) = refs[:count], refs[count:]
    width = blocks[0].shape[0]
    strip = side_ref.shape[0]
    for f in range(count):
        stacked[f * width : (f + 1) * width, :] = blocks[f][...]
    for t in range(total_ref.shape[0] // strip):
        span = slice(t * strip, (t + 1) * strip)
        total_ref[span, :] = matmul(panel_ref[span, : count * width], stacked[...])
    own = pl.ds(pl.multiple_of(index_ref[1] * strip, strip), strip)
    total_ref[own, :] = total_ref[own, :] - side_ref[...]


def bulk(index, panel, side, blocks):
    count = len(blocks)
    width, nrhs = blocks[0].shape
    scratch = [pltpu.VMEM((count * width, nrhs), BF16)]
    kernel = functools.partial(bulk_kernel, count)
    return local(kernel, shape_of((panel.shape[0], nrhs), F32), [index, panel, side] + blocks, scratch, us=8)


def split_kernel(n_col, index_ref, panel_ref, *refs):
    blocks, (total_ref, kept_ref, sent_ref) = refs[:-3], refs[-3:]
    chunk = kept_ref.shape[2]
    width = blocks[0].shape[0]
    strip = total_ref.shape[0] // n_col
    core = lax.rem(index_ref[1], 2)
    first = panel_ref.shape[1] - len(blocks) * width

    def tile(t, carry):
        span = pl.ds(pl.multiple_of(t * strip, strip), strip)
        total = total_ref[span, :]
        for b, block in enumerate(blocks):
            total = total + matmul(panel_ref[span, first + b * width : first + (b + 1) * width], block[...])
        for parity in range(2):

            @pl.when(core == parity)
            def _():
                for h in range(n_col // 2):
                    mine, other = 2 * h + parity, 2 * h + 1 - parity
                    kept_ref[h, span, :] = total[:, mine * chunk : (mine + 1) * chunk]
                    sent_ref[h, span, :] = total[:, other * chunk : (other + 1) * chunk].astype(BF16)

        return carry

    lax.fori_loop(0, n_col, tile, 0)


def reduce_kernel(bit, index_ref, kept_ref, moved_ref, keep_ref, also_ref, send_ref):
    mine = lax.rem(index_ref[1] // bit, 2)
    keep = kept_ref[mine] + moved_ref[mine].astype(F32)
    keep_ref[...] = keep
    also_ref[...] = keep.astype(BF16)
    send_ref[...] = (kept_ref[1 - mine] + moved_ref[1 - mine].astype(F32)).astype(BF16)


def apply_strips(col, strips, value, store):
    refs, slot = strips
    width = refs[0].shape[1]
    for f, strip in enumerate(refs):
        span = pl.ds(pl.multiple_of((col ^ f) * width, width), width)
        store(span, matmul(strip[slot], value))


def store_solved(index_ref, strips, k, current_ref, solved_ref):
    def store(span, product):
        solved_ref[span, :] = product.astype(BF16)

    @pl.when(index_ref[0] == k)
    def _():
        apply_strips(index_ref[1], strips, current_ref[...].astype(BF16), store)

    @pl.when(index_ref[0] != k)
    def _():
        solved_ref[...] = jnp.zeros_like(solved_ref)


def subtract(index_ref, strips, value, chosen, source_ref, target_ref):
    def store(span, product):
        target_ref[span, :] = source_ref[span, :] - product

    @pl.when(chosen)
    def _():
        apply_strips(index_ref[1], strips, value, store)

    @pl.when(jnp.logical_not(chosen))
    def _():
        target_ref[...] = source_ref[...]


def added(parts):
    return functools.reduce(jnp.add, [part[...] for part in parts])


def copy_where(chosen, source_ref, target_ref):
    @pl.when(chosen)
    def _():
        target_ref[...] = source_ref[...]


def product_kernel(n_col, index_ref, *refs):
    strips, (out_ref, right, last) = refs[:n_col], refs[n_col:]
    row, col = index_ref[0], index_ref[1]
    width = strips[0].shape[1]
    spans = [pl.ds(pl.multiple_of((col ^ f) * width, width), width) for f in range(n_col)]

    @pl.when(row == 1)
    def _():
        for span, strip in zip(spans, strips):
            right[span, :] = strip[0]
            last[span, :] = strip[2]
        for span, strip in zip(spans, strips):
            part = matmul(strip[1], right[...]).astype(BF16)
            out_ref[span, :] = matmul(part, last[...]).astype(BF16)

    @pl.when(row == 2)
    def _():
        for span, strip in zip(spans, strips):
            right[span, :] = strip[1]
        for span, strip in zip(spans, strips):
            out_ref[span, :] = matmul(strip[2], right[...]).astype(BF16)

    @pl.when((row < 1) | (row > 2))
    def _():
        out_ref[...] = jnp.zeros_like(out_ref)


def start_kernel(n_col, index_ref, kept_ref, moved_ref, *refs):
    strips, (current_ref, solved_ref, ahead_ref) = refs[:n_col], refs[n_col:]
    current_ref[...] = -(kept_ref[...] + moved_ref[...].astype(F32))
    store_solved(index_ref, (strips, 0), 0, current_ref, solved_ref)

    def store(span, product):
        ahead_ref[span, :] = product

    @pl.when(index_ref[0] == 1)
    def _():
        apply_strips(index_ref[1], (strips, 1), current_ref[...].astype(BF16), store)


def first_step_kernel(index_ref, own_ref, ahead_ref, product_ref, at1a_ref, at1b_ref, solved_ref):
    row = index_ref[0]

    @pl.when(row == 1)
    def _():
        rows0 = -(at1a_ref[...].astype(F32) + at1b_ref[...].astype(F32))
        solved_ref[...] = (ahead_ref[...] - matmul(product_ref[...], rows0.astype(BF16))).astype(BF16)

    copy_where(row == 0, own_ref, solved_ref)

    @pl.when(row > 1)
    def _():
        solved_ref[...] = jnp.zeros_like(solved_ref)


def between_kernel(n_col, index_ref, current_ref, value_ref, *refs):
    strips, (out_ref, ahead_ref) = refs[:n_col], refs[n_col:]
    row = index_ref[0]
    subtract(index_ref, (strips, 0), value_ref[...], row == 2, current_ref, out_ref)

    def store(span, product):
        ahead_ref[span, :] = product

    @pl.when(row == 2)
    def _():
        apply_strips(index_ref[1], (strips, 2), out_ref[...].astype(BF16), store)


def second_step_kernel(index_ref, own_ref, ahead_ref, product_ref, first_ref, second_ref, solved_ref):
    row = index_ref[0]

    @pl.when(row == 2)
    def _():
        solved_ref[...] = (ahead_ref[...] - matmul(product_ref[...], first_ref[...])).astype(BF16)

    copy_where(row == 0, own_ref, solved_ref)
    copy_where(row == 3, second_ref, solved_ref)

    @pl.when((row == 1) | (row > 3))
    def _():
        solved_ref[...] = jnp.zeros_like(solved_ref)


def pick_kernel(holders, index_ref, *refs):
    parts, (out_ref,) = refs[:-1], refs[-1:]
    for row, part in enumerate(holders):
        copy_where(index_ref[0] == row, parts[part], out_ref)


def pick(index, holders, *parts):
    return local(functools.partial(pick_kernel, holders), shape_of(parts[0].shape, BF16), [index] + list(parts))


def known_kernel(index_ref, own0_ref, to1_ref, at2_ref, fourth_ref, line0_ref, across0_ref, line_ref, known_ref, pieces_ref):
    row = index_ref[0]
    for holder, part in enumerate((own0_ref, to1_ref, at2_ref, fourth_ref, line0_ref, across0_ref, line0_ref, across0_ref)):
        copy_where(row == holder, part, known_ref)
    cut(index_ref, known_ref, pieces_ref, 0)
    cut(index_ref, line_ref, pieces_ref, 1)


def middle_kernel(n_col, index_ref, current_ref, known_ref, first_ref, line_ref, *refs):
    strips, (out_ref, between) = refs[:n_col], refs[n_col:]
    row = index_ref[0]
    odd = lax.rem(row, 2) == 1
    subtract(index_ref, (strips, 0), known_ref[...], (row == 1) | (row > 2), current_ref, between)
    copy_where(row < 2, between, out_ref)

    @pl.when(row == 2)
    def _():
        subtract(index_ref, (strips, 1), first_ref[...], row == 2, between, out_ref)

    for slot, mine in ((1, odd), (2, jnp.logical_not(odd))):

        @pl.when((row > 2) & mine)
        def _():
            subtract(index_ref, (strips, slot), line_ref[...], row > 2, between, out_ref)


def finish_kernel(distances, index_ref, current_ref, value_ref, *refs):
    strips, (pieces_ref,) = refs[:-1], refs[-1:]
    row, col = index_ref[0], index_ref[1]
    odd = lax.rem(row, 2) == 1
    width = pieces_ref.shape[2]
    for i, (f, strip) in enumerate(zip(distances, strips)):
        span = pl.ds(pl.multiple_of((col ^ f) * width, width), width)
        pieces_ref[i, 0] = value_ref[span, :]

        @pl.when(row <= 2)
        def _():
            pieces_ref[i, 1] = current_ref[span, :].astype(BF16)

        for slot, mine in ((2, odd), (1, jnp.logical_not(odd))):

            @pl.when((row > 2) & mine)
            def _():
                pieces_ref[i, 1] = (current_ref[span, :] - matmul(strip[slot], value_ref[...])).astype(BF16)


def cut(index_ref, value_ref, pieces_ref, k):
    width = pieces_ref.shape[2]
    for f in range(pieces_ref.shape[0]):
        span = pl.ds(pl.multiple_of((index_ref[1] ^ f) * width, width), width)
        pieces_ref[f, k] = value_ref[span, :].astype(BF16)


def assemble_kernel(n_col, index_ref, *refs):
    groups, (solved_ref, remaining_ref, remaining, sems, last_sem) = refs[: 2 * n_col], refs[2 * n_col :]
    middle, late = groups[:n_col], groups[n_col:]
    chunk = middle[0].shape[2]
    odd = lax.rem(index_ref[0], 2)
    spans = [pl.ds(pl.multiple_of((index_ref[1] ^ f) * chunk, chunk), chunk) for f in range(n_col)]
    copies = []
    for f, span in enumerate(spans):
        for part, k in ((middle[f].at[0], 0), (middle[f].at[1], 2 - odd), (late[f].at[0], 1 + odd)):
            copies.append(pltpu.make_async_copy(part, solved_ref.at[k, :, span], sems.at[len(copies)]))
            copies[-1].start()
    for f, span in enumerate(spans):
        remaining[:, span] = late[f][1].astype(F32)
    copies.append(pltpu.make_async_copy(remaining, remaining_ref, last_sem))
    copies[-1].start()
    for copy in copies:
        copy.wait()


def assemble(index, middle, late, outs):
    n_col = len(middle)
    return pl.pallas_call(
        functools.partial(assemble_kernel, n_col),
        out_shape=outs,
        in_specs=[SMEM] + [VMEM] * (2 * n_col),
        out_specs=(HBM, HBM),
        scratch_shapes=[pltpu.VMEM(outs[1].shape, F32), pltpu.SemaphoreType.DMA((3 * n_col,)), pltpu.SemaphoreType.DMA],
        compiler_params=PARAMS,
        cost_estimate=cost(1),
    )(index, *middle, *late)


def local(kernel, out_shape, operands, scratch=(), us=1):
    out_specs = jax.tree.map(lambda _: VMEM, out_shape)
    return pl.pallas_call(
        kernel,
        out_shape=out_shape,
        in_specs=[SMEM] + [VMEM] * (len(operands) - 1),
        out_specs=out_specs,
        scratch_shapes=list(scratch),
        compiler_params=PARAMS,
        cost_estimate=cost(us),
    )(*operands)


def hop(value, *pairs):
    return lax.ppermute(value, "row", pairs)


def gate(*values):
    return lax.optimization_barrier(values)


def swap_pieces(pieces, n_col):
    return [pieces[0]] + [flip(pieces[f], "col", n_col, f) for f in range(1, n_col)]


def fast(shape, right_side, earlier_panel, earlier_solution, window_panel, diag_inverse):
    n_row, n_col = shape
    step_count = diag_inverse.shape[0]
    row, col = lax.axis_index("row"), lax.axis_index("col")
    index = flat_index(row, col)
    strip, nrhs = right_side.shape
    rows = earlier_panel.shape[0]
    chunk = nrhs // n_col

    block = earlier_solution[0]
    own = [jnp.where(row == j, diag_inverse[j], window_panel[:, j, :]) for j in range(step_count)]
    own = jnp.stack(own[:2] + [jnp.where(row == 1, diag_inverse[0], own[2])])
    over = flip(own, "col", n_col, 2)
    b4 = flip(block, "row", n_row, 4)
    b2 = flip(block, "row", n_row, 2)
    b1 = flip(block, "row", n_row, 1)
    panel = order_panel(index, earlier_panel)
    b2, again, panel = gate(b2, block, panel)
    b4, b1 = gate(b4, b1)
    b6 = flip(again, "row", n_row, 6)
    b3 = flip(b2, "row", n_row, 1)
    b5 = flip(b4, "row", n_row, 1)
    b7 = flip(b6, "row", n_row, 1)
    total = bulk(index, panel, right_side, [block, b1, b2, b3, b4, b5, b6])
    total, b7 = gate(total, b7)
    part = (n_col // 2, rows, chunk)
    split = functools.partial(split_kernel, n_col)
    kept, sent = local(split, (shape_of(part, F32), shape_of(part, BF16)), [index, panel, b7, total])
    moved = flip(sent, "col", n_col, 1)
    moved, over = gate(moved, over)
    slots = [own, flip(own, "col", n_col, 1), over, flip(over, "col", n_col, 1)]
    wide, narrow = shape_of((rows, chunk), F32), shape_of((rows, chunk), BF16)
    kept, also, sent = local(functools.partial(reduce_kernel, 2), (wide, narrow, narrow), [index, kept, moved])
    at1a = hop(also, (0, 1))
    at1b = lax.ppermute(sent, ("row", "col"), [(c, n_col + (c ^ 2)) for c in range(n_col)])
    moved = flip(sent, "col", n_col, 2)
    scratch = [pltpu.VMEM((rows, rows), BF16)] * 2
    product = local(functools.partial(product_kernel, n_col), shape_of((rows, rows), BF16), [index] + slots, scratch, us=8)

    kept, product = gate(kept, product)
    start = functools.partial(start_kernel, n_col)
    current, own0, ahead = local(start, (wide, narrow, wide), [index, kept, moved] + slots)
    at2 = hop(own0, (0, 2))
    to1 = hop(own0, (0, 1))
    at2, to1 = gate(at2, to1)
    own1 = local(first_step_kernel, narrow, [index, own0, ahead, product, at1a, at1b])
    first, second = hop(own1, (1, 2), (0, 6)), hop(own1, (1, 3))
    third, fourth = hop(own1, (0, 4)), hop(own1, (1, 7), (0, 3))
    between = functools.partial(between_kernel, n_col)
    current, ahead = local(between, (wide, wide), [index, current, at2] + slots, us=8)
    own2 = local(second_step_kernel, narrow, [index, own0, ahead, product, first, second])
    z4 = hop(own2, (2, 4), (3, 5))
    z6 = hop(own2, (2, 6))
    z0 = hop(own2, (2, 0))
    line0 = pick(index, (0, 0, 0, 0, 1, 0, 2, 0), own0, third, first)
    across0 = hop(line0, (4, 5), (6, 7))
    line = pick(index, (5, 0, 1, 1, 2, 2, 3, 4), own1, own2, z4, z6, fourth, z0)
    across = flip(line, "row", n_row, 1)
    pieces = shape_of((n_col, 2, strip, chunk), BF16)
    known, middle = local(known_kernel, (narrow, pieces), [index, own0, to1, at2, fourth, line0, across0, line])
    middle = swap_pieces(middle, n_col)
    scratch = [pltpu.VMEM((rows, chunk), F32)]
    current = local(functools.partial(middle_kernel, n_col), wide, [index, current, known, first, line] + slots, scratch, us=8)
    late = {}
    for distances, us in (((2, 3), 1), ((0, 1), 8)):
        part = shape_of((2, 2, strip, chunk), BF16)
        finish = functools.partial(finish_kernel, distances)
        part = local(finish, part, [index, current, across] + [slots[f] for f in distances], us=us)
        late.update(zip(distances, (part[0], part[1])))
    late = swap_pieces([late[f] for f in range(n_col)], n_col)
    outs = (shape_of((step_count, strip, nrhs), BF16), shape_of((strip, nrhs), F32))
    return assemble(index, middle, late, outs)


def solution(mesh):
    shape = (mesh.shape["row"], mesh.shape["col"])

    def step(*args):
        chunk = args[0].shape[1] // shape[1]
        plan = fast if shape == (8, 4) and chunk % 128 == 0 and args[4].shape[0] == 3 else on_device
        return plan(shape, *args)

    return jax.shard_map(
        step,
        mesh=mesh,
        in_specs=(
            P(("row", "col"), None),
            P("row", None, "col"),
            P("row", "col", None),
            P(("row", "col"), None, None),
            P(None, "col", None),
        ),
        out_specs=(P(None, "col", None), P(("row", "col"), None)),
        check_vma=False,
    )
```
